32 devices in a mesh: fsdp: 16 (over z, y, core), rep: 2 (over x).
Axes of the slice: x: 2, y: 2, z: 4, core: 2. Of those that a mesh axis runs over, the one named last changes fastest.
Arguments:
- token_ids: int32 [16384], P(('fsdp', 'rep')), may hold values from 0 to 30719
- boxes: int32 [4, 16384], P(None, ('fsdp', 'rep')), may hold values from 0 to 999
- lengths: int32 [32], P(('fsdp', 'rep')), may hold values from 40 to 512, as said below
- slots: int32 [32, 128], P(('fsdp', 'rep')), may hold values from 0 to 255, as said below
- labels: int32 [32, 128], P(('fsdp', 'rep')), may hold values from 0 to 30719
- table: float32 [30720, 768], P('fsdp')
- mats: float32 [7, 768, 768], P(None, 'fsdp')
- up: float32 [768, 3072], P('fsdp'), may hold values from -0.21875 to 0.21875
- down: float32 [3072, 768], P('fsdp'), may hold values from -0.109375 to 0.109375
- vectors: float32 [11, 768], P(None, 'fsdp')
- up_bias: float32 [3072], P('fsdp'), may hold values from -1.8 to 1.8
- table_rows: float32 [30720], P('fsdp'), may hold values from 3.0825835e-11 to 4.6238754e-10
- table_cols: float32 [768], replicated, may hold values from 3.0825835e-11 to 4.6238754e-10
- mats_rows: float32 [7, 768], P(None, 'fsdp'), may hold values from 3.0825835e-11 to 4.6238754e-10
- mats_cols: float32 [7, 768], replicated, may hold values from 3.0825835e-11 to 4.6238754e-10
- up_rows: float32 [768], P('fsdp'), may hold values from 3.0825835e-11 to 4.6238754e-10
- up_cols: float32 [3072], replicated, may hold values from 3.0825835e-11 to 4.6238754e-10
- down_rows: float32 [3072], P('fsdp'), may hold values from 3.0825835e-11 to 4.6238754e-10
- down_cols: float32 [768], replicated, may hold values from 3.0825835e-11 to 4.6238754e-10
- vectors_second: float32 [11, 768], P(None, 'fsdp'), may hold values from 1.5412918e-10 to 2.3119378e-09
- up_bias_second: float32 [3072], P('fsdp'), may hold values from 1.5412917e-11 to 6.165167e-11
Outputs:
- table_grad: float32 [30720, 768], P('fsdp')
- table_rows_new: float32 [30720], P('fsdp')
- table_cols_new: float32 [768], replicated
- table_new: float32 [30720, 768], P('fsdp')
- mats_grad: float32 [7, 768, 768], P(None, 'fsdp')
- mats_rows_new: float32 [7, 768], P(None, 'fsdp')
- mats_cols_new: float32 [7, 768], replicated
- mats_new: float32 [7, 768, 768], P(None, 'fsdp')
- up_grad: float32 [768, 3072], P('fsdp')
- up_rows_new: float32 [768], P('fsdp')
- up_cols_new: float32 [3072], replicated
- up_new: float32 [768, 3072], P('fsdp')
- down_grad: float32 [3072, 768], P('fsdp')
- down_rows_new: float32 [3072], P('fsdp')
- down_cols_new: float32 [768], replicated
- down_new: float32 [3072, 768], P('fsdp')
- vectors_grad: float32 [11, 768], P(None, 'fsdp')
- vectors_second_new: float32 [11, 768], P(None, 'fsdp')
- vectors_new: float32 [11, 768], P(None, 'fsdp')
- up_bias_grad: float32 [3072], P('fsdp')
- up_bias_second_new: float32 [3072], P('fsdp')
- up_bias_new: float32 [3072], P('fsdp')
- grad_norm: float32 [], replicated
- loss_parts: float32 [4], replicated
The draws below stay inside these ranges and needn't reach their ends.
Inputs may be any that keep to these rules, and one draw needn't show every extreme that they name: `lengths`: real tokens of each page; some page has exactly 512 and some exactly 40. `slots`: a slot's place along its page's real tokens, in 256ths of its length.
All inputs are finite; a program needn't handle non-finite values.
Results may differ from the reference program's by a relative error of at most 0.013.
The reference program's roundings to bfloat16 on the way count: a program that leaves them out, or rounds other values in their place, can miss the bound.
Values may be sent and summed in bfloat16 or wider, within the bound.
No kernel may reach another device: no remote copies, remote signals or barrier semaphores. Data moves between devices by JAX's collectives and lax.ppermute only.
A program may use at most 320 MiB of HBM per device.

```python
import math
from functools import partial
import jax
import jax.numpy as jnp
import numpy as np
from jax import lax

D = 768
HEADS = 12
HEAD_DIM = 64
FF = 3072
VOCAB = 30720
PAGE_LEN = 512
LEN_MIN = 40
M_TOK = 64
M_AREA = 64
QUANT = 1000
STEP = 10
PAGES_DEV = 1
GROUPS = 16
COPIES = 2
PAGES = 32
TOKENS = 16384
SLOTS = 128


def draw_lengths(key, part):
    key = jax.random.fold_in(key, 11)
    first, second = jax.random.split(key)
    page = jnp.arange(PAGES, dtype=jnp.int32)
    place = page // PAGES_DEV
    along = place // COPIES
    across = place % COPIES
    reach = ((along + 1) * COPIES + (across + 1) * GROUPS) * (PAGE_LEN - LEN_MIN) // (2 * GROUPS * COPIES)
    drawn = jax.random.randint(first, (PAGES,), LEN_MIN, LEN_MIN + 1 + reach)
    chosen = jax.random.randint(second, (), 0, PAGES)
    drawn = jnp.where(page == chosen, PAGE_LEN, drawn)
    other = (chosen + PAGES // 2 + 1) % PAGES
    drawn = jnp.where((page == other) & (other != chosen), LEN_MIN, drawn)
    return drawn.astype(jnp.int32)


def draw_slots(key, part):
    key = jax.random.fold_in(key, 13)
    first, second = jax.random.split(key)
    count = PAGES * SLOTS
    drawn = jax.random.randint(first, (count,), 0, 256)
    chosen = jax.random.randint(second, (), 0, count)
    index = jnp.arange(count, dtype=jnp.int32)
    drawn = jnp.where(index == chosen, 255, drawn)
    drawn = jnp.where(index == (chosen + 1) % count, 0, drawn)
    return drawn.reshape(PAGES, SLOTS).astype(jnp.int32)


def draw_table(key, part):
    key = jax.random.fold_in(key, 17)
    rise = jnp.arange(VOCAB, dtype=jnp.float32)[:, None] / VOCAB
    base = jax.random.normal(key, (VOCAB, D), jnp.float32)
    return base * (1.0 + 2.0 * rise) / (2.0 * math.sqrt(D))


def draw_mats(key, part):
    key = jax.random.fold_in(key, 19)
    factor = jnp.array([1.0, 0.5, 0.5, 1.0, 1.0, 1.0, 3.0], jnp.float32)[:, None, None] / math.sqrt(D)
    base = jax.random.normal(key, (7, D, D), jnp.float32)
    return base * factor


def draw_vectors(key, part):
    key = jax.random.fold_in(key, 23)
    first, second = jax.random.split(key)
    rise = jnp.arange(D, dtype=jnp.float32)[None, :] / D
    jitter = jax.random.uniform(first, (11, D), jnp.float32, 0.8, 1.25)
    ramp = 1.0 + 2.0 * rise
    noise = 0.3 * jax.random.normal(second, (11, D), jnp.float32)
    row = jnp.arange(11)[:, None]
    is_gain = (row == 0) | (row == 2) | (row == 4)
    return jnp.where(is_gain, ramp * jitter, noise)


def set_ends(values, key, smallest, top_value):
    longest = values.shape.index(max(values.shape))
    spots = []
    for shift in (0, 1):
        where = [jax.random.randint(jax.random.fold_in(key, axis), (), 0, length) for axis, length in enumerate(values.shape)]
        where[longest] = (where[longest] + shift) % values.shape[longest]
        spots.append(tuple(where))
    return values.at[spots[0]].set(smallest).at[spots[1]].set(top_value)


def block_levels(key, extent, cuts, low, high):
    loudness, own = 1.0, jax.random.fold_in(key, 6)
    for position, shards_of in cuts:
        heights = jnp.exp(jax.random.uniform(jax.random.fold_in(own, position), (shards_of,), jnp.float32, low / len(cuts), high / len(cuts)))
        loudness = loudness * jnp.repeat(heights, extent[position] // shards_of).reshape([-1 if axis == position else 1 for axis in range(len(extent))])
    return loudness


def rank_table(count, lean):
    portions = [(1 << 20) // math.isqrt(rank ** lean) + 1 for rank in range(1, count + 1)]
    scale = 1 + sum(portions) // (1 << 30)
    return np.cumsum(np.array([max(1, weight // scale) for weight in portions]))


def ranked(rng, extent, count, slope):
    grid = rank_table(count, slope)
    pick = jax.random.randint(jax.random.fold_in(rng, 1), extent, 0, int(grid[count - 1]))
    grade = jnp.searchsorted(jnp.asarray(grid, jnp.int32), pick, side="right")
    return jax.random.permutation(jax.random.fold_in(rng, 2), count)[grade].astype(jnp.int32)


def scatter_about(rng, shape, deviation, bound, pieces=(), kind=jnp.bfloat16):
    values = jax.random.normal(rng, shape, jnp.float32) * deviation
    if len(pieces) > 0:
        values = block_levels(rng, shape, pieces, -0.22, 0.18) * values
    return jnp.clip(values, min=-bound, max=bound).astype(kind)


def setup_inputs(seed: int = 0) -> dict:
    streams_of = jax.random.split(jax.random.key(seed), 22)
    token_ids = set_ends(ranked(streams_of[0], (TOKENS,), VOCAB, 2), jax.random.fold_in(streams_of[0], 3), 0, VOCAB - 1).astype(jnp.int32)
    boxes = set_ends(jax.random.randint(streams_of[1], (4, TOKENS), 0, QUANT), jax.random.fold_in(streams_of[1], 1), 0, QUANT - 1).astype(jnp.int32)
    lengths = draw_lengths(jax.random.fold_in(streams_of[21], 71), 0)
    slots = draw_slots(jax.random.fold_in(streams_of[21], 71), 0)
    labels = set_ends(ranked(streams_of[4], (PAGES, SLOTS), VOCAB, 2), jax.random.fold_in(streams_of[4], 3), 0, VOCAB - 1).astype(jnp.int32)
    table = draw_table(jax.random.fold_in(streams_of[21], 71), 0)
    mats = draw_mats(jax.random.fold_in(streams_of[21], 71), 0)
    up = scatter_about(streams_of[7], (D, FF), D ** -0.5, 0.21875, ((0, 16),), jnp.float32)
    down = scatter_about(streams_of[8], (FF, D), FF ** -0.5, 0.109375, ((0, 16),), jnp.float32)
    vectors = draw_vectors(jax.random.fold_in(streams_of[21], 71), 0)
    up_bias = scatter_about(streams_of[10], (FF,), 0.3, 1.8, ((0, 16),), jnp.float32)
    table_rows = jnp.clip(jnp.exp(math.log(4.6238754491945144e-10) - 2.7080502 * jax.random.uniform(streams_of[11], (VOCAB,), jnp.float32) ** block_levels(streams_of[11], (VOCAB,), ((0, 16),), -0.2, 0.2)), 3.082583494018465e-11, 4.6238754491945144e-10)
    table_cols = jnp.clip(jnp.exp(jax.random.uniform(streams_of[12], (D,), jnp.float32, math.log(3.082583494018465e-11), math.log(4.6238754491945144e-10))), 3.082583494018465e-11, 4.6238754491945144e-10)
    mats_rows = jnp.clip(jnp.exp(math.log(4.6238754491945144e-10) - 2.7080502 * jax.random.uniform(streams_of[13], (7, D), jnp.float32) ** block_levels(streams_of[13], (7, D), ((1, 16),), -0.2, 0.2)), 3.082583494018465e-11, 4.6238754491945144e-10)
    mats_cols = jnp.clip(jnp.exp(jax.random.uniform(streams_of[14], (7, D), jnp.float32, math.log(3.082583494018465e-11), math.log(4.6238754491945144e-10))), 3.082583494018465e-11, 4.6238754491945144e-10)
    up_rows = jnp.clip(jnp.exp(math.log(4.6238754491945144e-10) - 2.7080502 * jax.random.uniform(streams_of[15], (D,), jnp.float32) ** block_levels(streams_of[15], (D,), ((0, 16),), -0.2, 0.2)), 3.082583494018465e-11, 4.6238754491945144e-10)
    up_cols = jnp.clip(jnp.exp(jax.random.uniform(streams_of[16], (FF,), jnp.float32, math.log(3.082583494018465e-11), math.log(4.6238754491945144e-10))), 3.082583494018465e-11, 4.6238754491945144e-10)
    down_rows = jnp.clip(jnp.exp(math.log(4.6238754491945144e-10) - 2.7080502 * jax.random.uniform(streams_of[17], (FF,), jnp.float32) ** block_levels(streams_of[17], (FF,), ((0, 16),), -0.2, 0.2)), 3.082583494018465e-11, 4.6238754491945144e-10)
    down_cols = jnp.clip(jnp.exp(jax.random.uniform(streams_of[18], (D,), jnp.float32, math.log(3.082583494018465e-11), math.log(4.6238754491945144e-10))), 3.082583494018465e-11, 4.6238754491945144e-10)
    vectors_second = jnp.clip(jnp.exp(math.log(2.311937752352833e-09) - 2.7080502 * jax.random.uniform(streams_of[19], (11, D), jnp.float32) ** block_levels(streams_of[19], (11, D), ((1, 16),), -0.2, 0.2)), 1.5412918163981715e-10, 2.311937752352833e-09)
    up_bias_second = jnp.clip(jnp.exp(math.log(6.16516698803693e-11) - 1.3862944 * jax.random.uniform(streams_of[20], (FF,), jnp.float32) ** block_levels(streams_of[20], (FF,), ((0, 16),), -0.2, 0.2)), 1.5412917470092324e-11, 6.16516698803693e-11)
    return dict(token_ids=token_ids, boxes=boxes, lengths=lengths, slots=slots, labels=labels, table=table, mats=mats, up=up, down=down, vectors=vectors, up_bias=up_bias, table_rows=table_rows, table_cols=table_cols, mats_rows=mats_rows, mats_cols=mats_cols, up_rows=up_rows, up_cols=up_cols, down_rows=down_rows, down_cols=down_cols, vectors_second=vectors_second, up_bias_second=up_bias_second)


EPSILON = 1e-05
CLIP_NORM = 0.1
LEARN_RATE = 0.02
VECTOR_RATE = 0.3
TINY_TERM = 1e-30
NEGATIVE = -1e+30
HIGHEST = lax.Precision.HIGHEST

@jax.custom_vjp
def low(v):
    return lax.optimization_barrier(v.astype(jnp.bfloat16)).astype(jnp.float32)

@jax.custom_vjp
def low_back(v):
    return v

def low_keep(v):
    return (low(v), None)

def low_pass(kept, grad):
    return (grad,)

def back_keep(v):
    return (v, None)

def back_low(kept, grad):
    return (low(grad),)
low.defvjp(low_keep, low_pass)
low_back.defvjp(back_keep, back_low)

def rounded(value):
    return low(low_back(value))

def matmul(left, right):
    return jnp.dot(left, right, precision=HIGHEST, preferred_element_type=jnp.float32)

def layer_norm(value, gain, shift):
    center = value - lax.optimization_barrier(jnp.mean(value, axis=-1, keepdims=True))
    spread = lax.optimization_barrier(jnp.mean(center * center, axis=-1, keepdims=True))
    return center * lax.rsqrt(spread + EPSILON) * gain + shift

def box_features(boxes):
    count = D // 8
    freqs = jnp.exp(-math.log(10000.0) * jnp.arange(count, dtype=jnp.float32) / count)
    angle = boxes.astype(jnp.float32)[:, :, None] * freqs[None, None, :]
    waves = jnp.concatenate([jnp.sin(angle), jnp.cos(angle)], axis=2)
    return jnp.transpose(waves, (1, 0, 2)).reshape(boxes.shape[1], D)

def slot_info(lengths, slots):
    n_tok = jnp.minimum(M_TOK, 1 + lengths * M_TOK // PAGE_LEN)
    n_area = jnp.minimum(M_AREA, 1 + lengths * (3 * M_AREA) // (4 * PAGE_LEN))
    index = jnp.arange(M_TOK + M_AREA, dtype=jnp.int32)[None, :]
    valid = jnp.where(index < M_TOK, index < n_tok[:, None], index - M_TOK < n_area[:, None])
    where_at = (slots * lengths[:, None] // 256).astype(jnp.int32)
    return (valid, where_at)

def split_heads(value):
    return value.reshape(PAGE_LEN, HEADS, HEAD_DIM)

def page_loss(weights, token_ids, features, length, where_at, labels, scale, valid):
    table, mats, up, down, vectors, up_bias = weights
    keep = jnp.arange(PAGE_LEN) < length
    start_state = layer_norm(table[token_ids], vectors[0], vectors[1])
    act = low(start_state)
    place = rounded(matmul(low(features), mats[0]) + vectors[9])
    query = split_heads(rounded(matmul(act, mats[1]) + vectors[6]))
    keys = split_heads(rounded(matmul(act, mats[2])))
    values = split_heads(rounded(matmul(act, mats[3]) + vectors[7]))
    box_query = split_heads(rounded(matmul(place, mats[4])))
    box_key = split_heads(rounded(matmul(place, mats[5])))
    score = jnp.einsum('qhe,khe->hqk', query, keys, precision=HIGHEST)
    score = score + jnp.einsum('qhe,khe->hqk', query, box_key, precision=HIGHEST)
    score = score + jnp.einsum('qhe,khe->hqk', box_query, keys, precision=HIGHEST)
    score = low_back(score * HEAD_DIM ** (-0.5))
    score = jnp.where(keep[None, None, :], score, NEGATIVE)
    peak = lax.optimization_barrier(jnp.max(score, axis=-1, keepdims=True))
    expo = jnp.exp(score - peak)
    prob = expo / lax.optimization_barrier(jnp.sum(expo, axis=-1, keepdims=True))
    mixed = jnp.einsum('hqk,khe->qhe', low(prob), values, precision=HIGHEST)
    mixed = rounded(mixed.reshape(PAGE_LEN, D))
    attended = low_back(matmul(mixed, mats[6]) + vectors[8])
    middle = layer_norm(start_state + attended, vectors[2], vectors[3])
    upper = low_back(matmul(low(middle), up) + up_bias)
    active = low(jax.nn.gelu(upper, approximate=False))
    feed = low_back(matmul(active, down) + vectors[10])
    final = layer_norm(middle + feed, vectors[4], vectors[5])
    rows = low(final[where_at])
    logits = low_back(matmul(rows, table.T))
    top = lax.optimization_barrier(jnp.max(logits, axis=-1, keepdims=True))
    log_total = top[:, 0] + jnp.log(lax.optimization_barrier(jnp.sum(jnp.exp(logits - top), axis=-1)))
    target = lax.optimization_barrier(jnp.sum(rows * table[labels], axis=-1))
    loss_rows = log_total - target
    is_token = jnp.arange(M_TOK + M_AREA) < M_TOK
    parts = jnp.stack([jnp.sum(jnp.where(is_token, valid * loss_rows, 0.0)), jnp.sum(jnp.where(is_token, 0.0, valid * loss_rows))])
    return (jnp.sum(scale * loss_rows), parts)

def factored(grad, weight, rows, cols, decay):
    square = grad * grad + TINY_TERM
    rows_new = decay * rows + (1.0 - decay) * lax.optimization_barrier(jnp.mean(square, axis=-1))
    cols_new = decay * cols + (1.0 - decay) * lax.optimization_barrier(jnp.mean(square, axis=-2))
    second = rows_new[..., :, None] * cols_new[..., None, :] / lax.optimization_barrier(jnp.mean(rows_new, axis=-1))[..., None, None]
    return (rows_new, cols_new, weight - LEARN_RATE * grad * lax.rsqrt(second))

def plain(grad, weight, second, decay):
    second_new = decay * second + (1.0 - decay) * (grad * grad + TINY_TERM)
    return (second_new, weight - VECTOR_RATE * grad * lax.rsqrt(second_new))

def reference(token_ids, boxes, lengths, slots, labels, table, mats, up, down, vectors, up_bias, table_rows, table_cols, mats_rows, mats_cols, up_rows, up_cols, down_rows, down_cols, vectors_second, up_bias_second):
    valid, where_at = slot_info(lengths, slots)
    is_token = (jnp.arange(M_TOK + M_AREA) < M_TOK)[None, :]
    validf = valid.astype(jnp.float32)
    count_token = jnp.sum(jnp.where(is_token, validf, 0.0))
    count_area = jnp.sum(jnp.where(is_token, 0.0, validf))
    scale = validf * jnp.where(is_token, 1.0 / count_token, 1.0 / count_area)
    features = box_features(boxes).reshape(PAGES, PAGE_LEN, D)
    block = math.gcd(PAGES, max(1, 4096 // PAGE_LEN))
    data = (token_ids.reshape(PAGES, PAGE_LEN), features, lengths, where_at, labels, scale, validf)
    data = tuple((item.reshape((PAGES // block, block) + item.shape[1:]) for item in data))

    def total_loss(params):
        weights = tuple((low(item) for item in params))

        def run(carry, batch):
            losses, parts = jax.vmap(partial(page_loss, weights))(*batch)
            return (carry + jnp.sum(losses), lax.optimization_barrier(jnp.sum(parts, axis=0)))
        loss, parts = lax.scan(jax.checkpoint(run), jnp.zeros((), jnp.float32), data)
        return (loss, lax.optimization_barrier(jnp.sum(parts, axis=0)))
    params = (table, mats, up, down, vectors, up_bias)
    loss, pull, parts = jax.vjp(total_loss, params, has_aux=True)
    grads = pull(jnp.ones((), jnp.float32))[0]
    norm_sq = sum((jnp.sum(item * item) for item in grads))
    grad_norm = jnp.sqrt(norm_sq)
    clip = jnp.minimum(1.0, CLIP_NORM / grad_norm)
    table_grad, mats_grad, up_grad, down_grad, vectors_grad, bias_grad = tuple((item * clip for item in grads))
    decay = 1.0 - STEP ** (-0.8)
    table_rows_new, table_cols_new, table_new = factored(table_grad, table, table_rows, table_cols, decay)
    mats_rows_new, mats_cols_new, mats_new = factored(mats_grad, mats, mats_rows, mats_cols, decay)
    up_rows_new, up_cols_new, up_new = factored(up_grad, up, up_rows, up_cols, decay)
    down_rows_new, down_cols_new, down_new = factored(down_grad, down, down_rows, down_cols, decay)
    vectors_second_new, vectors_new = plain(vectors_grad, vectors, vectors_second, decay)
    bias_second_new, bias_new = plain(bias_grad, up_bias, up_bias_second, decay)
    loss_parts = jnp.stack([parts[0], count_token, parts[1], count_area])
    return (table_grad, table_rows_new, table_cols_new, table_new, mats_grad, mats_rows_new, mats_cols_new, mats_new, up_grad, up_rows_new, up_cols_new, up_new, down_grad, down_rows_new, down_cols_new, down_new, vectors_grad, vectors_second_new, vectors_new, bias_grad, bias_second_new, bias_new, grad_norm, loss_parts)
```

```python
from functools import partial
import math
from typing import NamedTuple

import jax
import jax.numpy as jnp
from jax import lax
from jax.experimental import pallas as pl
from jax.experimental.pallas import tpu as pltpu
from jax.sharding import PartitionSpec as P

HEAD_DIM = 64
PAGE_LEN = 512
M_TOK = 64
M_AREA = 64
STEP = 10


EPSILON = 1e-05
CLIP_NORM = 0.1
LEARN_RATE = 0.02
VECTOR_RATE = 0.3
TINY_TERM = 1e-30
NEGATIVE = -1e30
BFLOAT = jnp.bfloat16
FLOAT = jnp.float32
LANES = 128
DECAY = 1.0 - STEP ** (-0.8)


class Line(NamedTuple):
    axis: str
    total: int
    stride: int
    count: int


def lines_of(groups, copies):
    cores = min(2, groups)
    rest = (groups // cores).bit_length() - 1
    y_count = 1 << (rest // 2)
    z_count = groups // (cores * y_count)
    return {
        "z": Line("fsdp", groups, cores * y_count, z_count),
        "y": Line("fsdp", groups, cores, y_count),
        "core": Line("fsdp", groups, 1, cores),
        "x": Line("rep", copies, 1, copies),
    }


def place_on(line):
    return lax.axis_index(line.axis) // line.stride % line.count


def hop(value, line, step, senders):
    pairs = [
        (i, i + step * line.stride)
        for i in range(line.total)
        if i // line.stride % line.count in senders
    ]
    return lax.ppermute(value, line.axis, pairs)


def swap(value, line):
    pairs = [
        (i, i + line.stride if i // line.stride % 2 == 0 else i - line.stride)
        for i in range(line.total)
    ]
    return lax.ppermute(value, line.axis, pairs)


def gather_line(value, line, axis):
    count = line.count
    if count == 1:
        return value
    here = place_on(line)
    if count == 2:
        other = swap(value, line)
        first = jnp.where(here == 0, value, other)
        second = jnp.where(here == 0, other, value)
        return jnp.concatenate([first, second], axis=axis)
    lower, upper = [value], [value]
    for step in range(1, count):
        lower.append(hop(lower[-1], line, 1, range(step - 1, count - 1)))
        upper.append(hop(upper[-1], line, -1, range(1, count - step + 1)))
    blocks = []
    for place in range(count):
        choices = [upper[place - i] if i <= place else lower[i - place] for i in range(count)]
        blocks.append(lax.select_n(here, *choices))
    return jnp.concatenate(blocks, axis=axis)


def reduce_line(value, line, axis):
    count = line.count
    if count == 1:
        return value.astype(FLOAT)
    here = place_on(line)
    size = value.shape[axis] // count

    def block(place):
        return lax.dynamic_slice_in_dim(value, place * size, size, axis)

    if count == 2:
        return block(here).astype(FLOAT) + swap(block(1 - here).astype(BFLOAT), line).astype(FLOAT)
    lower = upper = None
    for step in range(count - 1):
        to_upper = block(jnp.minimum(here + count - 1 - step, count - 1)).astype(FLOAT)
        to_lower = block(jnp.maximum(here - (count - 1 - step), 0)).astype(FLOAT)
        if lower is not None:
            to_upper = to_upper + lower
            to_lower = to_lower + upper
        lower = hop(to_upper.astype(BFLOAT), line, 1, range(0, step + 1)).astype(FLOAT)
        upper = hop(to_lower.astype(BFLOAT), line, -1, range(count - 1 - step, count)).astype(FLOAT)
    return block(here).astype(FLOAT) + (lower + upper)


def paired(value, axis, combine):
    size = lax.axis_size(axis)
    bit = 1
    while bit < size:
        pairs = [(i, i ^ bit) for i in range(size)]
        value = combine(value, jax.tree.map(lambda v: lax.ppermute(v, axis, pairs), value))
        bit *= 2
    return value


def gather_weight(value, lines, order):
    x = lines["x"]
    part = value.shape[2] // x.count
    piece = lax.dynamic_slice_in_dim(value, place_on(x) * part, part, 2)
    piece = piece[:, None, None, None]
    axes = {"z": 1, "y": 2, "core": 3, "x": 5}
    for name in order:
        piece = gather_line(piece, lines[name], axes[name])
    count, rows, columns = value.shape
    return piece.reshape(count, -1, columns)


def reduce_weight(value, lines, order):
    count, _, columns = value.shape
    z, y, core = lines["z"].count, lines["y"].count, lines["core"].count
    piece = value.reshape(count, z, y, core, -1, columns)
    axes = {"z": 1, "y": 2, "core": 3, "x": 5}
    for name in order:
        piece = reduce_line(piece, lines[name], axes[name]).astype(BFLOAT)
    return gather_line(piece[:, 0, 0, 0], lines["x"], 2).astype(FLOAT)


def layer_norm(value, gain, shift):
    center = value - jnp.mean(value, axis=-1, keepdims=True)
    spread = jnp.mean(center * center, axis=-1, keepdims=True)
    return center * lax.rsqrt(spread + EPSILON) * gain + shift


def box_features(boxes, width):
    count = width // 8
    freqs = jnp.exp(-math.log(10000.0) * jnp.arange(count, dtype=FLOAT) / count)
    angle = boxes.astype(FLOAT)[:, :, None] * freqs[None, None, :]
    waves = jnp.concatenate([jnp.sin(angle), jnp.cos(angle)], axis=2)
    return jnp.transpose(waves, (1, 0, 2)).reshape(boxes.shape[1], width)


def valid_slots(lengths, slot_count):
    n_tok = jnp.minimum(M_TOK, 1 + lengths * M_TOK // PAGE_LEN)
    n_area = jnp.minimum(M_AREA, 1 + lengths * (3 * M_AREA) // (4 * PAGE_LEN))
    index = jnp.arange(slot_count, dtype=jnp.int32)[None, :]
    return jnp.where(index < M_TOK, index < n_tok[:, None], index - M_TOK < n_area[:, None])


def product(left, right):
    return jnp.dot(left, right, preferred_element_type=FLOAT)


def contract_rows(left, right):
    return lax.dot_general(left, right, (((0,), (0,)), ((), ())), preferred_element_type=FLOAT)


def times_transposed(left, right):
    return lax.dot_general(left, right, (((1,), (1,)), ((), ())), preferred_element_type=FLOAT)


def two_parts(value):
    high = value.astype(BFLOAT)
    return high, (value - high.astype(FLOAT)).astype(BFLOAT)


def side(index):
    lane = lax.broadcasted_iota(jnp.int32, (1, LANES), 1)
    return lane // HEAD_DIM == index


def only(mask, value):
    return jnp.where(mask, value, jnp.zeros_like(value))


def attend_kernel(length_ref, query_ref, key_ref, value_ref, box_query_ref, box_key_ref, out_ref):
    length = length_ref[pl.program_id(0)]
    query, key, box_query, box_key = query_ref[...], key_ref[...], box_query_ref[...], box_key_ref[...]
    keys = jnp.concatenate([key, box_key, key], axis=1)
    keep = lax.broadcasted_iota(jnp.int32, (1, key.shape[0]), 1) < length
    mixed = jnp.zeros(out_ref.shape, FLOAT)
    for head in range(LANES // HEAD_DIM):
        mask = side(head)
        own = only(mask, query)
        score = times_transposed(jnp.concatenate([own, own, only(mask, box_query)], axis=1), keys)
        score = jnp.where(keep, score * HEAD_DIM ** (-0.5), NEGATIVE)
        expo = jnp.exp(score - jnp.max(score, axis=1, keepdims=True))
        prob = (expo * (1.0 / jnp.sum(expo, axis=1, keepdims=True))).astype(BFLOAT)
        mixed = jnp.where(mask, product(prob, value_ref[...]), mixed)
    out_ref[...] = mixed.astype(BFLOAT)


def attend_back_kernel(
    length_ref,
    query_ref,
    key_ref,
    value_ref,
    box_query_ref,
    box_key_ref,
    grad_ref,
    grad_query_ref,
    grad_key_ref,
    grad_value_ref,
    grad_box_query_ref,
    grad_box_key_ref,
):
    length = length_ref[pl.program_id(0)]
    query, key, value, box_query, box_key = (
        query_ref[...],
        key_ref[...],
        value_ref[...],
        box_query_ref[...],
        box_key_ref[...],
    )
    grad = grad_ref[...]
    rows = key.shape[0]
    keys = jnp.concatenate([key, box_key, key], axis=1)
    both_queries = jnp.concatenate([query, box_query], axis=1)
    both_keys = jnp.concatenate([key, box_key], axis=1)
    keep = lax.broadcasted_iota(jnp.int32, (rows, 1), 0) < length
    outs = [jnp.zeros((rows, LANES), FLOAT) for _ in range(5)]
    for head in range(LANES // HEAD_DIM):
        mask = side(head)
        own = only(mask, query)
        score = times_transposed(keys, jnp.concatenate([own, own, only(mask, box_query)], axis=1))
        score = jnp.where(keep, score * HEAD_DIM ** (-0.5), NEGATIVE)
        expo = jnp.exp(score - jnp.max(score, axis=0, keepdims=True))
        prob = expo * (1.0 / jnp.sum(expo, axis=0, keepdims=True))
        grad_value = product(prob.astype(BFLOAT), grad)
        grad_prob = times_transposed(only(mask, value), grad)
        grad_score = prob * (grad_prob - jnp.sum(prob * grad_prob, axis=0, keepdims=True))
        low = grad_score.astype(BFLOAT) * jnp.asarray(HEAD_DIM ** (-0.5), BFLOAT)
        with_queries = product(low, both_queries)
        with_keys = contract_rows(low, both_keys)
        fresh = (
            with_keys[:, :LANES] + with_keys[:, LANES:],
            with_queries[:, :LANES] + with_queries[:, LANES:],
            grad_value,
            with_keys[:, :LANES],
            with_queries[:, :LANES],
        )
        outs = [jnp.where(mask, new, old) for new, old in zip(fresh, outs)]
    for ref, out in zip(
        (grad_query_ref, grad_key_ref, grad_value_ref, grad_box_query_ref, grad_box_key_ref), outs
    ):
        ref[...] = out.astype(BFLOAT)


def attention_call(kernel, lengths, arrays, out_count):
    tokens, width = arrays[0].shape
    pages = lengths.shape[0]
    spec = pl.BlockSpec((tokens // pages, LANES), lambda page, pair: (page, pair))
    out = jax.ShapeDtypeStruct((tokens, width), BFLOAT)
    return pl.pallas_call(
        kernel,
        grid=(pages, width // LANES),
        in_specs=[pl.BlockSpec(memory_space=pltpu.SMEM)] + [spec] * len(arrays),
        out_specs=[spec] * out_count,
        out_shape=[out] * out_count,
        compiler_params=pltpu.CompilerParams(vmem_limit_bytes=48 * 1024 * 1024),
    )(lengths, *arrays)


class Buckets(NamedTuple):
    owner: jax.Array
    row: jax.Array
    first: jax.Array
    rank: jax.Array
    fullest: jax.Array


def bucket_ids(ids, shard_rows):
    owner, row = ids // shard_rows, ids % shard_rows
    index = jnp.arange(ids.shape[0], dtype=jnp.int32)
    earlier = index[None, :] < index[:, None]
    same = ids[:, None] == ids[None, :]
    first = ~jnp.any(same & earlier, axis=1)
    before = (owner[:, None] == owner[None, :]) & earlier & first[None, :]
    rank = jnp.sum(before.astype(jnp.int32), axis=1)
    rank = jnp.sum(jnp.where(same & first[None, :], rank[None, :], 0), axis=1)
    return Buckets(owner, row, first, rank, jnp.max(rank) + 1)


def bucket_places(buckets, capacity, turn):
    shifted = buckets.rank - turn * capacity
    inside = (shifted >= 0) & (shifted < capacity)
    return jnp.where(inside, buckets.owner * capacity + shifted, -1)


def bucket_requests(buckets, places, groups, capacity):
    hit = (places[:, None] == jnp.arange(groups * capacity)[None, :]) & buckets.first[:, None]
    return jnp.sum(jnp.where(hit, buckets.row[:, None], 0), axis=0).reshape(groups, capacity)


def one_hot(index, count):
    return (index[:, None] == jnp.arange(count, dtype=jnp.int32)[None, :]).astype(BFLOAT)


def layer_forward(weights, embedded, place, box_query, box_key, lengths):
    mats, up, down, gains, up_bias = weights
    start_state = layer_norm(embedded, gains[0], gains[1])
    act = start_state.astype(BFLOAT)
    query = (product(act, mats[1]) + gains[6]).astype(BFLOAT)
    keys = product(act, mats[2]).astype(BFLOAT)
    values = (product(act, mats[3]) + gains[7]).astype(BFLOAT)
    (mixed,) = attention_call(attend_kernel, lengths, (query, keys, values, box_query, box_key), 1)
    first_sum = start_state + (product(mixed, mats[6]) + gains[8])
    middle = layer_norm(first_sum, gains[2], gains[3])
    middle_low = middle.astype(BFLOAT)
    upper = product(middle_low, up) + up_bias
    active = jax.nn.gelu(upper, approximate=False).astype(BFLOAT)
    second_sum = middle + (product(active, down) + gains[10])
    kept = (
        embedded,
        act,
        place,
        query,
        keys,
        values,
        box_query,
        box_key,
        mixed,
        first_sum,
        middle_low,
        upper,
        active,
        second_sum,
    )
    return (layer_norm(second_sum, gains[4], gains[5]), kept)


def layer_backward(weights, features_low, lengths, kept, grad_out, lines):
    mats, up, down, gains, up_bias = weights
    (
        embedded,
        act,
        place,
        query,
        keys,
        values,
        box_query,
        box_key,
        mixed,
        first_sum,
        middle_low,
        upper,
        active,
        second_sum,
    ) = kept

    def column_sum(value):
        return jnp.sum(value.astype(FLOAT), axis=0)

    grad_second, gain_four, gain_five = jax.vjp(layer_norm, second_sum, gains[4], gains[5])[1](
        grad_out
    )
    order = ("core", "y", "z", "x")
    grad_feed = grad_second.astype(BFLOAT)
    grad_down = reduce_weight(contract_rows(active, grad_feed)[None], lines, order)
    grad_active = times_transposed(grad_feed, down)
    grad_upper = jax.vjp(partial(jax.nn.gelu, approximate=False), upper)[1](grad_active)[0].astype(
        BFLOAT
    )
    grad_up = reduce_weight(contract_rows(middle_low, grad_upper)[None], lines, order)
    grad_middle = grad_second + times_transposed(grad_upper, up)
    grad_first, gain_two, gain_three = jax.vjp(layer_norm, first_sum, gains[2], gains[3])[1](
        grad_middle
    )
    grad_attended = grad_first.astype(BFLOAT)
    grad_output = contract_rows(mixed, grad_attended)
    grad_mixed = times_transposed(grad_attended, mats[6]).astype(BFLOAT)
    grad_query, grad_keys, grad_values, grad_box_query, grad_box_key = attention_call(
        attend_back_kernel, lengths, (query, keys, values, box_query, box_key, grad_mixed), 5
    )
    grad_place = (
        times_transposed(grad_box_query, mats[4]) + times_transposed(grad_box_key, mats[5])
    ).astype(BFLOAT)
    grad_start = (
        grad_first + times_transposed(grad_query, mats[1]) + times_transposed(grad_keys, mats[2])
    )
    grad_start = grad_start + times_transposed(grad_values, mats[3])
    grad_embedded, gain_zero, gain_one = jax.vjp(layer_norm, embedded, gains[0], gains[1])[1](
        grad_start
    )
    grad_mats = jnp.stack(
        [
            contract_rows(features_low, grad_place),
            contract_rows(act, grad_query),
            contract_rows(act, grad_keys),
            contract_rows(act, grad_values),
            contract_rows(place, grad_box_query),
            contract_rows(place, grad_box_key),
            grad_output,
        ]
    )
    grad_mats = reduce_weight(grad_mats, lines, order)
    grad_vectors = jnp.stack(
        [
            gain_zero,
            gain_one,
            gain_two,
            gain_three,
            gain_four,
            gain_five,
            column_sum(grad_query),
            column_sum(grad_values),
            column_sum(grad_attended),
            column_sum(grad_place),
            column_sum(grad_feed),
        ]
    )
    layer_grads = (grad_mats, grad_up[0], grad_down[0], grad_vectors, column_sum(grad_upper))
    return (layer_grads, grad_embedded)


def combine_mass(first, second):
    peak = jnp.maximum(first[0], second[0])
    mass = first[1] * jnp.exp(first[0] - peak) + second[1] * jnp.exp(second[0] - peak)
    return (peak, mass, first[2] + second[2])


def add_trees(first, second):
    return jax.tree.map(jnp.add, first, second)


def body(
    token_ids,
    boxes,
    lengths,
    slots,
    labels,
    table,
    mats,
    up,
    down,
    vectors,
    up_bias,
    table_rows,
    table_cols,
    mats_rows,
    mats_cols,
    up_rows,
    up_cols,
    down_rows,
    down_cols,
    vectors_second,
    up_bias_second,
):
    pages = lengths.shape[0]
    tokens = token_ids.shape[0]
    page_len = tokens // pages
    width = table.shape[1]
    shard_rows = table.shape[0]
    slot_count = slots.shape[1]
    groups, copies = lax.axis_size("fsdp"), lax.axis_size("rep")
    group, copy = lax.axis_index("fsdp"), lax.axis_index("rep")
    lines = lines_of(groups, copies)
    depth = mats.shape[0]
    table_low = table.astype(BFLOAT)

    capacity = 16 + -(-tokens // (16 * groups)) * 16
    buckets = bucket_ids(token_ids, shard_rows)
    places = bucket_places(buckets, capacity, 0)
    requests = bucket_requests(buckets, places, groups, capacity)
    own_news = jnp.concatenate([labels.reshape(-1), lengths, buckets.fullest[None]])
    news = jnp.concatenate(
        [
            jnp.repeat(requests, copies, axis=0),
            jnp.broadcast_to(own_news[None], (groups * copies, own_news.shape[0])),
        ],
        axis=1,
    )
    news = lax.all_to_all(news, ("fsdp", "rep"), 0, 0, tiled=True)
    asked = news[:, :capacity].reshape(groups, copies, capacity)
    asked = jnp.transpose(asked, (1, 0, 2)).reshape(copies, groups * capacity)
    labels_all = news[:, capacity : capacity + pages * slot_count]
    labels_all = labels_all.reshape(groups, copies, pages * slot_count)
    labels_all = lax.dynamic_index_in_dim(labels_all, copy, 1, False).reshape(-1)
    lengths_all = news[:, capacity + pages * slot_count : -1]
    turns = (jnp.max(news[:, -1]) + capacity - 1) // capacity

    def fetch(spots, wanted):
        rows = product(one_hot(wanted, shard_rows), table_low).astype(BFLOAT)
        rows = lax.all_to_all(rows.reshape(groups, capacity, width), "fsdp", 0, 0, tiled=True)
        return product(one_hot(spots, groups * capacity), rows.reshape(groups * capacity, width))

    def ask(turn):
        spots = bucket_places(buckets, capacity, turn)
        wanted = bucket_requests(buckets, spots, groups, capacity)
        return spots, lax.all_to_all(wanted, "fsdp", 0, 0, tiled=True).reshape(-1)

    embedded = fetch(places, lax.dynamic_index_in_dim(asked, copy, 0, False))
    embedded = lax.while_loop(
        lambda state: state[0] < turns,
        lambda state: (state[0] + 1, state[1] + fetch(*ask(state[0]))),
        (jnp.int32(1), embedded),
    )[1]

    mats_low = mats.astype(BFLOAT)
    small = jnp.concatenate([vectors.astype(BFLOAT).reshape(-1), up_bias.astype(BFLOAT)])[None]

    def lay(first, second, bit):
        low = (group & bit) == 0
        return jnp.concatenate([jnp.where(low, first, second), jnp.where(low, second, first)])

    bit = 1
    while bit < groups:
        pairs = [(i, i ^ bit) for i in range(groups)]
        small = lay(small, lax.ppermute(small, "fsdp", pairs), bit)
        bit *= 2
    split = vectors.size
    gains = small[:, :split].reshape(groups, vectors.shape[0], -1)
    gains = jnp.transpose(gains, (1, 0, 2)).reshape(vectors.shape[0], width).astype(FLOAT)
    bias = small[:, split:].reshape(-1).astype(FLOAT)
    box_mats = gather_weight(
        jnp.stack([mats_low[0], mats_low[4], mats_low[5]]), lines, ("z", "x", "y", "core")
    )
    token_mats = gather_weight(mats_low[1:4], lines, ("z", "y", "x", "core"))
    out_mat = gather_weight(mats_low[6:7], lines, ("z", "y", "x", "core"))
    up_low = gather_weight(up.astype(BFLOAT)[None], lines, ("z", "x", "y", "core"))[0]
    down_low = gather_weight(down.astype(BFLOAT)[None], lines, ("z", "y", "x", "core"))[0]
    layer_mats = (
        box_mats[0],
        token_mats[0],
        token_mats[1],
        token_mats[2],
        box_mats[1],
        box_mats[2],
        out_mat[0],
    )
    weights = (layer_mats, up_low, down_low, gains, bias)

    features_low = box_features(boxes, width).astype(BFLOAT)
    place = (product(features_low, layer_mats[0]) + gains[9]).astype(BFLOAT)
    box_query = product(place, layer_mats[4]).astype(BFLOAT)
    box_key = product(place, layer_mats[5]).astype(BFLOAT)
    top_state, kept = layer_forward(weights, embedded, place, box_query, box_key, lengths)

    where_at = slots * lengths[:, None] // 256 + jnp.arange(pages)[:, None] * page_len
    pick = one_hot(where_at.reshape(-1), tokens)
    rows_low = product(pick, top_state.astype(BFLOAT)).astype(BFLOAT)
    rows_all = rows_low[None, None, None]
    for axis, name in enumerate(("z", "y", "core")):
        rows_all = gather_line(rows_all, lines[name], axis)
    rows_all = rows_all.reshape(-1, width)
    logits = times_transposed(rows_all, table_low)
    mine = labels_all[:, None] - group * shard_rows == jnp.arange(shard_rows)[None, :]
    peak = jnp.max(logits, axis=1)
    mass = jnp.sum(jnp.exp(logits - peak[:, None]), axis=1)
    target = jnp.sum(jnp.where(mine, logits, 0.0), axis=1)
    peak, mass, target = paired((peak, mass, target), "fsdp", combine_mass)
    log_total = peak + jnp.log(mass)

    is_token = jnp.arange(slot_count) < M_TOK
    valid_all = valid_slots(lengths_all.reshape(-1), slot_count).astype(FLOAT)
    count_token = jnp.sum(jnp.where(is_token, valid_all, 0.0))
    count_area = jnp.sum(jnp.where(is_token, 0.0, valid_all))
    valid = valid_all.reshape(groups, copies, pages, slot_count)
    valid = lax.dynamic_index_in_dim(valid, copy, 1, False).reshape(-1, slot_count)
    loss_rows = (log_total - target).reshape(-1, slot_count) * valid
    sums = jnp.stack(
        [jnp.sum(jnp.where(is_token, loss_rows, 0.0)), jnp.sum(jnp.where(is_token, 0.0, loss_rows))]
    )
    sums = paired(sums, "rep", jnp.add)
    loss_parts = jnp.stack([sums[0], count_token, sums[1], count_area])
    share = jnp.where(is_token, 1.0 / count_token, 1.0 / count_area)
    weight = (valid * share[None, :]).reshape(-1)
    grad_logits = (jnp.exp(logits - log_total[:, None]) - mine.astype(FLOAT)).astype(BFLOAT)
    grad_rows = product(grad_logits, table_low) * weight[:, None]
    grad_rows = grad_rows.reshape(
        lines["z"].count, lines["y"].count, lines["core"].count, -1, width
    )
    for axis, name in ((2, "core"), (1, "y"), (0, "z")):
        grad_rows = reduce_line(grad_rows.astype(BFLOAT), lines[name], axis)
    grad_rows = grad_rows.reshape(-1, width)
    head_grad = contract_rows(
        grad_logits, (rows_all.astype(FLOAT) * weight[:, None]).astype(BFLOAT)
    ).astype(BFLOAT)
    if copies == 2:
        head_grad = head_grad.astype(FLOAT) + swap(head_grad, lines["x"]).astype(FLOAT)
    else:
        head_grad = lax.psum(head_grad, "rep").astype(FLOAT)
    grad_top = sum(contract_rows(pick, part) for part in two_parts(grad_rows))

    layer_grads, grad_embedded = layer_backward(
        weights, features_low, lengths, kept, grad_top, lines
    )
    mats_grad, up_grad, down_grad, vectors_sum, bias_sum = layer_grads
    vectors_sum, bias_sum = paired(
        paired((vectors_sum, bias_sum), "fsdp", add_trees), "rep", add_trees
    )
    vectors_grad = lax.dynamic_slice_in_dim(
        vectors_sum, group * vectors.shape[1], vectors.shape[1], 1
    )
    bias_grad = lax.dynamic_slice_in_dim(bias_sum, group * up_bias.shape[0], up_bias.shape[0], 0)

    embedded_parts = two_parts(grad_embedded)

    def give(spots):
        spread = one_hot(spots, groups * capacity)
        rows = sum(contract_rows(spread, part) for part in embedded_parts).astype(BFLOAT)
        rows = lax.all_to_all(rows.reshape(groups, capacity, width), "fsdp", 0, 0, tiled=True)
        return gather_line(rows.reshape(1, groups * capacity, width), lines["x"], 0)

    def spread_rows(wanted, rows):
        return contract_rows(
            one_hot(wanted.reshape(-1), shard_rows), rows.reshape(-1, width)
        )

    table_grad = head_grad + spread_rows(asked, give(places))

    def another(state):
        turn, total = state
        spots, wanted = ask(turn)
        wanted = gather_line(wanted[None], lines["x"], 0)
        return turn + 1, total + spread_rows(wanted, give(spots))

    table_grad = lax.while_loop(lambda state: state[0] < turns, another, (jnp.int32(1), table_grad))[1]

    items = (
        (table_grad[None], table[None], table_rows[None], table_cols[None]),
        (mats_grad, mats, mats_rows, mats_cols),
        (up_grad[None], up[None], up_rows[None], up_cols[None]),
        (down_grad[None], down[None], down_rows[None], down_cols[None]),
    )
    row_squares = [jnp.sum(item[0] * item[0], axis=2) for item in items]
    col_squares = [jnp.sum(item[0] * item[0], axis=1) for item in items]
    sums = jnp.concatenate(
        [value.reshape(-1) for value in col_squares]
        + [jnp.sum(item[2], axis=1) for item in items]
        + [jnp.stack([jnp.sum(vectors_grad * vectors_grad), jnp.sum(bias_grad * bias_grad)])]
    )
    length = sums.shape[0]
    padded = -(-length // (8 * LANES)) * 8 * LANES
    sums = jnp.pad(sums, (0, padded - length)).reshape(-1, LANES)
    sums = paired(sums, "fsdp", jnp.add).reshape(-1)[:length]
    col_totals, row_totals, offset = [], [], 0
    for value in col_squares:
        col_totals.append(sums[offset : offset + value.size].reshape(value.shape))
        offset += value.size
    for value in col_squares:
        row_totals.append(sums[offset : offset + value.shape[0]])
        offset += value.shape[0]
    square_totals = [jnp.sum(value, axis=1) for value in col_totals]
    grad_norm = jnp.sqrt(sum(jnp.sum(value) for value in square_totals) + jnp.sum(sums[offset:]))
    clip = jnp.minimum(1.0, CLIP_NORM / grad_norm)
    results = []
    for item, row_square, col_total, row_total, square_total in zip(
        items, row_squares, col_totals, row_totals, square_totals
    ):
        grad, param, rows_old, cols_old = item
        rows_count, cols_count = grad.shape[1] * groups, grad.shape[2]

        def renewed(old, square):
            return DECAY * old + (1.0 - DECAY) * (square + TINY_TERM)

        square = clip * clip
        rows_new = renewed(rows_old, square * row_square / cols_count)
        cols_new = renewed(cols_old, square * col_total / rows_count)
        mean = renewed(row_total / rows_count, square * square_total / (rows_count * cols_count))
        clipped = grad * clip
        second = rows_new[:, :, None] * cols_new[:, None, :] / mean[:, None, None]
        results.append((clipped, rows_new, cols_new, param - LEARN_RATE * clipped * lax.rsqrt(second)))
    clipped_vectors = vectors_grad * clip
    vectors_second_new = DECAY * vectors_second + (1.0 - DECAY) * (
        clipped_vectors * clipped_vectors + TINY_TERM
    )
    vectors_new = vectors - VECTOR_RATE * clipped_vectors * lax.rsqrt(vectors_second_new)
    clipped_bias = bias_grad * clip
    bias_second_new = DECAY * up_bias_second + (1.0 - DECAY) * (
        clipped_bias * clipped_bias + TINY_TERM
    )
    bias_new = up_bias - VECTOR_RATE * clipped_bias * lax.rsqrt(bias_second_new)
    table_out, mats_out, up_out, down_out = results
    return (
        table_out[0][0],
        table_out[1][0],
        table_out[2][0],
        table_out[3][0],
        mats_out[0],
        mats_out[1],
        mats_out[2],
        mats_out[3],
        up_out[0][0],
        up_out[1][0],
        up_out[2][0],
        up_out[3][0],
        down_out[0][0],
        down_out[1][0],
        down_out[2][0],
        down_out[3][0],
        clipped_vectors,
        vectors_second_new,
        vectors_new,
        clipped_bias,
        bias_second_new,
        bias_new,
        grad_norm,
        loss_parts,
    )


def solution(mesh):
    return jax.shard_map(
        body,
        mesh=mesh,
        in_specs=(
            P(("fsdp", "rep")),
            P(None, ("fsdp", "rep")),
            P(("fsdp", "rep")),
            P(("fsdp", "rep"), None),
            P(("fsdp", "rep"), None),
            P("fsdp", None),
            P(None, "fsdp", None),
            P("fsdp", None),
            P("fsdp", None),
            P(None, "fsdp"),
            P("fsdp"),
            P("fsdp"),
            P(),
            P(None, "fsdp"),
            P(),
            P("fsdp"),
            P(),
            P("fsdp"),
            P(),
            P(None, "fsdp"),
            P("fsdp"),
        ),
        out_specs=(
            P("fsdp", None),
            P("fsdp"),
            P(),
            P("fsdp", None),
            P(None, "fsdp", None),
            P(None, "fsdp"),
            P(),
            P(None, "fsdp", None),
            P("fsdp", None),
            P("fsdp"),
            P(),
            P("fsdp", None),
            P("fsdp", None),
            P("fsdp"),
            P(),
            P("fsdp", None),
            P(None, "fsdp"),
            P(None, "fsdp"),
            P(None, "fsdp"),
            P("fsdp"),
            P("fsdp"),
            P("fsdp"),
            P(),
            P(),
        ),
        check_vma=False,
    )
```

```python
import math
from typing import NamedTuple

import jax
import jax.numpy as jnp
from jax import lax
from jax.experimental import pallas as pl
from jax.experimental.pallas import tpu as pltpu
from jax.sharding import PartitionSpec as P

HEAD_DIM = 64
PAGE_LEN = 512
M_TOK = 64
M_AREA = 64
STEP = 10


EPSILON = 1e-05
CLIP_NORM = 0.1
LEARN_RATE = 0.02
VECTOR_RATE = 0.3
TINY_TERM = 1e-30
NEGATIVE = -1e30
BFLOAT = jnp.bfloat16
FLOAT = jnp.float32
LANES = 128
DECAY = 1.0 - STEP ** (-0.8)


class Line(NamedTuple):
    axis: str
    total: int
    stride: int
    count: int


def lines_of(groups, copies):
    cores = min(2, groups)
    rest = (groups // cores).bit_length() - 1
    y_count = 1 << (rest // 2)
    z_count = groups // (cores * y_count)
    return {
        "z": Line("fsdp", groups, cores * y_count, z_count),
        "y": Line("fsdp", groups, cores, y_count),
        "core": Line("fsdp", groups, 1, cores),
        "x": Line("rep", copies, 1, copies),
    }


def place_on(line):
    return lax.axis_index(line.axis) // line.stride % line.count


def shifted(value, line, step):
    pairs = []
    for i in range(line.total):
        place = i // line.stride % line.count
        pairs.append((i, i + ((place + step) % line.count - place) * line.stride))
    return lax.ppermute(value, line.axis, pairs)


def gather_line(value, line, axis):
    count = line.count
    if count == 1:
        return value
    here = place_on(line)
    pieces = [value] + [shifted(value, line, step) for step in range(1, count)]
    blocks = []
    for place in range(count):
        blocks.append(lax.select_n(here, *[pieces[(i - place) % count] for i in range(count)]))
    return jnp.concatenate(blocks, axis=axis)


def sends(value, line, axis):
    size = value.shape[axis] // line.count
    here = place_on(line)

    def block(place):
        return lax.dynamic_slice_in_dim(value, place * size, size, axis)

    return block(here), [
        block((here + step) % line.count).astype(BFLOAT) for step in range(1, line.count)
    ]


def received(own, blocks, line):
    total = own.astype(FLOAT)
    for step, value in enumerate(blocks, 1):
        total = total + shifted(value, line, step).astype(FLOAT)
    return total


def reduce_line(value, line, axis):
    return received(*sends(value, line, axis), line)


def after(value, *others):
    return lax.optimization_barrier((value, *others))[0]


def paired(value, axis, combine):
    size = lax.axis_size(axis)
    bit = 1
    while bit < size:
        pairs = [(i, i ^ bit) for i in range(size)]
        value = combine(value, jax.tree.map(lambda v: lax.ppermute(v, axis, pairs), value))
        bit *= 2
    return value


def by_owner(value, lines):
    count, _, columns = value.shape
    return value.reshape(count, lines["z"].count, lines["y"].count, lines["core"].count, -1, columns)


AXES = {"z": 1, "y": 2, "core": 3, "x": 5}


def part_sends(value, lines, name):
    return sends(value, lines[name], AXES[name])


def part_received(pair, lines, name):
    return received(*pair, lines[name]).astype(BFLOAT)


def both_copies(value, lines):
    if lines["x"].count == 2:
        return value.astype(FLOAT) + shifted(value, lines["x"], 1).astype(FLOAT)
    return lax.psum(value, "rep").astype(FLOAT)


def from_other_copies(value, lines):
    if lines["x"].count == 2:
        return shifted(value, lines["x"], 1)
    return (lax.psum(value, "rep").astype(FLOAT) - value.astype(FLOAT)).astype(BFLOAT)


def layer_norm(value, gain, shift):
    center = value - jnp.mean(value, axis=-1, keepdims=True)
    spread = jnp.mean(center * center, axis=-1, keepdims=True)
    return center * lax.rsqrt(spread + EPSILON) * gain + shift


def box_features(boxes, width):
    count = width // 8
    freqs = jnp.exp(-math.log(10000.0) * jnp.arange(count, dtype=FLOAT) / count)
    angle = boxes.astype(FLOAT)[:, :, None] * freqs[None, None, :]
    waves = jnp.concatenate([jnp.sin(angle), jnp.cos(angle)], axis=2)
    return jnp.transpose(waves, (1, 0, 2)).reshape(boxes.shape[1], width)


def valid_slots(lengths, slot_count):
    n_tok = jnp.minimum(M_TOK, 1 + lengths * M_TOK // PAGE_LEN)
    n_area = jnp.minimum(M_AREA, 1 + lengths * (3 * M_AREA) // (4 * PAGE_LEN))
    index = jnp.arange(slot_count, dtype=jnp.int32)[None, :]
    return jnp.where(index < M_TOK, index < n_tok[:, None], index - M_TOK < n_area[:, None])


def product(left, right):
    return jnp.dot(left, right, preferred_element_type=FLOAT)


def contract_rows(left, right):
    return lax.dot_general(left, right, (((0,), (0,)), ((), ())), preferred_element_type=FLOAT)


def times_transposed(left, right):
    return lax.dot_general(left, right, (((1,), (1,)), ((), ())), preferred_element_type=FLOAT)


def two_parts(value):
    high = value.astype(BFLOAT)
    return high, (value - high.astype(FLOAT)).astype(BFLOAT)


def side(index):
    lane = lax.broadcasted_iota(jnp.int32, (1, LANES), 1)
    return lane // HEAD_DIM == index


def only(mask, value):
    return jnp.where(mask, value, jnp.zeros_like(value))


def attend_kernel(length_ref, query_ref, key_ref, value_ref, box_query_ref, box_key_ref, out_ref):
    length = length_ref[pl.program_id(0)]
    query, key, box_query, box_key = query_ref[...], key_ref[...], box_query_ref[...], box_key_ref[...]
    keys = jnp.concatenate([key, box_key, key], axis=1)
    keep = lax.broadcasted_iota(jnp.int32, (1, key.shape[0]), 1) < length
    mixed = jnp.zeros(out_ref.shape, FLOAT)
    for head in range(LANES // HEAD_DIM):
        mask = side(head)
        own = only(mask, query)
        score = times_transposed(jnp.concatenate([own, own, only(mask, box_query)], axis=1), keys)
        score = jnp.where(keep, score * HEAD_DIM ** (-0.5), NEGATIVE)
        expo = jnp.exp(score - jnp.max(score, axis=1, keepdims=True))
        prob = (expo * (1.0 / jnp.sum(expo, axis=1, keepdims=True))).astype(BFLOAT)
        mixed = jnp.where(mask, product(prob, value_ref[...]), mixed)
    out_ref[...] = mixed.astype(BFLOAT)


def attend_back_kernel(
    length_ref,
    query_ref,
    key_ref,
    value_ref,
    box_query_ref,
    box_key_ref,
    grad_ref,
    grad_query_ref,
    grad_key_ref,
    grad_value_ref,
    grad_box_query_ref,
    grad_box_key_ref,
):
    length = length_ref[pl.program_id(0)]
    query, key, value, box_query, box_key = (
        query_ref[...],
        key_ref[...],
        value_ref[...],
        box_query_ref[...],
        box_key_ref[...],
    )
    grad = grad_ref[...]
    rows = key.shape[0]
    keys = jnp.concatenate([key, box_key, key], axis=1)
    both_queries = jnp.concatenate([query, box_query], axis=1)
    both_keys = jnp.concatenate([key, box_key], axis=1)
    keep = lax.broadcasted_iota(jnp.int32, (rows, 1), 0) < length
    outs = [jnp.zeros((rows, LANES), FLOAT) for _ in range(5)]
    for head in range(LANES // HEAD_DIM):
        mask = side(head)
        own = only(mask, query)
        score = times_transposed(keys, jnp.concatenate([own, own, only(mask, box_query)], axis=1))
        score = jnp.where(keep, score * HEAD_DIM ** (-0.5), NEGATIVE)
        expo = jnp.exp(score - jnp.max(score, axis=0, keepdims=True))
        prob = expo * (1.0 / jnp.sum(expo, axis=0, keepdims=True))
        grad_value = product(prob.astype(BFLOAT), grad)
        grad_prob = times_transposed(only(mask, value), grad)
        grad_score = prob * (grad_prob - jnp.sum(prob * grad_prob, axis=0, keepdims=True))
        low = grad_score.astype(BFLOAT) * jnp.asarray(HEAD_DIM ** (-0.5), BFLOAT)
        with_queries = product(low, both_queries)
        with_keys = contract_rows(low, both_keys)
        fresh = (
            with_keys[:, :LANES] + with_keys[:, LANES:],
            with_queries[:, :LANES] + with_queries[:, LANES:],
            grad_value,
            with_keys[:, :LANES],
            with_queries[:, :LANES],
        )
        outs = [jnp.where(mask, new, old) for new, old in zip(fresh, outs)]
    for ref, out in zip(
        (grad_query_ref, grad_key_ref, grad_value_ref, grad_box_query_ref, grad_box_key_ref), outs
    ):
        ref[...] = out.astype(BFLOAT)


def attention_call(kernel, lengths, arrays, out_count):
    tokens, width = arrays[0].shape
    pages = lengths.shape[0]
    spec = pl.BlockSpec((tokens // pages, LANES), lambda page, pair: (page, pair))
    out = jax.ShapeDtypeStruct((tokens, width), BFLOAT)
    return pl.pallas_call(
        kernel,
        grid=(pages, width // LANES),
        in_specs=[pl.BlockSpec(memory_space=pltpu.SMEM)] + [spec] * len(arrays),
        out_specs=[spec] * out_count,
        out_shape=[out] * out_count,
        compiler_params=pltpu.CompilerParams(vmem_limit_bytes=48 * 1024 * 1024),
    )(lengths, *arrays)


class Buckets(NamedTuple):
    owner: jax.Array
    row: jax.Array
    first: jax.Array
    rank: jax.Array
    fullest: jax.Array


def bucket_ids(ids, shard_rows):
    owner, row = ids // shard_rows, ids % shard_rows
    index = jnp.arange(ids.shape[0], dtype=jnp.int32)
    earlier = index[None, :] < index[:, None]
    same = ids[:, None] == ids[None, :]
    first = ~jnp.any(same & earlier, axis=1)
    before = (owner[:, None] == owner[None, :]) & earlier & first[None, :]
    rank = jnp.sum(before.astype(jnp.int32), axis=1)
    rank = jnp.sum(jnp.where(same & first[None, :], rank[None, :], 0), axis=1)
    return Buckets(owner, row, first, rank, jnp.max(rank) + 1)


def bucket_places(buckets, capacity, turn):
    shifted = buckets.rank - turn * capacity
    inside = (shifted >= 0) & (shifted < capacity)
    return jnp.where(inside, buckets.owner * capacity + shifted, -1)


def bucket_requests(buckets, places, groups, capacity):
    hit = (places[:, None] == jnp.arange(groups * capacity)[None, :]) & buckets.first[:, None]
    return jnp.sum(jnp.where(hit, buckets.row[:, None], 0), axis=0).reshape(groups, capacity)


def one_hot(index, count):
    return (index[:, None] == jnp.arange(count, dtype=jnp.int32)[None, :]).astype(BFLOAT)


def feed_kernel(middle_ref, up_ref, bias_ref, down_ref, active_ref, slope_ref, out_ref):
    value = product(middle_ref[...], up_ref[...]) + bias_ref[...]
    share = 0.5 * (1.0 + lax.erf(value * math.sqrt(0.5)))
    density = jnp.exp(-0.5 * value * value) * (1.0 / math.sqrt(2.0 * math.pi))
    active = (value * share).astype(BFLOAT)
    active_ref[...] = active
    slope_ref[...] = share + value * density
    out = product(active, down_ref[...])

    @pl.when(pl.program_id(0) == 0)
    def _():
        out_ref[...] = out

    @pl.when(pl.program_id(0) > 0)
    def _():
        out_ref[...] += out


def feed_forward(middle_low, packed, bias, down):
    tokens, width = middle_low.shape
    hidden = down.shape[0]
    whole = pl.BlockSpec((tokens, width), lambda j: (0, 0))
    columns = pl.BlockSpec((tokens, width), lambda j: (0, j))
    return pl.pallas_call(
        feed_kernel,
        grid=(hidden // width,),
        in_specs=[
            whole,
            pl.BlockSpec((None, width, width), lambda j: (j, 0, 0)),
            pl.BlockSpec((1, width), lambda j: (0, j)),
            pl.BlockSpec((width, width), lambda j: (j, 0)),
        ],
        out_specs=[columns, columns, whole],
        out_shape=[
            jax.ShapeDtypeStruct((tokens, hidden), BFLOAT),
            jax.ShapeDtypeStruct((tokens, hidden), FLOAT),
            jax.ShapeDtypeStruct((tokens, width), FLOAT),
        ],
        compiler_params=pltpu.CompilerParams(vmem_limit_bytes=48 * 1024 * 1024),
    )(middle_low, packed, bias[None], down)


def feed_back_kernel(
    grad_ref,
    middle_ref,
    active_ref,
    slope_ref,
    up_ref,
    down_ref,
    grad_up_ref,
    grad_down_ref,
    grad_bias_ref,
    out_ref,
):
    grad = grad_ref[...]
    grad_upper = (times_transposed(grad, down_ref[...]) * slope_ref[...]).astype(BFLOAT)
    grad_bias_ref[...] = jnp.sum(grad_upper.astype(FLOAT), axis=0, keepdims=True)
    grad_down_ref[...] = contract_rows(active_ref[...], grad).astype(BFLOAT)
    grad_up_ref[...] = contract_rows(middle_ref[...], grad_upper).astype(BFLOAT)
    out = times_transposed(grad_upper, up_ref[...])

    @pl.when(pl.program_id(0) == 0)
    def _():
        out_ref[...] = out

    @pl.when(pl.program_id(0) > 0)
    def _():
        out_ref[...] += out


def feed_backward(grad_feed, middle_low, active, slope, packed, down):
    tokens, width = middle_low.shape
    hidden = down.shape[0]
    whole = pl.BlockSpec((tokens, width), lambda j: (0, 0))
    columns = pl.BlockSpec((tokens, width), lambda j: (0, j))
    return pl.pallas_call(
        feed_back_kernel,
        grid=(hidden // width,),
        in_specs=[
            whole,
            whole,
            columns,
            columns,
            pl.BlockSpec((None, width, width), lambda j: (j, 0, 0)),
            pl.BlockSpec((width, width), lambda j: (j, 0)),
        ],
        out_specs=[
            pl.BlockSpec((width, width), lambda j: (0, j)),
            pl.BlockSpec((width, width), lambda j: (j, 0)),
            pl.BlockSpec((1, width), lambda j: (0, j)),
            whole,
        ],
        out_shape=[
            jax.ShapeDtypeStruct((width, hidden), BFLOAT),
            jax.ShapeDtypeStruct((hidden, width), BFLOAT),
            jax.ShapeDtypeStruct((1, hidden), FLOAT),
            jax.ShapeDtypeStruct((tokens, width), FLOAT),
        ],
        compiler_params=pltpu.CompilerParams(vmem_limit_bytes=48 * 1024 * 1024),
    )(grad_feed, middle_low, active, slope, packed, down)


def logits_kernel(rows_ref, table_ref, label_ref, expo_ref, stats_ref):
    logits = times_transposed(rows_ref[...], table_ref[...])
    peak = jnp.max(logits, axis=1, keepdims=True)
    expo = jnp.exp(logits - peak)
    expo_ref[...] = expo.astype(BFLOAT)
    mass = jnp.sum(expo, axis=1, keepdims=True)
    column = lax.broadcasted_iota(jnp.int32, logits.shape, 1)
    target = jnp.sum(jnp.where(column == label_ref[...], logits, 0.0), axis=1, keepdims=True)
    lane = lax.broadcasted_iota(jnp.int32, (logits.shape[0], LANES), 1)
    stats = jnp.where(lane == 0, peak, jnp.where(lane == 1, mass, target))
    stats_ref[...] = stats.T[:8]


def head_logits(rows_all, table_low, own_labels):
    count, width = rows_all.shape
    shard_rows = table_low.shape[0]
    step = 256
    return pl.pallas_call(
        logits_kernel,
        grid=(count // step,),
        in_specs=[
            pl.BlockSpec((step, width), lambda i: (i, 0)),
            pl.BlockSpec((shard_rows, width), lambda i: (0, 0)),
            pl.BlockSpec((step, 1), lambda i: (i, 0)),
        ],
        out_specs=[
            pl.BlockSpec((step, shard_rows), lambda i: (i, 0)),
            pl.BlockSpec((8, step), lambda i: (0, i)),
        ],
        out_shape=[
            jax.ShapeDtypeStruct((count, shard_rows), BFLOAT),
            jax.ShapeDtypeStruct((8, count), FLOAT),
        ],
        compiler_params=pltpu.CompilerParams(vmem_limit_bytes=48 * 1024 * 1024),
    )(rows_all, table_low, own_labels[:, None])


def column_sum(value):
    return jnp.sum(value.astype(FLOAT), axis=0)


def layer_forward(weights, embedded, place, box_query, box_key, lengths):
    mats, packed, down, gains, up_bias = weights
    start_state = layer_norm(embedded, gains[0], gains[1])
    act = start_state.astype(BFLOAT)
    query = (product(act, mats[1]) + gains[6]).astype(BFLOAT)
    keys = product(act, mats[2]).astype(BFLOAT)
    values = (product(act, mats[3]) + gains[7]).astype(BFLOAT)
    (mixed,) = attention_call(attend_kernel, lengths, (query, keys, values, box_query, box_key), 1)
    first_sum = start_state + (product(mixed, mats[6]) + gains[8])
    middle = layer_norm(first_sum, gains[2], gains[3])
    middle_low = middle.astype(BFLOAT)
    active, slope, feed = feed_forward(middle_low, packed, up_bias, down)
    second_sum = middle + (feed + gains[10])
    kept = (
        embedded,
        act,
        place,
        query,
        keys,
        values,
        box_query,
        box_key,
        mixed,
        first_sum,
        middle_low,
        slope,
        active,
        second_sum,
    )
    return (layer_norm(second_sum, gains[4], gains[5]), kept)


def layer_backward(weights, features_low, lengths, kept, grad_out, head_parts, lines, tools):
    mats, packed, down, gains, up_bias = weights
    (
        embedded,
        act,
        place,
        query,
        keys,
        values,
        box_query,
        box_key,
        mixed,
        first_sum,
        middle_low,
        slope,
        active,
        second_sum,
    ) = kept
    compacted, give, over_copies = tools

    def send(value, name):
        own, blocks = sends(value, lines[name], AXES[name])
        return own, blocks

    def travel(pair, name, until=None):
        line = lines[name]
        moved = [shifted(block, line, step) for step, block in enumerate(pair[1], 1)]
        if until is not None:
            moved = list(after(tuple(moved), until))
        total = pair[0].astype(FLOAT)
        for value in moved:
            total = total + value.astype(FLOAT)
        return total.astype(BFLOAT)

    grad_second, gain_four, gain_five = jax.vjp(layer_norm, second_sum, gains[4], gains[5])[1](
        grad_out
    )
    grad_feed = grad_second.astype(BFLOAT)
    grad_up, grad_down, grad_bias, fed_back = feed_backward(
        grad_feed, middle_low, active, slope, packed, down
    )
    down_core = send(by_owner(grad_down[None], lines), "core")
    up_core = send(by_owner(grad_up[None], lines), "core")
    fed_back = after(fed_back, *down_core[1], *up_core[1], head_parts[1])
    grad_first, gain_two, gain_three = jax.vjp(layer_norm, first_sum, gains[2], gains[3])[1](
        grad_second + fed_back
    )
    grad_attended = grad_first.astype(BFLOAT)
    down_y = send(travel(down_core, "core", grad_attended), "y")
    grad_attended = after(grad_attended, *down_y[1])
    grad_mixed = times_transposed(grad_attended, mats[6]).astype(BFLOAT)
    up_x = send(travel(up_core, "core", grad_mixed), "x")
    grad_mixed = after(grad_mixed, *up_x[1])
    pieces = attention_call(
        attend_back_kernel, lengths, (query, keys, values, box_query, box_key, grad_mixed), 5
    )
    down_z = send(travel(down_y, "y", pieces[0]), "z")
    pieces = after(tuple(pieces), *down_z[1], *head_parts[2:])
    grad_query, grad_keys, grad_values, grad_box_query, grad_box_key = pieces
    grad_start = (
        grad_first + times_transposed(grad_query, mats[1]) + times_transposed(grad_keys, mats[2])
    )
    grad_start = grad_start + times_transposed(grad_values, mats[3])
    grad_embedded, gain_zero, gain_one = jax.vjp(layer_norm, embedded, gains[0], gains[1])[1](
        grad_start
    )
    parts = two_parts(grad_embedded)
    compact = compacted(parts)
    returned = give(compact)
    pieces = after(tuple(pieces), compact)
    grad_query, grad_keys, grad_values, grad_box_query, grad_box_key = pieces
    token_part = jnp.stack(
        [
            contract_rows(act, grad_query),
            contract_rows(act, grad_keys),
            contract_rows(act, grad_values),
            contract_rows(mixed, grad_attended),
        ]
    ).astype(BFLOAT)
    token_core = send(by_owner(token_part, lines), "core")
    grad_box_query = after(grad_box_query, *token_core[1])
    grad_place = (
        times_transposed(grad_box_query, mats[4]) + times_transposed(grad_box_key, mats[5])
    ).astype(BFLOAT)
    token_y = send(travel(token_core, "core", grad_place), "y")
    features_low, grad_place = after((features_low, grad_place), *token_y[1])
    box_part = jnp.stack(
        [
            contract_rows(features_low, grad_place),
            contract_rows(place, grad_box_query),
            contract_rows(place, grad_box_key),
        ]
    ).astype(BFLOAT)
    box_core = send(by_owner(box_part, lines), "core")
    up_y = send(travel(up_x, "x", box_core[1][0]), "y")
    box_x = send(travel(box_core, "core", up_y[1][0]), "x")
    down_sum = travel(down_z, "z", box_x[1][0])[:, 0, 0, 0]
    grad_vectors = jnp.stack(
        [
            gain_zero,
            gain_one,
            gain_two,
            gain_three,
            gain_four,
            gain_five,
            column_sum(grad_query),
            column_sum(grad_values),
            column_sum(grad_attended),
            column_sum(grad_place),
            column_sum(grad_feed),
        ]
    )
    small = jnp.concatenate([grad_vectors.reshape(-1), grad_bias[0]])
    returned = after(returned, down_sum, small)
    lookup_rows = over_copies(returned)
    small = after(small, returned)
    token_x = send(travel(token_y, "y", returned), "x")
    up_z = send(travel(up_y, "y", token_x[1][0]), "z")
    box_y = send(travel(box_x, "x", token_x[1][0]), "y")
    token_z = send(travel(token_x, "x", box_y[1][0]), "z")
    box_z = send(travel(box_y, "y", token_z[1][0]), "z")
    grad_down = both_copies(down_sum, lines)
    up_half = travel(up_z, "z", box_y[1][0])[:, 0, 0, 0]
    token_half = travel(token_z, "z", box_z[1][0])[:, 0, 0, 0]
    box_half = travel(box_z, "z")[:, 0, 0, 0]
    grad_up = gather_line(up_half, lines["x"], 2)
    token_mats = gather_line(token_half, lines["x"], 2)
    box_mats = gather_line(box_half, lines["x"], 2)
    grad_mats = jnp.concatenate([box_mats[:1], token_mats[:3], box_mats[1:], token_mats[3:]])
    layer_grads = (grad_mats.astype(FLOAT), grad_up[0].astype(FLOAT), grad_down[0], small)
    return (layer_grads, lookup_rows, parts)


def combine_mass(first, second):
    peak = jnp.maximum(first[0], second[0])
    mass = first[1] * jnp.exp(first[0] - peak) + second[1] * jnp.exp(second[0] - peak)
    return jnp.stack([peak, mass, first[2] + second[2]])


def body(
    token_ids,
    boxes,
    lengths,
    slots,
    labels,
    table,
    mats,
    up,
    down,
    vectors,
    up_bias,
    table_rows,
    table_cols,
    mats_rows,
    mats_cols,
    up_rows,
    up_cols,
    down_rows,
    down_cols,
    vectors_second,
    up_bias_second,
):
    pages = lengths.shape[0]
    tokens = token_ids.shape[0]
    page_len = tokens // pages
    width = table.shape[1]
    shard_rows = table.shape[0]
    slot_count = slots.shape[1]
    groups, copies = lax.axis_size("fsdp"), lax.axis_size("rep")
    group, copy = lax.axis_index("fsdp"), lax.axis_index("rep")
    lines = lines_of(groups, copies)
    table_low = table.astype(BFLOAT)

    capacity = 16 + -(-tokens // (16 * groups)) * 16
    buckets = bucket_ids(token_ids, shard_rows)
    places = bucket_places(buckets, capacity, 0)
    requests = bucket_requests(buckets, places, groups, capacity)
    own_news = jnp.concatenate([labels.reshape(-1), lengths, buckets.fullest[None]])
    news = jnp.concatenate(
        [
            jnp.repeat(requests, copies, axis=0),
            jnp.broadcast_to(own_news[None], (groups * copies, own_news.shape[0])),
        ],
        axis=1,
    )
    news = lax.all_to_all(news, ("fsdp", "rep"), 0, 0, tiled=True)
    asked = news[:, :capacity].reshape(groups, copies, capacity)
    asked = jnp.transpose(asked, (1, 0, 2)).reshape(copies, groups * capacity)
    labels_all = news[:, capacity : capacity + pages * slot_count]
    labels_all = labels_all.reshape(groups, copies, pages * slot_count)
    labels_all = lax.dynamic_index_in_dim(labels_all, copy, 1, False).reshape(-1)
    lengths_all = news[:, capacity + pages * slot_count : -1]
    turns = (jnp.max(news[:, -1]) + capacity - 1) // capacity

    def fetch(spots, wanted):
        rows = product(one_hot(wanted, shard_rows), table_low).astype(BFLOAT)
        rows = lax.all_to_all(rows.reshape(groups, capacity, width), "fsdp", 0, 0, tiled=True)
        return product(one_hot(spots, groups * capacity), rows.reshape(groups * capacity, width))

    def ask(turn):
        spots = bucket_places(buckets, capacity, turn)
        wanted = bucket_requests(buckets, spots, groups, capacity)
        return spots, lax.all_to_all(wanted, "fsdp", 0, 0, tiled=True).reshape(-1)

    embedded = fetch(places, lax.dynamic_index_in_dim(asked, copy, 0, False))
    embedded = lax.while_loop(
        lambda state: state[0] < turns,
        lambda state: (state[0] + 1, state[1] + fetch(*ask(state[0]))),
        (jnp.int32(1), embedded),
    )[1]

    own_labels = labels_all - group * shard_rows
    label_rows = product(one_hot(own_labels, shard_rows), table_low)
    embedded = after(embedded, label_rows)

    small = jnp.concatenate([vectors.astype(BFLOAT).reshape(-1), up_bias.astype(BFLOAT)])[None]

    def lay(first, second, bit):
        low = (group & bit) == 0
        return jnp.concatenate([jnp.where(low, first, second), jnp.where(low, second, first)])

    bit = 1
    while bit < groups:
        pairs = [(i, i ^ bit) for i in range(groups)]
        small = lay(small, lax.ppermute(small, "fsdp", pairs), bit)
        bit *= 2
    split = vectors.size
    gains = small[:, :split].reshape(groups, vectors.shape[0], -1)
    gains = jnp.transpose(gains, (1, 0, 2)).reshape(vectors.shape[0], width).astype(FLOAT)
    bias = small[:, split:].reshape(-1).astype(FLOAT)
    gains, bias = lax.optimization_barrier((gains, bias))
    rows, hidden = up.shape
    blocks = hidden // width
    up_blocks = jnp.transpose(up.astype(BFLOAT).reshape(rows, blocks, width), (1, 0, 2))
    down_blocks = down.astype(BFLOAT).reshape(blocks, rows, width)
    packed = jnp.concatenate([up_blocks, down_blocks, mats.astype(BFLOAT)])
    packed = lax.all_gather(packed, "fsdp", axis=1, tiled=True)
    layer_mats = packed[2 * blocks :]
    down_low = packed[blocks : 2 * blocks].reshape(blocks, groups, rows, width)
    down_low = jnp.transpose(down_low, (1, 0, 2, 3)).reshape(hidden, width)
    weights = (layer_mats, packed, down_low, gains, bias)

    features_low = box_features(boxes, width).astype(BFLOAT)
    place = (product(features_low, layer_mats[0]) + gains[9]).astype(BFLOAT)
    box_query = product(place, layer_mats[4]).astype(BFLOAT)
    box_key = product(place, layer_mats[5]).astype(BFLOAT)
    top_state, kept = layer_forward(weights, embedded, place, box_query, box_key, lengths)

    where_at = slots * lengths[:, None] // 256 + jnp.arange(pages)[:, None] * page_len
    pick = one_hot(where_at.reshape(-1), tokens)
    rows_low = product(pick, top_state.astype(BFLOAT)).astype(BFLOAT)
    rows_all = rows_low[None, None, None]
    for axis, name in enumerate(("z", "y", "core")):
        rows_all = gather_line(rows_all, lines[name], axis)
    rows_all = rows_all.reshape(-1, width)
    expo, stats = head_logits(rows_all, table_low, own_labels)
    peak_here = stats[0]
    products = product(expo, table_low)
    stats = paired(stats[:3].reshape(3, -1, LANES), "fsdp", combine_mass).reshape(3, -1)
    peak, mass, target = stats
    log_total = peak + jnp.log(mass)
    factor = jnp.exp(peak_here - log_total)

    is_token = jnp.arange(slot_count) < M_TOK
    valid_all = valid_slots(lengths_all.reshape(-1), slot_count).astype(FLOAT)
    count_token = jnp.sum(jnp.where(is_token, valid_all, 0.0))
    count_area = jnp.sum(jnp.where(is_token, 0.0, valid_all))
    valid = valid_all.reshape(groups, copies, pages, slot_count)
    valid = lax.dynamic_index_in_dim(valid, copy, 1, False).reshape(-1, slot_count)
    loss_rows = (log_total - target).reshape(-1, slot_count) * valid
    sums = jnp.stack(
        [jnp.sum(jnp.where(is_token, loss_rows, 0.0)), jnp.sum(jnp.where(is_token, 0.0, loss_rows))]
    )
    sums = paired(sums, "rep", jnp.add)
    loss_parts = jnp.stack([sums[0], count_token, sums[1], count_area])
    share = jnp.where(is_token, 1.0 / count_token, 1.0 / count_area)
    weight = (valid * share[None, :]).reshape(-1)
    grad_rows = (products * factor[:, None] - label_rows) * weight[:, None]
    grad_rows = grad_rows.reshape(
        lines["z"].count, lines["y"].count, lines["core"].count, -1, width
    )
    own, blocks = sends(grad_rows, lines["core"], 2)
    weighted = (rows_all.astype(FLOAT) * weight[:, None]).astype(BFLOAT)
    expo, weighted = after((expo, weighted), *blocks)
    mine = own_labels[:, None] == jnp.arange(shard_rows)[None, :]
    grad_logits = expo.astype(FLOAT) * factor[:, None] - mine.astype(FLOAT)
    own, blocks = sends(received(own, blocks, lines["core"]), lines["y"], 1)
    grad_logits = after(grad_logits.astype(BFLOAT), *blocks)
    head_low = contract_rows(grad_logits, weighted).astype(BFLOAT)
    own, blocks = sends(received(own, blocks, lines["y"]), lines["z"], 0)
    blocks = list(after(tuple(blocks), head_low))
    grad_rows = received(own, blocks, lines["z"]).reshape(-1, width)
    head_parts = [from_other_copies(part, lines) for part in jnp.split(head_low, 4)]
    grad_rows = after(grad_rows, head_parts[0])
    grad_top = sum(contract_rows(pick, part) for part in two_parts(grad_rows))

    def compacted(spots, parts):
        spread = one_hot(spots, groups * capacity)
        return sum(contract_rows(spread, part) for part in parts).astype(BFLOAT)

    def give(rows):
        rows = lax.all_to_all(rows.reshape(groups, capacity, width), "fsdp", 0, 0, tiled=True)
        return rows.reshape(1, groups * capacity, width)

    def over_copies(rows):
        return gather_line(rows, lines["x"], 0)

    tools = (lambda parts: compacted(places, parts), give, over_copies)
    layer_grads, lookup_rows, embedded_parts = layer_backward(
        weights, features_low, lengths, kept, grad_top, head_parts, lines, tools
    )
    mats_grad, up_grad, down_grad, small_sum = layer_grads
    small_sum = paired(small_sum.reshape(-1, LANES), "fsdp", jnp.add)
    small_sum = paired(small_sum, "rep", jnp.add).reshape(-1)
    vectors_sum = small_sum[: vectors.shape[0] * width].reshape(-1, width)
    bias_sum = small_sum[vectors.shape[0] * width :]
    vectors_grad = lax.dynamic_slice_in_dim(
        vectors_sum, group * vectors.shape[1], vectors.shape[1], 1
    )
    bias_grad = lax.dynamic_slice_in_dim(bias_sum, group * up_bias.shape[0], up_bias.shape[0], 0)

    def spread_rows(wanted, rows):
        return contract_rows(
            one_hot(wanted.reshape(-1), shard_rows), rows.reshape(-1, width)
        )

    head_grad = head_low.astype(FLOAT) + jnp.concatenate(head_parts).astype(FLOAT)
    table_grad = head_grad + spread_rows(asked, lookup_rows)

    def another(state):
        turn, total = state
        spots, wanted = ask(turn)
        wanted = gather_line(wanted[None], lines["x"], 0)
        return turn + 1, total + spread_rows(
            wanted, over_copies(give(compacted(spots, embedded_parts)))
        )

    table_grad = lax.while_loop(lambda state: state[0] < turns, another, (jnp.int32(1), table_grad))[1]

    items = (
        (table_grad[None], table[None], table_rows[None], table_cols[None]),
        (mats_grad, mats, mats_rows, mats_cols),
        (up_grad[None], up[None], up_rows[None], up_cols[None]),
        (down_grad[None], down[None], down_rows[None], down_cols[None]),
    )
    row_squares = [jnp.sum(item[0] * item[0], axis=2) for item in items]
    col_squares = [jnp.sum(item[0] * item[0], axis=1) for item in items]
    sums = jnp.concatenate(
        [value.reshape(-1) for value in col_squares]
        + [jnp.sum(item[2], axis=1) for item in items]
        + [jnp.stack([jnp.sum(vectors_grad * vectors_grad), jnp.sum(bias_grad * bias_grad)])]
    )
    length = sums.shape[0]
    padded = -(-length // (8 * LANES)) * 8 * LANES
    sums = jnp.pad(sums, (0, padded - length)).reshape(-1, LANES)
    sums = paired(sums, "fsdp", jnp.add).reshape(-1)[:length]
    col_totals, row_totals, offset = [], [], 0
    for value in col_squares:
        col_totals.append(sums[offset : offset + value.size].reshape(value.shape))
        offset += value.size
    for value in col_squares:
        row_totals.append(sums[offset : offset + value.shape[0]])
        offset += value.shape[0]
    square_totals = [jnp.sum(value, axis=1) for value in col_totals]
    grad_norm = jnp.sqrt(sum(jnp.sum(value) for value in square_totals) + jnp.sum(sums[offset:]))
    clip = jnp.minimum(1.0, CLIP_NORM / grad_norm)
    results = []
    for item, row_square, col_total, row_total, square_total in zip(
        items, row_squares, col_totals, row_totals, square_totals
    ):
        grad, param, rows_old, cols_old = item
        rows_count, cols_count = grad.shape[1] * groups, grad.shape[2]

        def renewed(old, square):
            return DECAY * old + (1.0 - DECAY) * (square + TINY_TERM)

        square = clip * clip
        rows_new = renewed(rows_old, square * row_square / cols_count)
        cols_new = renewed(cols_old, square * col_total / rows_count)
        mean = renewed(row_total / rows_count, square * square_total / (rows_count * cols_count))
        clipped = grad * clip
        second = rows_new[:, :, None] * cols_new[:, None, :] / mean[:, None, None]
        results.append((clipped, rows_new, cols_new, param - LEARN_RATE * clipped * lax.rsqrt(second)))
    clipped_vectors = vectors_grad * clip
    vectors_second_new = DECAY * vectors_second + (1.0 - DECAY) * (
        clipped_vectors * clipped_vectors + TINY_TERM
    )
    vectors_new = vectors - VECTOR_RATE * clipped_vectors * lax.rsqrt(vectors_second_new)
    clipped_bias = bias_grad * clip
    bias_second_new = DECAY * up_bias_second + (1.0 - DECAY) * (
        clipped_bias * clipped_bias + TINY_TERM
    )
    bias_new = up_bias - VECTOR_RATE * clipped_bias * lax.rsqrt(bias_second_new)
    table_out, mats_out, up_out, down_out = results
    return (
        table_out[0][0],
        table_out[1][0],
        table_out[2][0],
        table_out[3][0],
        mats_out[0],
        mats_out[1],
        mats_out[2],
        mats_out[3],
        up_out[0][0],
        up_out[1][0],
        up_out[2][0],
        up_out[3][0],
        down_out[0][0],
        down_out[1][0],
        down_out[2][0],
        down_out[3][0],
        clipped_vectors,
        vectors_second_new,
        vectors_new,
        clipped_bias,
        bias_second_new,
        bias_new,
        grad_norm,
        loss_parts,
    )


def solution(mesh):
    return jax.shard_map(
        body,
        mesh=mesh,
        in_specs=(
            P(("fsdp", "rep")),
            P(None, ("fsdp", "rep")),
            P(("fsdp", "rep")),
            P(("fsdp", "rep"), None),
            P(("fsdp", "rep"), None),
            P("fsdp", None),
            P(None, "fsdp", None),
            P("fsdp", None),
            P("fsdp", None),
            P(None, "fsdp"),
            P("fsdp"),
            P("fsdp"),
            P(),
            P(None, "fsdp"),
            P(),
            P("fsdp"),
            P(),
            P("fsdp"),
            P(),
            P(None, "fsdp"),
            P("fsdp"),
        ),
        out_specs=(
            P("fsdp", None),
            P("fsdp"),
            P(),
            P("fsdp", None),
            P(None, "fsdp", None),
            P(None, "fsdp"),
            P(),
            P(None, "fsdp", None),
            P("fsdp", None),
            P("fsdp"),
            P(),
            P("fsdp", None),
            P("fsdp", None),
            P("fsdp"),
            P(),
            P("fsdp", None),
            P(None, "fsdp"),
            P(None, "fsdp"),
            P(None, "fsdp"),
            P("fsdp"),
            P("fsdp"),
            P("fsdp"),
            P(),
            P(),
        ),
        check_vma=False,
    )
```

```python
import math
from typing import NamedTuple

import jax
import jax.numpy as jnp
from jax import lax
from jax.experimental import pallas as pl
from jax.experimental.pallas import tpu as pltpu
from jax.sharding import PartitionSpec as P

HEAD_DIM = 64
PAGE_LEN = 512
M_TOK = 64
M_AREA = 64
STEP = 10


EPSILON = 1e-05
CLIP_NORM = 0.1
LEARN_RATE = 0.02
VECTOR_RATE = 0.3
TINY_TERM = 1e-30
NEGATIVE = -1e30
BFLOAT = jnp.bfloat16
FLOAT = jnp.float32
LANES = 128
DECAY = 1.0 - STEP ** (-0.8)


class Line(NamedTuple):
    axis: str
    total: int
    stride: int
    count: int


def lines_of(groups, copies):
    cores = min(2, groups)
    rest = (groups // cores).bit_length() - 1
    y_count = 1 << (rest // 2)
    z_count = groups // (cores * y_count)
    return {
        "z": Line("fsdp", groups, cores * y_count, z_count),
        "y": Line("fsdp", groups, cores, y_count),
        "core": Line("fsdp", groups, 1, cores),
        "x": Line("rep", copies, 1, copies),
    }


def place_on(line):
    return lax.axis_index(line.axis) // line.stride % line.count


def shifted(value, line, step):
    pairs = []
    for i in range(line.total):
        place = i // line.stride % line.count
        pairs.append((i, i + ((place + step) % line.count - place) * line.stride))
    return lax.ppermute(value, line.axis, pairs)


def gather_line(value, line, axis):
    count = line.count
    if count == 1:
        return value
    here = place_on(line)
    pieces = [value] + [shifted(value, line, step) for step in range(1, count)]
    blocks = []
    for place in range(count):
        blocks.append(lax.select_n(here, *[pieces[(i - place) % count] for i in range(count)]))
    return jnp.concatenate(blocks, axis=axis)


def sends(value, line, axis):
    size = value.shape[axis] // line.count
    here = place_on(line)

    def block(place):
        return lax.dynamic_slice_in_dim(value, place * size, size, axis)

    return block(here), [
        block((here + step) % line.count).astype(BFLOAT) for step in range(1, line.count)
    ]


def received(own, blocks, line):
    total = own.astype(FLOAT)
    for step, value in enumerate(blocks, 1):
        total = total + shifted(value, line, step).astype(FLOAT)
    return total


def reduce_line(value, line, axis):
    return received(*sends(value, line, axis), line)


def after(value, *others):
    return lax.optimization_barrier((value, *others))[0]


def paired(value, axis, combine, beside=None):
    size = lax.axis_size(axis)
    bit = 1
    while bit < size:
        pairs = [(i, i ^ bit) for i in range(size)]
        other = lax.ppermute(value, axis, pairs)
        if beside is not None and bit == 2:
            other = after(other, beside)
        value = combine(value, other)
        bit *= 2
    return value


def by_owner(value, lines):
    count, _, columns = value.shape
    return value.reshape(count, lines["z"].count, lines["y"].count, lines["core"].count, -1, columns)


AXES = {"z": 1, "y": 2, "core": 3, "x": 5}


def part_sends(value, lines, name):
    return sends(value, lines[name], AXES[name])


def part_received(pair, lines, name):
    return received(*pair, lines[name]).astype(BFLOAT)


def both_copies(value, lines):
    if lines["x"].count == 2:
        return value.astype(FLOAT) + shifted(value, lines["x"], 1).astype(FLOAT)
    return lax.psum(value, "rep").astype(FLOAT)


def from_other_copies(value, lines):
    if lines["x"].count == 2:
        return shifted(value, lines["x"], 1)
    return (lax.psum(value, "rep").astype(FLOAT) - value.astype(FLOAT)).astype(BFLOAT)


def layer_norm(value, gain, shift):
    center = value - jnp.mean(value, axis=-1, keepdims=True)
    spread = jnp.mean(center * center, axis=-1, keepdims=True)
    return center * lax.rsqrt(spread + EPSILON) * gain + shift


def box_features(boxes, width):
    count = width // 8
    freqs = jnp.exp(-math.log(10000.0) * jnp.arange(count, dtype=FLOAT) / count)
    angle = boxes.astype(FLOAT)[:, :, None] * freqs[None, None, :]
    waves = jnp.concatenate([jnp.sin(angle), jnp.cos(angle)], axis=2)
    return jnp.transpose(waves, (1, 0, 2)).reshape(boxes.shape[1], width)


def valid_slots(lengths, slot_count):
    n_tok = jnp.minimum(M_TOK, 1 + lengths * M_TOK // PAGE_LEN)
    n_area = jnp.minimum(M_AREA, 1 + lengths * (3 * M_AREA) // (4 * PAGE_LEN))
    index = jnp.arange(slot_count, dtype=jnp.int32)[None, :]
    return jnp.where(index < M_TOK, index < n_tok[:, None], index - M_TOK < n_area[:, None])


def product(left, right):
    return jnp.dot(left, right, preferred_element_type=FLOAT)


def contract_rows(left, right):
    return lax.dot_general(left, right, (((0,), (0,)), ((), ())), preferred_element_type=FLOAT)


def times_transposed(left, right):
    return lax.dot_general(left, right, (((1,), (1,)), ((), ())), preferred_element_type=FLOAT)


def two_parts(value):
    high = value.astype(BFLOAT)
    return high, (value - high.astype(FLOAT)).astype(BFLOAT)


def side(index):
    lane = lax.broadcasted_iota(jnp.int32, (1, LANES), 1)
    return lane // HEAD_DIM == index


def only(mask, value):
    return jnp.where(mask, value, jnp.zeros_like(value))


def attend_kernel(length_ref, query_ref, key_ref, value_ref, box_query_ref, box_key_ref, out_ref):
    length = length_ref[pl.program_id(0)]
    query, key, box_query, box_key = query_ref[...], key_ref[...], box_query_ref[...], box_key_ref[...]
    keys = jnp.concatenate([key, box_key, key], axis=1)
    keep = lax.broadcasted_iota(jnp.int32, (1, key.shape[0]), 1) < length
    scale = jnp.asarray(HEAD_DIM ** (-0.5), BFLOAT)
    mixed = jnp.zeros(out_ref.shape, FLOAT)
    for head in range(LANES // HEAD_DIM):
        mask = side(head)
        own = only(mask, query) * scale
        other = only(mask, box_query) * scale
        score = times_transposed(jnp.concatenate([own, own, other], axis=1), keys)
        score = jnp.where(keep, score, NEGATIVE)
        expo = jnp.exp(score - jnp.max(score, axis=1, keepdims=True))
        prob = (expo * (1.0 / jnp.sum(expo, axis=1, keepdims=True))).astype(BFLOAT)
        mixed = jnp.where(mask, product(prob, value_ref[...]), mixed)
    out_ref[...] = mixed.astype(BFLOAT)


def attend_back_kernel(
    length_ref, query_ref, key_ref, value_ref, box_query_ref, box_key_ref, grad_ref, out_ref
):
    length = length_ref[pl.program_id(0)]
    query, key, value, box_query, box_key = (
        query_ref[...],
        key_ref[...],
        value_ref[...],
        box_query_ref[...],
        box_key_ref[...],
    )
    grad = grad_ref[...]
    rows = key.shape[0]
    keys = jnp.concatenate([key, box_key, key], axis=1)
    both_queries = jnp.concatenate([query, box_query], axis=1)
    both_keys = jnp.concatenate([key, box_key], axis=1)
    keep = lax.broadcasted_iota(jnp.int32, (rows, 1), 0) < length
    scale = jnp.asarray(HEAD_DIM ** (-0.5), BFLOAT)
    outs = [jnp.zeros((rows, LANES), FLOAT) for _ in range(5)]
    for head in range(LANES // HEAD_DIM):
        mask = side(head)
        own = only(mask, query) * scale
        other = only(mask, box_query) * scale
        score = times_transposed(keys, jnp.concatenate([own, own, other], axis=1))
        score = jnp.where(keep, score, NEGATIVE)
        expo = jnp.exp(score - jnp.max(score, axis=0, keepdims=True))
        prob = expo * (1.0 / jnp.sum(expo, axis=0, keepdims=True))
        grad_value = product(prob.astype(BFLOAT), grad)
        grad_prob = times_transposed(only(mask, value), grad)
        grad_score = prob * (grad_prob - jnp.sum(prob * grad_prob, axis=0, keepdims=True))
        low = grad_score.astype(BFLOAT) * scale
        with_queries = product(low, both_queries)
        with_keys = contract_rows(low, both_keys)
        fresh = (
            with_keys[:, :LANES] + with_keys[:, LANES:],
            with_queries[:, :LANES] + with_queries[:, LANES:],
            grad_value,
            with_keys[:, :LANES],
            with_queries[:, :LANES],
        )
        outs = [jnp.where(mask, new, old) for new, old in zip(fresh, outs)]
    for index, out in enumerate(outs):
        out_ref[index] = out.astype(BFLOAT)


FREE = pl.CostEstimate(flops=0, transcendentals=0, bytes_accessed=0)


ROOMY = pltpu.CompilerParams(vmem_limit_bytes=48 * 1024 * 1024)


def attention_call(kernel, lengths, arrays, stacked):
    tokens, width = arrays[0].shape
    pages = lengths.shape[0]
    spec = pl.BlockSpec((tokens // pages, LANES), lambda page, pair: (page, pair))
    out_spec, shape = spec, (tokens, width)
    if stacked:
        shape = (stacked, tokens, width)
        out_spec = pl.BlockSpec(
            (stacked, tokens // pages, LANES), lambda page, pair: (0, page, pair)
        )
    return pl.pallas_call(
        kernel,
        grid=(pages, width // LANES),
        in_specs=[pl.BlockSpec(memory_space=pltpu.SMEM)] + [spec] * len(arrays),
        out_specs=out_spec,
        out_shape=jax.ShapeDtypeStruct(shape, BFLOAT),
        compiler_params=ROOMY,
        cost_estimate=FREE,
    )(lengths, *arrays)


def start_kernel(first_ref, grad_ref, mat_ref, out_ref, place_ref, sums_ref, total):
    step = pl.program_id(0)
    grad = grad_ref[...]
    term = times_transposed(grad, mat_ref[...])
    sums_ref[...] = jnp.sum(grad.astype(FLOAT), axis=0, keepdims=True)

    @pl.when(step == 0)
    def _():
        total[...] = term

    @pl.when(step == 1)
    def _():
        low = (total[...] + term).astype(BFLOAT)
        place_ref[...] = low
        sums_ref[...] = jnp.sum(low.astype(FLOAT), axis=0, keepdims=True)

    @pl.when(step == 2)
    def _():
        out_ref[...] = first_ref[...] + term

    @pl.when(step > 2)
    def _():
        out_ref[...] += term


def start_gradient(grad_first, pieces, packed, first_mat):
    tokens, width = grad_first.shape
    whole = pl.BlockSpec((tokens, width), lambda k: (0, 0))

    def piece(k):
        return jnp.where(k < 2, k + 3, k - 2)

    def mat(k):
        return first_mat + jnp.where(k < 2, k + 4, k - 1)

    return pl.pallas_call(
        start_kernel,
        grid=(5,),
        in_specs=[
            whole,
            pl.BlockSpec((None, tokens, width), lambda k: (piece(k), 0, 0)),
            pl.BlockSpec((None, width, width), lambda k: (mat(k), 0, 0)),
        ],
        out_specs=[whole, whole, pl.BlockSpec((None, 1, width), lambda k: (k, 0, 0))],
        out_shape=[
            jax.ShapeDtypeStruct((tokens, width), FLOAT),
            jax.ShapeDtypeStruct((tokens, width), BFLOAT),
            jax.ShapeDtypeStruct((5, 1, width), FLOAT),
        ],
        scratch_shapes=[pltpu.VMEM((tokens, width), FLOAT)],
        compiler_params=ROOMY,
        cost_estimate=FREE,
    )(grad_first, pieces, packed)


def token_kernel(act_ref, mixed_ref, grad_ref, attended_ref, out_ref):
    @pl.when(pl.program_id(0) < 3)
    def _():
        out_ref[...] = contract_rows(act_ref[...], grad_ref[...]).astype(BFLOAT)

    @pl.when(pl.program_id(0) == 3)
    def _():
        out_ref[...] = contract_rows(mixed_ref[...], attended_ref[...]).astype(BFLOAT)


def token_gradients(act, mixed, pieces, grad_attended):
    tokens, width = act.shape
    whole = pl.BlockSpec((tokens, width), lambda k: (0, 0))
    return pl.pallas_call(
        token_kernel,
        grid=(4,),
        in_specs=[
            whole,
            whole,
            pl.BlockSpec((None, tokens, width), lambda k: (jnp.minimum(k, 2), 0, 0)),
            whole,
        ],
        out_specs=pl.BlockSpec((None, width, width), lambda k: (k, 0, 0)),
        out_shape=jax.ShapeDtypeStruct((4, width, width), BFLOAT),
        compiler_params=ROOMY,
        cost_estimate=FREE,
    )(act, mixed, pieces, grad_attended)


def box_kernel(features_ref, place_ref, grad_ref, grad_place_ref, out_ref):
    @pl.when(pl.program_id(0) < 2)
    def _():
        out_ref[...] = contract_rows(place_ref[...], grad_ref[...]).astype(BFLOAT)

    @pl.when(pl.program_id(0) == 2)
    def _():
        out_ref[...] = contract_rows(features_ref[...], grad_place_ref[...]).astype(BFLOAT)


def box_gradients(features_low, place, pieces, grad_place):
    tokens, width = place.shape
    whole = pl.BlockSpec((tokens, width), lambda k: (0, 0))
    return pl.pallas_call(
        box_kernel,
        grid=(3,),
        in_specs=[
            whole,
            whole,
            pl.BlockSpec((None, tokens, width), lambda k: (jnp.minimum(k, 1) + 3, 0, 0)),
            whole,
        ],
        out_specs=pl.BlockSpec((None, width, width), lambda k: (k, 0, 0)),
        out_shape=jax.ShapeDtypeStruct((3, width, width), BFLOAT),
        compiler_params=ROOMY,
        cost_estimate=FREE,
    )(features_low, place, pieces, grad_place)


class Buckets(NamedTuple):
    owner: jax.Array
    row: jax.Array
    first: jax.Array
    rank: jax.Array
    fullest: jax.Array


def bucket_ids(ids, shard_rows):
    owner, row = ids // shard_rows, ids % shard_rows
    index = jnp.arange(ids.shape[0], dtype=jnp.int32)
    earlier = index[None, :] < index[:, None]
    same = ids[:, None] == ids[None, :]
    first = ~jnp.any(same & earlier, axis=1)
    before = (owner[:, None] == owner[None, :]) & earlier & first[None, :]
    rank = jnp.sum(before.astype(jnp.int32), axis=1)
    rank = jnp.sum(jnp.where(same & first[None, :], rank[None, :], 0), axis=1)
    return Buckets(owner, row, first, rank, jnp.max(rank) + 1)


def bucket_places(buckets, capacity, stride, turn):
    shifted = buckets.rank - turn * capacity
    inside = (shifted >= 0) & (shifted < capacity)
    return jnp.where(inside, buckets.owner * stride + shifted, -1)


def bucket_requests(buckets, places, groups, stride):
    hit = (places[:, None] == jnp.arange(groups * stride)[None, :]) & buckets.first[:, None]
    rows = jnp.sum(jnp.where(hit, buckets.row[:, None] + 1, 0), axis=0) - 1
    return rows.reshape(groups, stride)


def one_hot(index, count):
    return (index[:, None] == jnp.arange(count, dtype=jnp.int32)[None, :]).astype(BFLOAT)


def feed_kernel(middle_ref, up_ref, bias_ref, down_ref, active_ref, slope_ref, out_ref):
    value = product(middle_ref[...], up_ref[...]) + bias_ref[...]
    share = 0.5 * (1.0 + lax.erf(value * math.sqrt(0.5)))
    density = jnp.exp(-0.5 * value * value) * (1.0 / math.sqrt(2.0 * math.pi))
    active = (value * share).astype(BFLOAT)
    active_ref[...] = active
    slope_ref[...] = share + value * density
    out = product(active, down_ref[...])

    @pl.when(pl.program_id(0) == 0)
    def _():
        out_ref[...] = out

    @pl.when(pl.program_id(0) > 0)
    def _():
        out_ref[...] += out


def feed_forward(middle_low, packed, bias):
    tokens, width = middle_low.shape
    hidden = bias.shape[0]
    blocks = hidden // width
    whole = pl.BlockSpec((tokens, width), lambda j: (0, 0))
    columns = pl.BlockSpec((tokens, width), lambda j: (0, j))
    return pl.pallas_call(
        feed_kernel,
        grid=(blocks,),
        in_specs=[
            whole,
            pl.BlockSpec((None, width, width), lambda j: (j, 0, 0)),
            pl.BlockSpec((1, width), lambda j: (0, j)),
            pl.BlockSpec((None, width, width), lambda j: (blocks + j, 0, 0)),
        ],
        out_specs=[columns, columns, whole],
        out_shape=[
            jax.ShapeDtypeStruct((tokens, hidden), BFLOAT),
            jax.ShapeDtypeStruct((tokens, hidden), FLOAT),
            jax.ShapeDtypeStruct((tokens, width), FLOAT),
        ],
        compiler_params=ROOMY,
        cost_estimate=FREE,
    )(middle_low, packed, bias[None], packed)


def feed_back_kernel(
    grad_ref,
    middle_ref,
    active_ref,
    slope_ref,
    up_ref,
    down_ref,
    grads_ref,
    grad_bias_ref,
    out_ref,
):
    grad = grad_ref[...]
    grad_upper = (times_transposed(grad, down_ref[...]) * slope_ref[...]).astype(BFLOAT)
    grad_bias_ref[...] = jnp.sum(grad_upper.astype(FLOAT), axis=0, keepdims=True)
    grads_ref[0] = contract_rows(middle_ref[...], grad_upper).astype(BFLOAT)
    grads_ref[1] = contract_rows(active_ref[...], grad).astype(BFLOAT)
    out = times_transposed(grad_upper, up_ref[...])

    @pl.when(pl.program_id(0) == 0)
    def _():
        out_ref[...] = out

    @pl.when(pl.program_id(0) > 0)
    def _():
        out_ref[...] += out


def feed_backward(grad_feed, middle_low, active, slope, packed):
    tokens, width = middle_low.shape
    hidden = active.shape[1]
    blocks = hidden // width
    whole = pl.BlockSpec((tokens, width), lambda j: (0, 0))
    columns = pl.BlockSpec((tokens, width), lambda j: (0, j))
    return pl.pallas_call(
        feed_back_kernel,
        grid=(blocks,),
        in_specs=[
            whole,
            whole,
            columns,
            columns,
            pl.BlockSpec((None, width, width), lambda j: (j, 0, 0)),
            pl.BlockSpec((None, width, width), lambda j: (blocks + j, 0, 0)),
        ],
        out_specs=[
            pl.BlockSpec((2, None, width, width), lambda j: (0, j, 0, 0)),
            pl.BlockSpec((1, width), lambda j: (0, j)),
            whole,
        ],
        out_shape=[
            jax.ShapeDtypeStruct((2, blocks, width, width), BFLOAT),
            jax.ShapeDtypeStruct((1, hidden), FLOAT),
            jax.ShapeDtypeStruct((tokens, width), FLOAT),
        ],
        compiler_params=ROOMY,
        cost_estimate=FREE,
    )(grad_feed, middle_low, active, slope, packed, packed)


def logits_kernel(rows_ref, table_ref, label_ref, expo_ref, stats_ref):
    logits = times_transposed(rows_ref[...], table_ref[...])
    peak = jnp.max(logits, axis=1, keepdims=True)
    expo = jnp.exp(logits - peak)
    expo_ref[...] = expo.astype(BFLOAT)
    mass = jnp.sum(expo, axis=1, keepdims=True)
    column = lax.broadcasted_iota(jnp.int32, logits.shape, 1)
    target = jnp.sum(jnp.where(column == label_ref[...], logits, 0.0), axis=1, keepdims=True)
    lane = lax.broadcasted_iota(jnp.int32, (logits.shape[0], LANES), 1)
    stats = jnp.where(lane == 0, peak, jnp.where(lane == 1, mass, target))
    stats_ref[...] = stats.T[:8]


def head_logits(rows_all, table_low, own_labels):
    count, width = rows_all.shape
    shard_rows = table_low.shape[0]
    step = 256
    return pl.pallas_call(
        logits_kernel,
        grid=(count // step,),
        in_specs=[
            pl.BlockSpec((step, width), lambda i: (i, 0)),
            pl.BlockSpec((shard_rows, width), lambda i: (0, 0)),
            pl.BlockSpec((step, 1), lambda i: (i, 0)),
        ],
        out_specs=[
            pl.BlockSpec((step, shard_rows), lambda i: (i, 0)),
            pl.BlockSpec((8, step), lambda i: (0, i)),
        ],
        out_shape=[
            jax.ShapeDtypeStruct((count, shard_rows), BFLOAT),
            jax.ShapeDtypeStruct((8, count), FLOAT),
        ],
        compiler_params=ROOMY,
        cost_estimate=FREE,
    )(rows_all, table_low, own_labels[:, None])


def column_sum(value):
    return jnp.sum(value.astype(FLOAT), axis=0)


def layer_forward(weights, embedded, place, box_query, box_key, lengths):
    mats, packed, gains, up_bias = weights
    start_state = layer_norm(embedded, gains[0], gains[1])
    act = start_state.astype(BFLOAT)
    query = (product(act, mats[1]) + gains[6]).astype(BFLOAT)
    keys = product(act, mats[2]).astype(BFLOAT)
    values = (product(act, mats[3]) + gains[7]).astype(BFLOAT)
    mixed = attention_call(attend_kernel, lengths, (query, keys, values, box_query, box_key), 0)
    first_sum = start_state + (product(mixed, mats[6]) + gains[8])
    middle = layer_norm(first_sum, gains[2], gains[3])
    middle_low = middle.astype(BFLOAT)
    active, slope, feed = feed_forward(middle_low, packed, up_bias)
    second_sum = middle + (feed + gains[10])
    kept = (
        embedded,
        act,
        place,
        query,
        keys,
        values,
        box_query,
        box_key,
        mixed,
        first_sum,
        middle_low,
        slope,
        active,
        second_sum,
    )
    return (layer_norm(second_sum, gains[4], gains[5]), kept)


def layer_backward(weights, features_low, lengths, kept, grad_out, head_parts, lines, tools):
    mats, packed, gains, up_bias = weights
    (
        embedded,
        act,
        place,
        query,
        keys,
        values,
        box_query,
        box_key,
        mixed,
        first_sum,
        middle_low,
        slope,
        active,
        second_sum,
    ) = kept
    compacted, give, from_copies, give_rows = tools

    def send(value, name):
        own, blocks = sends(value, lines[name], AXES[name])
        return own, blocks

    def travel(pair, name, *until):
        line = lines[name]
        moved = [shifted(block, line, step) for step, block in enumerate(pair[1], 1)]
        if until:
            moved = list(after(tuple(moved), *until))
        total = pair[0].astype(FLOAT)
        for value in moved:
            total = total + value.astype(FLOAT)
        return total.astype(BFLOAT)

    grad_second, gain_four, gain_five = jax.vjp(layer_norm, second_sum, gains[4], gains[5])[1](
        grad_out
    )
    grad_feed = grad_second.astype(BFLOAT)
    grad_feeds, grad_bias, fed_back = feed_backward(grad_feed, middle_low, active, slope, packed)
    feeds_sum = lax.psum_scatter(grad_feeds, "fsdp", scatter_dimension=2, tiled=True)
    grad_first, gain_two, gain_three = jax.vjp(layer_norm, first_sum, gains[2], gains[3])[1](
        grad_second + fed_back
    )
    grad_attended = grad_first.astype(BFLOAT)
    grad_mixed = times_transposed(grad_attended, mats[6]).astype(BFLOAT)
    pieces = attention_call(
        attend_back_kernel, lengths, (query, keys, values, box_query, box_key, grad_mixed), 5
    )
    pieces = after(pieces, head_parts[2])
    first_mat = packed.shape[0] - mats.shape[0]
    grad_start, grad_place, sums = start_gradient(grad_first, pieces, packed, first_mat)
    grad_start = after(grad_start, head_parts[3])
    grad_embedded, gain_zero, gain_one = jax.vjp(layer_norm, embedded, gains[0], gains[1])[1](
        grad_start
    )
    grad_vectors = jnp.stack(
        [
            gain_zero,
            gain_one,
            gain_two,
            gain_three,
            gain_four,
            gain_five,
            sums[2, 0],
            sums[4, 0],
            column_sum(grad_attended),
            sums[1, 0],
            column_sum(grad_feed),
        ]
    )
    parts = two_parts(grad_embedded)
    compact = compacted(parts, grad_vectors, grad_bias)
    returned = give(compact)
    pieces = after(pieces, compact)
    token_part = token_gradients(act, mixed, pieces, grad_attended)
    token_core = send(by_owner(token_part, lines), "core")
    pieces = after(pieces, *token_core[1])
    box_part = box_gradients(features_low, place, pieces, grad_place)
    token_y = send(travel(token_core, "core", box_part), "y")
    box_part = after(box_part, *token_y[1])
    box_core = send(by_owner(box_part, lines), "core")
    box_x = send(travel(box_core, "core"), "x")
    returned = after(returned, *box_x[1])
    rows = from_copies(returned)
    feeds_sum = after(feeds_sum, returned)
    others = after(tuple(rows[1:]), feeds_sum)
    token_z = send(travel(token_y, "y", feeds_sum), "z")
    box_y = send(travel(box_x, "x", token_z[1][0]), "y")
    spread = [give_rows(0, after(rows[0], *box_y[1]))]
    token_sum = travel(token_z, "z", spread[0])[:, 0, 0, 0]
    box_z = send(travel(box_y, "y", token_sum), "z")
    others = after(others, *box_z[1])
    spread += [give_rows(index, value) for index, value in enumerate(others, 1)]
    box_half = travel(box_z, "z", spread[-1])[:, 0, 0, 0]
    feeds_other = after(from_other_copies(feeds_sum, lines), box_half)
    feeds_sum = feeds_sum.astype(FLOAT) + feeds_other.astype(FLOAT)
    token_mats = both_copies(token_sum, lines)
    box_mats = gather_line(box_half, lines["x"], 2).astype(FLOAT)
    grad_mats = jnp.concatenate([box_mats[2:], token_mats[:3], box_mats[:2], token_mats[3:]])
    return ((grad_mats, feeds_sum), spread, [rows[0], *others], parts)


def combine_mass(first, second):
    peak = jnp.maximum(first[0], second[0])
    mass = first[1] * jnp.exp(first[0] - peak) + second[1] * jnp.exp(second[0] - peak)
    return jnp.stack([peak, mass, first[2] + second[2]])


def body(
    token_ids,
    boxes,
    lengths,
    slots,
    labels,
    table,
    mats,
    up,
    down,
    vectors,
    up_bias,
    table_rows,
    table_cols,
    mats_rows,
    mats_cols,
    up_rows,
    up_cols,
    down_rows,
    down_cols,
    vectors_second,
    up_bias_second,
):
    pages = lengths.shape[0]
    tokens = token_ids.shape[0]
    page_len = tokens // pages
    width = table.shape[1]
    shard_rows = table.shape[0]
    slot_count = slots.shape[1]
    groups, copies = lax.axis_size("fsdp"), lax.axis_size("rep")
    group, copy = lax.axis_index("fsdp"), lax.axis_index("rep")
    lines = lines_of(groups, copies)
    table_low = table.astype(BFLOAT)

    own_small = vectors.size + up_bias.size
    small_rows = -(-own_small // width)
    stride = 16 + -(-tokens // (16 * groups)) * 16
    capacity = stride - 2 * small_rows
    buckets = bucket_ids(token_ids, shard_rows)
    places = bucket_places(buckets, capacity, stride, 0)
    requests = bucket_requests(buckets, places, groups, stride)
    own_news = jnp.concatenate([labels.reshape(-1), lengths, buckets.fullest[None]])
    news = jnp.concatenate(
        [
            jnp.repeat(requests, copies, axis=0),
            jnp.broadcast_to(own_news[None], (groups * copies, own_news.shape[0])),
        ],
        axis=1,
    )
    news = lax.all_to_all(news, ("fsdp", "rep"), 0, 0, tiled=True)
    asked = news[:, :stride].reshape(groups, copies, stride)
    asked = jnp.transpose(asked, (1, 0, 2)).reshape(copies, groups * stride)
    labels_all = news[:, stride : stride + pages * slot_count]
    labels_all = labels_all.reshape(groups, copies, pages * slot_count)
    labels_all = lax.dynamic_index_in_dim(labels_all, copy, 1, False).reshape(-1)
    lengths_all = news[:, stride + pages * slot_count : -1]
    turns = (jnp.max(news[:, -1]) + capacity - 1) // capacity

    def fetch(spots, wanted):
        rows = product(one_hot(wanted, shard_rows), table_low).astype(BFLOAT)
        rows = lax.all_to_all(rows.reshape(groups, stride, width), "fsdp", 0, 0, tiled=True)
        return product(one_hot(spots, groups * stride), rows.reshape(groups * stride, width))

    def ask(turn):
        spots = bucket_places(buckets, capacity, stride, turn)
        wanted = bucket_requests(buckets, spots, groups, stride)
        return spots, lax.all_to_all(wanted, "fsdp", 0, 0, tiled=True).reshape(-1)

    embedded = fetch(places, lax.dynamic_index_in_dim(asked, copy, 0, False))
    embedded = lax.while_loop(
        lambda state: state[0] < turns,
        lambda state: (state[0] + 1, state[1] + fetch(*ask(state[0]))),
        (jnp.int32(1), embedded),
    )[1]

    own_labels = labels_all - group * shard_rows
    label_rows = product(one_hot(own_labels, shard_rows), table_low).astype(BFLOAT)
    embedded = after(embedded, label_rows)

    small = jnp.concatenate([vectors.astype(BFLOAT).reshape(-1), up_bias.astype(BFLOAT)])[None]

    def lay(first, second, bit):
        low = (group & bit) == 0
        return jnp.concatenate([jnp.where(low, first, second), jnp.where(low, second, first)])

    bit = 1
    while bit < groups:
        pairs = [(i, i ^ bit) for i in range(groups)]
        small = lay(small, lax.ppermute(small, "fsdp", pairs), bit)
        bit *= 2
    split = vectors.size
    gains = small[:, :split].reshape(groups, vectors.shape[0], -1)
    gains = jnp.transpose(gains, (1, 0, 2)).reshape(vectors.shape[0], width).astype(FLOAT)
    own_rows, hidden = up.shape
    feed_blocks = hidden // width
    bias = small[:, split:].reshape(groups, feed_blocks, own_rows)
    bias = jnp.transpose(bias, (1, 0, 2)).reshape(-1).astype(FLOAT)
    gains, bias = lax.optimization_barrier((gains, bias))
    up_blocks = up.astype(BFLOAT).reshape(own_rows, groups, feed_blocks, own_rows)
    up_blocks = jnp.transpose(up_blocks, (2, 0, 1, 3)).reshape(feed_blocks, own_rows, width)
    down_blocks = down.astype(BFLOAT).reshape(feed_blocks, own_rows, width)
    packed = jnp.concatenate([up_blocks, down_blocks, mats.astype(BFLOAT)])
    packed = lax.all_gather(packed, "fsdp", axis=1, tiled=True)
    layer_mats = packed[2 * feed_blocks :]
    weights = (layer_mats, packed, gains, bias)

    features_low = box_features(boxes, width).astype(BFLOAT)
    place = (product(features_low, layer_mats[0]) + gains[9]).astype(BFLOAT)
    box_query = product(place, layer_mats[4]).astype(BFLOAT)
    box_key = product(place, layer_mats[5]).astype(BFLOAT)
    top_state, kept = layer_forward(weights, embedded, place, box_query, box_key, lengths)

    where_at = slots * lengths[:, None] // 256 + jnp.arange(pages)[:, None] * page_len
    pick = one_hot(where_at.reshape(-1), tokens)
    rows_low = product(pick, top_state.astype(BFLOAT)).astype(BFLOAT)
    rows_all = rows_low[None, None, None]
    for axis, name in enumerate(("z", "y", "core")):
        rows_all = gather_line(rows_all, lines[name], axis)
    rows_all = rows_all.reshape(-1, width)
    expo, stats = head_logits(rows_all, table_low, own_labels)
    peak_here = stats[0]
    products = product(expo, table_low)
    stats = stats[:3].reshape(3, -1, LANES)
    stats = paired(stats, "fsdp", combine_mass, products).reshape(3, -1)
    products, peak, mass, target = lax.optimization_barrier((products, *stats))
    log_total = peak + jnp.log(mass)
    factor = jnp.exp(peak_here - log_total)

    is_token = jnp.arange(slot_count) < M_TOK
    valid_all = valid_slots(lengths_all.reshape(-1), slot_count).astype(FLOAT)
    count_token = jnp.sum(jnp.where(is_token, valid_all, 0.0))
    count_area = jnp.sum(jnp.where(is_token, 0.0, valid_all))
    valid = valid_all.reshape(groups, copies, pages, slot_count)
    valid = lax.dynamic_index_in_dim(valid, copy, 1, False).reshape(-1, slot_count)
    loss_rows = (log_total - target).reshape(-1, slot_count) * valid
    token_loss = jnp.sum(jnp.where(is_token, loss_rows, 0.0))
    area_loss = jnp.sum(jnp.where(is_token, 0.0, loss_rows))
    figure = jnp.arange(4)
    losses = paired(jnp.where(figure < 2, token_loss, area_loss), "rep", jnp.add)
    loss_parts = jnp.where(figure == 1, count_token, jnp.where(figure == 3, count_area, losses))
    share = jnp.where(is_token, 1.0 / count_token, 1.0 / count_area)
    weight = (valid * share[None, :]).reshape(-1)
    grad_rows = (products * factor[:, None] - label_rows.astype(FLOAT)) * weight[:, None]
    grad_rows = grad_rows.astype(BFLOAT)
    grad_rows = grad_rows.reshape(
        lines["z"].count, lines["y"].count, lines["core"].count, -1, width
    )
    own, blocks = sends(grad_rows, lines["core"], 2)
    weighted = (rows_all.astype(FLOAT) * weight[:, None]).astype(BFLOAT)
    expo, weighted = after((expo, weighted), *blocks)
    mine = own_labels[:, None] == jnp.arange(shard_rows)[None, :]
    grad_logits = expo.astype(FLOAT) * factor[:, None] - mine.astype(FLOAT)
    own, blocks = sends(received(own, blocks, lines["core"]), lines["y"], 1)
    grad_logits = after(grad_logits.astype(BFLOAT), *blocks)
    head_low = contract_rows(grad_logits, weighted).astype(BFLOAT)
    own, blocks = sends(received(own, blocks, lines["y"]), lines["z"], 0)
    blocks = list(after(tuple(blocks), head_low))
    grad_rows = received(own, blocks, lines["z"]).reshape(-1, width)
    head_parts = [from_other_copies(part, lines) for part in jnp.split(head_low, 4)]
    grad_rows = after(grad_rows, *head_parts[:2])
    grad_top = sum(contract_rows(pick, part) for part in two_parts(grad_rows))

    def compacted(spots, parts):
        spread = one_hot(spots, groups * stride)
        return sum(contract_rows(spread, part) for part in parts)

    def compacted_first(parts, grad_vectors, grad_bias):
        small = grad_vectors.reshape(grad_vectors.shape[0], groups, -1)
        small = jnp.transpose(small, (1, 0, 2)).reshape(groups, -1)
        grad_bias = jnp.transpose(grad_bias.reshape(feed_blocks, groups, own_rows), (1, 0, 2))
        small = jnp.concatenate([small, grad_bias.reshape(groups, -1)], axis=1)
        small = jnp.pad(small, ((0, 0), (0, small_rows * width - own_small)))
        small = jnp.stack(two_parts(small.reshape(groups, small_rows, width)), axis=1)
        small = small.reshape(groups, 2 * small_rows, width).astype(FLOAT)
        small = jnp.pad(small, ((0, 0), (capacity, 0), (0, 0))).reshape(groups * stride, width)
        return (compacted(places, parts) + small).astype(BFLOAT)

    def give(rows):
        rows = lax.all_to_all(rows.reshape(groups, stride, width), "fsdp", 0, 0, tiled=True)
        return rows.reshape(groups * stride, width)

    def spread_rows(wanted, rows):
        return contract_rows(one_hot(wanted, shard_rows), rows)

    def small_sum(rows):
        rows = rows.reshape(groups, stride, width)[:, capacity:].astype(FLOAT)
        rows = jnp.sum(rows, axis=0).reshape(2, small_rows * width)
        return (rows[0] + rows[1])[:own_small]

    if copies == 2:
        from_copies = lambda value: [value, shifted(value, lines["x"], 1)]
        copy_order = [copy, 1 - copy]
    else:
        from_copies = lambda value: list(lax.all_gather(value, "rep"))
        copy_order = list(range(copies))
    asked_of = [lax.dynamic_index_in_dim(asked, index, 0, False) for index in copy_order]

    def give_rows(index, rows):
        return spread_rows(asked_of[index], rows)

    tools = (compacted_first, give, from_copies, give_rows)
    layer_grads, spread, given, embedded_parts = layer_backward(
        weights, features_low, lengths, kept, grad_top, head_parts, lines, tools
    )
    mats_grad, feeds_grad = layer_grads
    up_grad = jnp.transpose(feeds_grad[0].reshape(feed_blocks, own_rows, groups, own_rows), (1, 2, 0, 3))
    up_grad = up_grad.reshape(own_rows, hidden)
    down_grad = feeds_grad[1].reshape(hidden // groups, width)
    small = [small_sum(rows) for rows in given]
    small = sum(small[1:], small[0])
    vectors_grad = small[: vectors.size].reshape(vectors.shape)
    bias_grad = small[vectors.size :]

    head_grad = head_low.astype(FLOAT) + jnp.concatenate(head_parts).astype(FLOAT)
    table_grad = head_grad + sum(spread[1:], spread[0])

    def another(state):
        turn, total = state
        spots, wanted = ask(turn)
        given = from_copies(give(compacted(spots, embedded_parts).astype(BFLOAT)))
        spread = [spread_rows(*pair) for pair in zip(from_copies(wanted), given)]
        return turn + 1, total + sum(spread[1:], spread[0])

    table_grad = lax.while_loop(lambda state: state[0] < turns, another, (jnp.int32(1), table_grad))[1]

    depth = mats.shape[0]
    feed_cols = hidden // width
    sizes = [(shard_rows * groups, width)] + [(mats.shape[1] * groups, width)] * depth
    sizes += [(up.shape[0] * groups, hidden), (down.shape[0] * groups, width)]
    row_squares = [jnp.sum(grad * grad, axis=-1) for grad in (table_grad, mats_grad, up_grad, down_grad)]
    items = depth + 3
    lane = jnp.arange(width)
    singles = jnp.pad(jnp.sum(mats_rows, axis=1), (1, width - 1 - depth))
    for index, value in (
        (0, jnp.sum(table_rows)),
        (items - 2, jnp.sum(up_rows)),
        (items - 1, jnp.sum(down_rows)),
        (items, jnp.sum(vectors_grad * vectors_grad)),
        (items + 1, jnp.sum(bias_grad * bias_grad)),
    ):
        singles = jnp.where(lane == index, value, singles)
    sums = jnp.concatenate(
        [
            jnp.sum(table_grad * table_grad, axis=0)[None],
            jnp.sum(mats_grad * mats_grad, axis=1),
            jnp.sum(up_grad * up_grad, axis=0).reshape(feed_cols, width),
            jnp.sum(down_grad * down_grad, axis=0)[None],
            singles[None],
        ]
    )
    cols_old = jnp.concatenate(
        [table_cols[None], mats_cols, up_cols.reshape(feed_cols, width), down_cols[None]]
    )
    sums = paired(sums, "fsdp", jnp.add)
    totals = jnp.sum(sums[:-1], axis=1)
    norm_square = jnp.sum(totals) + sums[-1, items] + sums[-1, items + 1]
    grad_norm = jnp.sqrt(norm_square)
    clip = jnp.minimum(1.0, CLIP_NORM / grad_norm)
    square = clip * clip

    def renewed(old, value):
        return DECAY * old + (1.0 - DECAY) * (value + TINY_TERM)

    first_up, after_up = 1 + depth, 1 + depth + feed_cols
    of_item = [[k] for k in range(first_up)] + [list(range(first_up, after_up)), [after_up]]
    item_totals = jnp.concatenate(
        [totals[:first_up], jnp.sum(totals[first_up:after_up])[None], totals[after_up:]]
    )
    tall = jnp.array([size[0] for size in sizes], FLOAT)
    wide = jnp.array([size[1] for size in sizes], FLOAT)
    means = renewed(sums[-1, :items] / tall, square * item_totals / (tall * wide))
    repeats = [len(rows) for rows in of_item]
    tall_rows = jnp.array([s for size, n in zip(sizes, repeats) for s in [size[0]] * n], FLOAT)
    mean_rows = jnp.concatenate(
        [means[:first_up], jnp.broadcast_to(means[first_up], (feed_cols,)), means[first_up + 1 :]]
    )
    cols_new = renewed(cols_old, square * sums[:-1] / tall_rows[:, None])
    col_factors = lax.rsqrt(cols_new / mean_rows[:, None])
    step = LEARN_RATE * clip

    def updated(grad, param, rows_old, row_square, col_factor):
        rows_new = renewed(rows_old, square * row_square / grad.shape[-1])
        factor = step * lax.rsqrt(rows_new)
        return grad * clip, rows_new, param - grad * factor[..., None] * col_factor[..., None, :]

    up_factor = col_factors[first_up:after_up].reshape(hidden)
    table_out = updated(table_grad, table, table_rows, row_squares[0], col_factors[0])
    mats_out = updated(mats_grad, mats, mats_rows, row_squares[1], col_factors[1:first_up])
    up_out = updated(up_grad, up, up_rows, row_squares[2], up_factor)
    down_out = updated(down_grad, down, down_rows, row_squares[3], col_factors[after_up])
    clipped_vectors = vectors_grad * clip
    vectors_second_new = DECAY * vectors_second + (1.0 - DECAY) * (
        clipped_vectors * clipped_vectors + TINY_TERM
    )
    vectors_new = vectors - VECTOR_RATE * clipped_vectors * lax.rsqrt(vectors_second_new)
    clipped_bias = bias_grad * clip
    bias_second_new = DECAY * up_bias_second + (1.0 - DECAY) * (
        clipped_bias * clipped_bias + TINY_TERM
    )
    bias_new = up_bias - VECTOR_RATE * clipped_bias * lax.rsqrt(bias_second_new)
    return (
        table_out[0],
        table_out[1],
        cols_new[0],
        table_out[2],
        mats_out[0],
        mats_out[1],
        cols_new[1:first_up],
        mats_out[2],
        up_out[0],
        up_out[1],
        cols_new[first_up:after_up].reshape(hidden),
        up_out[2],
        down_out[0],
        down_out[1],
        cols_new[after_up],
        down_out[2],
        clipped_vectors,
        vectors_second_new,
        vectors_new,
        clipped_bias,
        bias_second_new,
        bias_new,
        grad_norm,
        loss_parts,
    )


def solution(mesh):
    return jax.shard_map(
        body,
        mesh=mesh,
        in_specs=(
            P(("fsdp", "rep")),
            P(None, ("fsdp", "rep")),
            P(("fsdp", "rep")),
            P(("fsdp", "rep"), None),
            P(("fsdp", "rep"), None),
            P("fsdp", None),
            P(None, "fsdp", None),
            P("fsdp", None),
            P("fsdp", None),
            P(None, "fsdp"),
            P("fsdp"),
            P("fsdp"),
            P(),
            P(None, "fsdp"),
            P(),
            P("fsdp"),
            P(),
            P("fsdp"),
            P(),
            P(None, "fsdp"),
            P("fsdp"),
        ),
        out_specs=(
            P("fsdp", None),
            P("fsdp"),
            P(),
            P("fsdp", None),
            P(None, "fsdp", None),
            P(None, "fsdp"),
            P(),
            P(None, "fsdp", None),
            P("fsdp", None),
            P("fsdp"),
            P(),
            P("fsdp", None),
            P("fsdp", None),
            P("fsdp"),
            P(),
            P("fsdp", None),
            P(None, "fsdp"),
            P(None, "fsdp"),
            P(None, "fsdp"),
            P("fsdp"),
            P("fsdp"),
            P("fsdp"),
            P(),
            P(),
        ),
        check_vma=False,
    )
```

```python
import math
from typing import NamedTuple

import jax
import jax.numpy as jnp
from jax import lax
from jax.experimental import pallas as pl
from jax.experimental.pallas import tpu as pltpu
from jax.sharding import PartitionSpec as P

HEAD_DIM = 64
PAGE_LEN = 512
M_TOK = 64
M_AREA = 64
STEP = 10


EPSILON = 1e-05
CLIP_NORM = 0.1
LEARN_RATE = 0.02
VECTOR_RATE = 0.3
TINY_TERM = 1e-30
NEGATIVE = -1e30
BFLOAT = jnp.bfloat16
FLOAT = jnp.float32
LANES = 128
DECAY = 1.0 - STEP ** (-0.8)


class Line(NamedTuple):
    axis: str
    total: int
    stride: int
    count: int


def lines_of(groups, copies):
    cores = min(2, groups)
    rest = (groups // cores).bit_length() - 1
    y_count = 1 << (rest // 2)
    z_count = groups // (cores * y_count)
    return {
        "z": Line("fsdp", groups, cores * y_count, z_count),
        "y": Line("fsdp", groups, cores, y_count),
        "core": Line("fsdp", groups, 1, cores),
        "x": Line("rep", copies, 1, copies),
    }


def place_on(line):
    return lax.axis_index(line.axis) // line.stride % line.count


def shifted(value, line, step):
    pairs = []
    for i in range(line.total):
        place = i // line.stride % line.count
        pairs.append((i, i + ((place + step) % line.count - place) * line.stride))
    return lax.ppermute(value, line.axis, pairs)


def gather_line(value, line, axis):
    count = line.count
    if count == 1:
        return value
    here = place_on(line)
    pieces = [value] + [shifted(value, line, step) for step in range(1, count)]
    blocks = []
    for place in range(count):
        blocks.append(lax.select_n(here, *[pieces[(i - place) % count] for i in range(count)]))
    return jnp.concatenate(blocks, axis=axis)


def sends(value, line, axis):
    size = value.shape[axis] // line.count
    here = place_on(line)

    def block(place):
        return lax.dynamic_slice_in_dim(value, place * size, size, axis)

    return block(here), [
        block((here + step) % line.count).astype(BFLOAT) for step in range(1, line.count)
    ]


def received(own, blocks, line):
    total = own.astype(FLOAT)
    for step, value in enumerate(blocks, 1):
        total = total + shifted(value, line, step).astype(FLOAT)
    return total


def reduce_line(value, line, axis):
    return received(*sends(value, line, axis), line)


def after(value, *others):
    return lax.optimization_barrier((value, *others))[0]


def paired(value, axis, combine, beside=None):
    size = lax.axis_size(axis)
    bit = 1
    while bit < size:
        pairs = [(i, i ^ bit) for i in range(size)]
        other = lax.ppermute(value, axis, pairs)
        if beside is not None and bit == 2:
            other = after(other, beside)
        value = combine(value, other)
        bit *= 2
    return value


def by_owner(value, lines):
    count, _, columns = value.shape
    return value.reshape(count, lines["z"].count, lines["y"].count, lines["core"].count, -1, columns)


AXES = {"z": 1, "y": 2, "core": 3, "x": 5}


def part_sends(value, lines, name):
    return sends(value, lines[name], AXES[name])


def part_received(pair, lines, name):
    return received(*pair, lines[name]).astype(BFLOAT)


def both_copies(value, lines):
    if lines["x"].count == 2:
        return value.astype(FLOAT) + shifted(value, lines["x"], 1).astype(FLOAT)
    return lax.psum(value, "rep").astype(FLOAT)


def from_other_copies(value, lines):
    if lines["x"].count == 2:
        return shifted(value, lines["x"], 1)
    return (lax.psum(value, "rep").astype(FLOAT) - value.astype(FLOAT)).astype(BFLOAT)


def layer_norm(value, gain, shift):
    center = value - jnp.mean(value, axis=-1, keepdims=True)
    spread = jnp.mean(center * center, axis=-1, keepdims=True)
    return center * lax.rsqrt(spread + EPSILON) * gain + shift


def box_features(boxes, width):
    count = width // 8
    freqs = jnp.exp(-math.log(10000.0) * jnp.arange(count, dtype=FLOAT) / count)
    angle = boxes.astype(FLOAT)[:, :, None] * freqs[None, None, :]
    waves = jnp.concatenate([jnp.sin(angle), jnp.cos(angle)], axis=2)
    return jnp.transpose(waves, (1, 0, 2)).reshape(boxes.shape[1], width)


def valid_slots(lengths, slot_count):
    n_tok = jnp.minimum(M_TOK, 1 + lengths * M_TOK // PAGE_LEN)
    n_area = jnp.minimum(M_AREA, 1 + lengths * (3 * M_AREA) // (4 * PAGE_LEN))
    index = jnp.arange(slot_count, dtype=jnp.int32)[None, :]
    return jnp.where(index < M_TOK, index < n_tok[:, None], index - M_TOK < n_area[:, None])


def product(left, right):
    return jnp.dot(left, right, preferred_element_type=FLOAT)


def contract_rows(left, right):
    return lax.dot_general(left, right, (((0,), (0,)), ((), ())), preferred_element_type=FLOAT)


def times_transposed(left, right):
    return lax.dot_general(left, right, (((1,), (1,)), ((), ())), preferred_element_type=FLOAT)


def two_parts(value):
    high = value.astype(BFLOAT)
    return high, (value - high.astype(FLOAT)).astype(BFLOAT)


def side(index):
    lane = lax.broadcasted_iota(jnp.int32, (1, LANES), 1)
    return lane // HEAD_DIM == index


def only(mask, value):
    return jnp.where(mask, value, jnp.zeros_like(value))


def attend_kernel(length_ref, stack_ref, out_ref):
    length = length_ref[pl.program_id(0)]
    box_query, box_key, query, key, value = (stack_ref[index] for index in range(1, 6))
    keys = jnp.concatenate([key, box_key, key], axis=1)
    keep = lax.broadcasted_iota(jnp.int32, (1, key.shape[0]), 1) < length
    scale = jnp.asarray(HEAD_DIM ** (-0.5), BFLOAT)
    mixed = jnp.zeros(out_ref.shape, FLOAT)
    for head in range(LANES // HEAD_DIM):
        mask = side(head)
        own = only(mask, query) * scale
        other = only(mask, box_query) * scale
        score = times_transposed(jnp.concatenate([own, own, other], axis=1), keys)
        score = jnp.where(keep, score, NEGATIVE)
        expo = jnp.exp(score - jnp.max(score, axis=1, keepdims=True))
        prob = (expo * (1.0 / jnp.sum(expo, axis=1, keepdims=True))).astype(BFLOAT)
        mixed = jnp.where(mask, product(prob, value), mixed)
    out_ref[...] = mixed.astype(BFLOAT)


def attend_back_kernel(length_ref, stack_ref, grad_ref, out_ref):
    length = length_ref[pl.program_id(0)]
    box_query, box_key, query, key, value = (stack_ref[index] for index in range(1, 6))
    grad = grad_ref[...]
    rows = key.shape[0]
    keys = jnp.concatenate([key, box_key, key], axis=1)
    both_queries = jnp.concatenate([query, box_query], axis=1)
    both_keys = jnp.concatenate([key, box_key], axis=1)
    keep = lax.broadcasted_iota(jnp.int32, (rows, 1), 0) < length
    scale = jnp.asarray(HEAD_DIM ** (-0.5), BFLOAT)
    outs = [jnp.zeros((rows, LANES), FLOAT) for _ in range(5)]
    for head in range(LANES // HEAD_DIM):
        mask = side(head)
        own = only(mask, query) * scale
        other = only(mask, box_query) * scale
        score = times_transposed(keys, jnp.concatenate([own, own, other], axis=1))
        score = jnp.where(keep, score, NEGATIVE)
        expo = jnp.exp(score - jnp.max(score, axis=0, keepdims=True))
        prob = expo * (1.0 / jnp.sum(expo, axis=0, keepdims=True))
        grad_value = product(prob.astype(BFLOAT), grad)
        grad_prob = times_transposed(only(mask, value), grad)
        grad_score = prob * (grad_prob - jnp.sum(prob * grad_prob, axis=0, keepdims=True))
        low = grad_score.astype(BFLOAT) * scale
        with_queries = product(low, both_queries)
        with_keys = contract_rows(low, both_keys)
        fresh = (
            with_keys[:, :LANES] + with_keys[:, LANES:],
            with_queries[:, :LANES] + with_queries[:, LANES:],
            grad_value,
            with_keys[:, :LANES],
            with_queries[:, :LANES],
        )
        outs = [jnp.where(mask, new, old) for new, old in zip(fresh, outs)]
    for index, out in enumerate(outs):
        out_ref[index] = out.astype(BFLOAT)


FREE = pl.CostEstimate(flops=0, transcendentals=0, bytes_accessed=0)


ROOMY = pltpu.CompilerParams(vmem_limit_bytes=48 * 1024 * 1024)


def attention_call(kernel, lengths, stack, arrays, stacked):
    count, tokens, width = stack.shape
    pages = lengths.shape[0]
    spec = pl.BlockSpec((tokens // pages, LANES), lambda page, pair: (page, pair))

    def stack_spec(count):
        return pl.BlockSpec((count, tokens // pages, LANES), lambda page, pair: (0, page, pair))

    shape = (stacked, tokens, width) if stacked else (tokens, width)
    return pl.pallas_call(
        kernel,
        grid=(pages, width // LANES),
        in_specs=[pl.BlockSpec(memory_space=pltpu.SMEM), stack_spec(count)] + [spec] * len(arrays),
        out_specs=stack_spec(stacked) if stacked else spec,
        out_shape=jax.ShapeDtypeStruct(shape, BFLOAT),
        compiler_params=ROOMY,
        cost_estimate=FREE,
    )(lengths, stack, *arrays)


def start_kernel(first_ref, grad_ref, mat_ref, out_ref, place_ref, sums_ref, total):
    step = pl.program_id(0)
    grad = grad_ref[...]
    term = times_transposed(grad, mat_ref[...])
    sums_ref[...] = jnp.sum(grad.astype(FLOAT), axis=0, keepdims=True)

    @pl.when(step == 0)
    def _():
        total[...] = term

    @pl.when(step == 1)
    def _():
        low = (total[...] + term).astype(BFLOAT)
        place_ref[...] = low
        sums_ref[...] = jnp.sum(low.astype(FLOAT), axis=0, keepdims=True)

    @pl.when(step == 2)
    def _():
        out_ref[...] = first_ref[...] + term

    @pl.when(step > 2)
    def _():
        out_ref[...] += term


def start_gradient(grad_first, pieces, packed, first_mat):
    tokens, width = grad_first.shape
    whole = pl.BlockSpec((tokens, width), lambda k: (0, 0))

    def piece(k):
        return jnp.where(k < 2, k + 3, k - 2)

    def mat(k):
        return first_mat + jnp.where(k < 2, k + 4, k - 1)

    return pl.pallas_call(
        start_kernel,
        grid=(5,),
        in_specs=[
            whole,
            pl.BlockSpec((None, tokens, width), lambda k: (piece(k), 0, 0)),
            pl.BlockSpec((None, width, width), lambda k: (mat(k), 0, 0)),
        ],
        out_specs=[whole, whole, pl.BlockSpec((None, 1, width), lambda k: (k, 0, 0))],
        out_shape=[
            jax.ShapeDtypeStruct((tokens, width), FLOAT),
            jax.ShapeDtypeStruct((tokens, width), BFLOAT),
            jax.ShapeDtypeStruct((5, 1, width), FLOAT),
        ],
        scratch_shapes=[pltpu.VMEM((tokens, width), FLOAT)],
        compiler_params=ROOMY,
        cost_estimate=FREE,
    )(grad_first, pieces, packed)


def token_kernel(act_ref, mixed_ref, grad_ref, attended_ref, out_ref):
    @pl.when(pl.program_id(0) < 3)
    def _():
        out_ref[...] = contract_rows(act_ref[...], grad_ref[...]).astype(BFLOAT)

    @pl.when(pl.program_id(0) == 3)
    def _():
        out_ref[...] = contract_rows(mixed_ref[...], attended_ref[...]).astype(BFLOAT)


def token_gradients(act, mixed, pieces, grad_attended):
    tokens, width = act.shape
    whole = pl.BlockSpec((tokens, width), lambda k: (0, 0))
    return pl.pallas_call(
        token_kernel,
        grid=(4,),
        in_specs=[
            whole,
            whole,
            pl.BlockSpec((None, tokens, width), lambda k: (jnp.minimum(k, 2), 0, 0)),
            whole,
        ],
        out_specs=pl.BlockSpec((None, width, width), lambda k: (k, 0, 0)),
        out_shape=jax.ShapeDtypeStruct((4, width, width), BFLOAT),
        compiler_params=ROOMY,
        cost_estimate=FREE,
    )(act, mixed, pieces, grad_attended)


def box_kernel(features_ref, place_ref, grad_ref, grad_place_ref, out_ref):
    @pl.when(pl.program_id(0) < 2)
    def _():
        out_ref[...] = contract_rows(place_ref[...], grad_ref[...]).astype(BFLOAT)

    @pl.when(pl.program_id(0) == 2)
    def _():
        out_ref[...] = contract_rows(features_ref[...], grad_place_ref[...]).astype(BFLOAT)


def box_gradients(features_low, stack, pieces, grad_place):
    tokens, width = grad_place.shape
    whole = pl.BlockSpec((tokens, width), lambda k: (0, 0))
    return pl.pallas_call(
        box_kernel,
        grid=(3,),
        in_specs=[
            whole,
            pl.BlockSpec((None, tokens, width), lambda k: (0, 0, 0)),
            pl.BlockSpec((None, tokens, width), lambda k: (jnp.minimum(k, 1) + 3, 0, 0)),
            whole,
        ],
        out_specs=pl.BlockSpec((None, width, width), lambda k: (k, 0, 0)),
        out_shape=jax.ShapeDtypeStruct((3, width, width), BFLOAT),
        compiler_params=ROOMY,
        cost_estimate=FREE,
    )(features_low, stack, pieces, grad_place)


def project_kernel(features_ref, act_ref, mat_ref, bias_ref, out_ref, place):
    step = pl.program_id(0)

    @pl.when(step == 0)
    def _():
        low = (product(features_ref[...], mat_ref[...]) + bias_ref[...]).astype(BFLOAT)
        place[...] = low
        out_ref[...] = low

    @pl.when((step > 0) & (step < 3))
    def _():
        out_ref[...] = product(place[...], mat_ref[...]).astype(BFLOAT)

    @pl.when(step >= 3)
    def _():
        out_ref[...] = (product(act_ref[...], mat_ref[...]) + bias_ref[...]).astype(BFLOAT)


def projections(features_low, act, packed, first_mat, gains):
    tokens, width = act.shape
    whole = pl.BlockSpec((tokens, width), lambda k: (0, 0))
    none = jnp.zeros_like(gains[0])
    biases = jnp.stack([gains[9], none, none, gains[6], none, gains[7]])[:, None]

    def mat(k):
        return first_mat + jnp.where(k == 0, 0, jnp.where(k < 3, k + 3, k - 2))

    return pl.pallas_call(
        project_kernel,
        grid=(6,),
        in_specs=[
            whole,
            whole,
            pl.BlockSpec((None, width, width), lambda k: (mat(k), 0, 0)),
            pl.BlockSpec((None, 1, width), lambda k: (k, 0, 0)),
        ],
        out_specs=pl.BlockSpec((None, tokens, width), lambda k: (k, 0, 0)),
        out_shape=jax.ShapeDtypeStruct((6, tokens, width), BFLOAT),
        scratch_shapes=[pltpu.VMEM((tokens, width), BFLOAT)],
        compiler_params=ROOMY,
        cost_estimate=FREE,
    )(features_low, act, packed, biases)


class Buckets(NamedTuple):
    owner: jax.Array
    row: jax.Array
    first: jax.Array
    rank: jax.Array
    fullest: jax.Array


def bucket_ids(ids, shard_rows):
    owner, row = ids // shard_rows, ids % shard_rows
    index = jnp.arange(ids.shape[0], dtype=jnp.int32)
    earlier = index[None, :] < index[:, None]
    same = ids[:, None] == ids[None, :]
    first = ~jnp.any(same & earlier, axis=1)
    before = (owner[:, None] == owner[None, :]) & earlier & first[None, :]
    rank = jnp.sum(before.astype(jnp.int32), axis=1)
    rank = jnp.sum(jnp.where(same & first[None, :], rank[None, :], 0), axis=1)
    return Buckets(owner, row, first, rank, jnp.max(rank) + 1)


def bucket_places(buckets, capacity, stride, turn):
    shifted = buckets.rank - turn * capacity
    inside = (shifted >= 0) & (shifted < capacity)
    return jnp.where(inside, buckets.owner * stride + shifted, -1)


def bucket_requests(buckets, places, groups, stride):
    hit = (places[:, None] == jnp.arange(groups * stride)[None, :]) & buckets.first[:, None]
    rows = jnp.sum(jnp.where(hit, buckets.row[:, None] + 1, 0), axis=0) - 1
    return rows.reshape(groups, stride)


def one_hot(index, count):
    return (index[:, None] == jnp.arange(count, dtype=jnp.int32)[None, :]).astype(BFLOAT)


def feed_kernel(middle_ref, up_ref, bias_ref, down_ref, active_ref, slope_ref, out_ref):
    value = product(middle_ref[...], up_ref[...]) + bias_ref[...]
    share = 0.5 * (1.0 + lax.erf(value * math.sqrt(0.5)))
    density = jnp.exp(-0.5 * value * value) * (1.0 / math.sqrt(2.0 * math.pi))
    active = (value * share).astype(BFLOAT)
    active_ref[...] = active
    slope_ref[...] = share + value * density
    out = product(active, down_ref[...])

    @pl.when(pl.program_id(0) == 0)
    def _():
        out_ref[...] = out

    @pl.when(pl.program_id(0) > 0)
    def _():
        out_ref[...] += out


def feed_forward(middle_low, packed, bias):
    tokens, width = middle_low.shape
    hidden = bias.shape[0]
    blocks = hidden // width
    whole = pl.BlockSpec((tokens, width), lambda j: (0, 0))
    columns = pl.BlockSpec((tokens, width), lambda j: (0, j))
    return pl.pallas_call(
        feed_kernel,
        grid=(blocks,),
        in_specs=[
            whole,
            pl.BlockSpec((None, width, width), lambda j: (j, 0, 0)),
            pl.BlockSpec((1, width), lambda j: (0, j)),
            pl.BlockSpec((None, width, width), lambda j: (blocks + j, 0, 0)),
        ],
        out_specs=[columns, columns, whole],
        out_shape=[
            jax.ShapeDtypeStruct((tokens, hidden), BFLOAT),
            jax.ShapeDtypeStruct((tokens, hidden), FLOAT),
            jax.ShapeDtypeStruct((tokens, width), FLOAT),
        ],
        compiler_params=ROOMY,
        cost_estimate=FREE,
    )(middle_low, packed, bias[None], packed)


def feed_back_kernel(
    grad_ref,
    middle_ref,
    active_ref,
    slope_ref,
    up_ref,
    down_ref,
    grads_ref,
    grad_bias_ref,
    out_ref,
):
    grad = grad_ref[...]
    grad_upper = (times_transposed(grad, down_ref[...]) * slope_ref[...]).astype(BFLOAT)
    grad_bias_ref[...] = jnp.sum(grad_upper.astype(FLOAT), axis=0, keepdims=True)
    grads_ref[0] = contract_rows(middle_ref[...], grad_upper).astype(BFLOAT)
    grads_ref[1] = contract_rows(active_ref[...], grad).astype(BFLOAT)
    out = times_transposed(grad_upper, up_ref[...])

    @pl.when(pl.program_id(0) == 0)
    def _():
        out_ref[...] = out

    @pl.when(pl.program_id(0) > 0)
    def _():
        out_ref[...] += out


def feed_backward(grad_feed, middle_low, active, slope, packed):
    tokens, width = middle_low.shape
    hidden = active.shape[1]
    blocks = hidden // width
    whole = pl.BlockSpec((tokens, width), lambda j: (0, 0))
    columns = pl.BlockSpec((tokens, width), lambda j: (0, j))
    return pl.pallas_call(
        feed_back_kernel,
        grid=(blocks,),
        in_specs=[
            whole,
            whole,
            columns,
            columns,
            pl.BlockSpec((None, width, width), lambda j: (j, 0, 0)),
            pl.BlockSpec((None, width, width), lambda j: (blocks + j, 0, 0)),
        ],
        out_specs=[
            pl.BlockSpec((2, None, width, width), lambda j: (0, j, 0, 0)),
            pl.BlockSpec((1, width), lambda j: (0, j)),
            whole,
        ],
        out_shape=[
            jax.ShapeDtypeStruct((2, blocks, width, width), BFLOAT),
            jax.ShapeDtypeStruct((1, hidden), FLOAT),
            jax.ShapeDtypeStruct((tokens, width), FLOAT),
        ],
        compiler_params=ROOMY,
        cost_estimate=FREE,
    )(grad_feed, middle_low, active, slope, packed, packed)


def logits_kernel(rows_ref, table_ref, expo_ref, stats_ref):
    logits = times_transposed(rows_ref[...], table_ref[...])
    peak = jnp.max(logits, axis=1, keepdims=True)
    expo = jnp.exp(logits - peak)
    expo_ref[...] = expo.astype(BFLOAT)
    mass = jnp.sum(expo, axis=1, keepdims=True)
    lane = lax.broadcasted_iota(jnp.int32, (logits.shape[0], LANES), 1)
    stats_ref[...] = jnp.where(lane == 0, peak, mass).T[:8]


def head_logits(rows_all, table_low):
    count, width = rows_all.shape
    shard_rows = table_low.shape[0]
    step = min(512, count)
    return pl.pallas_call(
        logits_kernel,
        grid=(count // step,),
        in_specs=[
            pl.BlockSpec((step, width), lambda i: (i, 0)),
            pl.BlockSpec((shard_rows, width), lambda i: (0, 0)),
        ],
        out_specs=[
            pl.BlockSpec((step, shard_rows), lambda i: (i, 0)),
            pl.BlockSpec((8, step), lambda i: (0, i)),
        ],
        out_shape=[
            jax.ShapeDtypeStruct((count, shard_rows), BFLOAT),
            jax.ShapeDtypeStruct((8, count), FLOAT),
        ],
        compiler_params=ROOMY,
        cost_estimate=FREE,
    )(rows_all, table_low)


def column_sum(value):
    return jnp.sum(value.astype(FLOAT), axis=0)


def layer_forward(weights, embedded, features_low, lengths):
    mats, packed, gains, up_bias = weights
    start_state = layer_norm(embedded, gains[0], gains[1])
    act = start_state.astype(BFLOAT)
    stack = projections(features_low, act, packed, packed.shape[0] - mats.shape[0], gains)
    mixed = attention_call(attend_kernel, lengths, stack, (), 0)
    first_sum = start_state + (product(mixed, mats[6]) + gains[8])
    middle = layer_norm(first_sum, gains[2], gains[3])
    middle_low = middle.astype(BFLOAT)
    active, slope, feed = feed_forward(middle_low, packed, up_bias)
    second_sum = middle + (feed + gains[10])
    kept = (
        embedded,
        act,
        stack,
        mixed,
        first_sum,
        middle_low,
        slope,
        active,
        second_sum,
    )
    return (layer_norm(second_sum, gains[4], gains[5]), kept)


def layer_backward(weights, features_low, lengths, kept, grad_out, head_parts, lines, tools):
    mats, packed, gains, up_bias = weights
    (
        embedded,
        act,
        stack,
        mixed,
        first_sum,
        middle_low,
        slope,
        active,
        second_sum,
    ) = kept
    compacted, give, from_copies, give_rows = tools

    def send(value, name):
        own, blocks = sends(value, lines[name], AXES[name])
        return own, blocks

    def travel(pair, name, *until):
        line = lines[name]
        moved = [shifted(block, line, step) for step, block in enumerate(pair[1], 1)]
        if until:
            moved = list(after(tuple(moved), *until))
        total = pair[0].astype(FLOAT)
        for value in moved:
            total = total + value.astype(FLOAT)
        return total.astype(BFLOAT)

    grad_second, gain_four, gain_five = jax.vjp(layer_norm, second_sum, gains[4], gains[5])[1](
        grad_out
    )
    grad_feed = grad_second.astype(BFLOAT)
    grad_feeds, grad_bias, fed_back = feed_backward(grad_feed, middle_low, active, slope, packed)
    feeds_sum = lax.psum_scatter(grad_feeds, "fsdp", scatter_dimension=2, tiled=True)
    grad_first, gain_two, gain_three = jax.vjp(layer_norm, first_sum, gains[2], gains[3])[1](
        grad_second + fed_back
    )
    grad_attended = grad_first.astype(BFLOAT)
    grad_mixed = times_transposed(grad_attended, mats[6]).astype(BFLOAT)
    pieces = attention_call(
        attend_back_kernel, lengths, stack, (grad_mixed,), 5
    )
    pieces = after(pieces, head_parts[2])
    first_mat = packed.shape[0] - mats.shape[0]
    grad_start, grad_place, sums = start_gradient(grad_first, pieces, packed, first_mat)
    grad_start = after(grad_start, head_parts[3])
    grad_embedded, gain_zero, gain_one = jax.vjp(layer_norm, embedded, gains[0], gains[1])[1](
        grad_start
    )
    grad_vectors = jnp.stack(
        [
            gain_zero,
            gain_one,
            gain_two,
            gain_three,
            gain_four,
            gain_five,
            sums[2, 0],
            sums[4, 0],
            column_sum(grad_attended),
            sums[1, 0],
            column_sum(grad_feed),
        ]
    )
    parts = two_parts(grad_embedded)
    compact = compacted(parts, grad_vectors, grad_bias)
    returned = give(compact)
    pieces = after(pieces, compact)
    token_part = token_gradients(act, mixed, pieces, grad_attended)
    token_core = send(by_owner(token_part, lines), "core")
    pieces = after(pieces, *token_core[1])
    box_part = box_gradients(features_low, stack, pieces, grad_place)
    token_y = send(travel(token_core, "core", box_part), "y")
    box_part = after(box_part, *token_y[1])
    box_core = send(by_owner(box_part, lines), "core")
    box_x = send(travel(box_core, "core"), "x")
    returned = after(returned, *box_x[1])
    rows = from_copies(returned)
    feeds_sum = after(feeds_sum, returned)
    others = after(tuple(rows[1:]), feeds_sum)
    token_z = send(travel(token_y, "y", feeds_sum), "z")
    box_y = send(travel(box_x, "x", token_z[1][0]), "y")
    spread = [give_rows(0, after(rows[0], *box_y[1]))]
    box_z = send(travel(box_y, "y", spread[0]), "z")
    others = after(others, *box_z[1])
    spread += [give_rows(index, value) for index, value in enumerate(others, 1)]
    token_sum = travel(token_z, "z", spread[-1])[:, 0, 0, 0]
    box_half = travel(box_z, "z", token_sum)[:, 0, 0, 0]
    feeds_other = after(from_other_copies(feeds_sum, lines), box_half)
    feeds_sum = feeds_sum.astype(FLOAT) + feeds_other.astype(FLOAT)
    token_mats = both_copies(token_sum, lines)
    box_mats = gather_line(box_half, lines["x"], 2).astype(FLOAT)
    grad_mats = jnp.concatenate([box_mats[2:], token_mats[:3], box_mats[:2], token_mats[3:]])
    return ((grad_mats, feeds_sum), spread, [rows[0], *others], parts)


def combine_mass(first, second):
    peak = jnp.maximum(first[0], second[0])
    mass = first[1] * jnp.exp(first[0] - peak) + second[1] * jnp.exp(second[0] - peak)
    return jnp.stack([peak, mass])


def body(
    token_ids,
    boxes,
    lengths,
    slots,
    labels,
    table,
    mats,
    up,
    down,
    vectors,
    up_bias,
    table_rows,
    table_cols,
    mats_rows,
    mats_cols,
    up_rows,
    up_cols,
    down_rows,
    down_cols,
    vectors_second,
    up_bias_second,
):
    pages = lengths.shape[0]
    tokens = token_ids.shape[0]
    page_len = tokens // pages
    width = table.shape[1]
    shard_rows = table.shape[0]
    slot_count = slots.shape[1]
    groups, copies = lax.axis_size("fsdp"), lax.axis_size("rep")
    group, copy = lax.axis_index("fsdp"), lax.axis_index("rep")
    lines = lines_of(groups, copies)
    table_low = table.astype(BFLOAT)

    own_small = vectors.size + up_bias.size
    small_rows = -(-own_small // width)
    stride = 16 + -(-tokens // (16 * groups)) * 16
    capacity = stride - 2 * small_rows
    buckets = bucket_ids(token_ids, shard_rows)
    places = bucket_places(buckets, capacity, stride, 0)
    requests = bucket_requests(buckets, places, groups, stride)
    own_news = jnp.concatenate([labels.reshape(-1), lengths, buckets.fullest[None]])
    news = jnp.concatenate(
        [
            jnp.repeat(requests, copies, axis=0),
            jnp.broadcast_to(own_news[None], (groups * copies, own_news.shape[0])),
        ],
        axis=1,
    )
    news = lax.all_to_all(news, ("fsdp", "rep"), 0, 0, tiled=True)
    asked = news[:, :stride].reshape(groups, copies, stride)
    asked = jnp.transpose(asked, (1, 0, 2)).reshape(copies, groups * stride)
    labels_all = news[:, stride : stride + pages * slot_count]
    labels_all = labels_all.reshape(groups, copies, pages * slot_count)
    labels_all = lax.dynamic_index_in_dim(labels_all, copy, 1, False).reshape(-1)
    lengths_all = news[:, stride + pages * slot_count : -1]
    turns = (jnp.max(news[:, -1]) + capacity - 1) // capacity

    def fetch(spots, wanted):
        rows = product(one_hot(wanted, shard_rows), table_low).astype(BFLOAT)
        rows = lax.all_to_all(rows.reshape(groups, stride, width), "fsdp", 0, 0, tiled=True)
        return product(one_hot(spots, groups * stride), rows.reshape(groups * stride, width))

    def ask(turn):
        spots = bucket_places(buckets, capacity, stride, turn)
        wanted = bucket_requests(buckets, spots, groups, stride)
        return spots, lax.all_to_all(wanted, "fsdp", 0, 0, tiled=True).reshape(-1)

    embedded = fetch(places, lax.dynamic_index_in_dim(asked, copy, 0, False))
    embedded = lax.while_loop(
        lambda state: state[0] < turns,
        lambda state: (state[0] + 1, state[1] + fetch(*ask(state[0]))),
        (jnp.int32(1), embedded),
    )[1]

    own_labels = labels_all - group * shard_rows
    label_rows = product(one_hot(own_labels, shard_rows), table_low).astype(BFLOAT)
    embedded = after(embedded, label_rows)

    depth = mats.shape[0]
    items = depth + 3
    lane = jnp.arange(width)
    singles = jnp.pad(jnp.sum(mats_rows, axis=1), (1, width - 1 - depth))
    for index, value in (
        (0, jnp.sum(table_rows)),
        (items - 2, jnp.sum(up_rows)),
        (items - 1, jnp.sum(down_rows)),
    ):
        singles = jnp.where(lane == index, value, singles)
    embedded = after(embedded, singles)

    small = jnp.concatenate([vectors.astype(BFLOAT).reshape(-1), up_bias.astype(BFLOAT)])[None]

    def lay(first, second, bit):
        low = (group & bit) == 0
        return jnp.concatenate([jnp.where(low, first, second), jnp.where(low, second, first)])

    bit = 1
    while bit < groups:
        pairs = [(i, i ^ bit) for i in range(groups)]
        small = lay(small, lax.ppermute(small, "fsdp", pairs), bit)
        bit *= 2
    split = vectors.size
    gains = small[:, :split].reshape(groups, vectors.shape[0], -1)
    gains = jnp.transpose(gains, (1, 0, 2)).reshape(vectors.shape[0], width).astype(FLOAT)
    own_rows, hidden = up.shape
    feed_blocks = hidden // width
    bias = small[:, split:].reshape(groups, feed_blocks, own_rows)
    bias = jnp.transpose(bias, (1, 0, 2)).reshape(-1).astype(FLOAT)
    gains, bias = lax.optimization_barrier((gains, bias))
    up_blocks = up.astype(BFLOAT).reshape(own_rows, groups, feed_blocks, own_rows)
    up_blocks = jnp.transpose(up_blocks, (2, 0, 1, 3)).reshape(feed_blocks, own_rows, width)
    down_blocks = down.astype(BFLOAT).reshape(feed_blocks, own_rows, width)
    packed = jnp.concatenate([up_blocks, down_blocks, mats.astype(BFLOAT)])
    packed = lax.all_gather(packed, "fsdp", axis=1, tiled=True)
    layer_mats = packed[2 * feed_blocks :]
    weights = (layer_mats, packed, gains, bias)

    features_low = box_features(boxes, width).astype(BFLOAT)
    top_state, kept = layer_forward(weights, embedded, features_low, lengths)

    where_at = slots * lengths[:, None] // 256 + jnp.arange(pages)[:, None] * page_len
    pick = one_hot(where_at.reshape(-1), tokens)
    rows_low = product(pick, top_state.astype(BFLOAT)).astype(BFLOAT)
    rows_all = rows_low[None, None, None]
    for axis, name in enumerate(("z", "y", "core")):
        rows_all = gather_line(rows_all, lines[name], axis)
    rows_all = rows_all.reshape(-1, width)
    expo, stats = head_logits(rows_all, table_low)
    peak_here = stats[0]
    products = product(expo, table_low)
    stats = paired(stats[:2].reshape(2, -1, LANES), "fsdp", combine_mass, products).reshape(2, -1)
    products, peak, mass = lax.optimization_barrier((products, *stats))
    log_total = peak + jnp.log(mass)
    factor = jnp.exp(peak_here - log_total)

    is_token = jnp.arange(slot_count) < M_TOK
    valid_all = valid_slots(lengths_all.reshape(-1), slot_count).astype(FLOAT)
    count_token = jnp.sum(jnp.where(is_token, valid_all, 0.0))
    count_area = jnp.sum(jnp.where(is_token, 0.0, valid_all))
    figure = jnp.arange(4)
    counts = jnp.where(figure == 1, count_token, jnp.where(figure == 3, count_area, 0.0))
    count_token, count_area, counts = lax.optimization_barrier((count_token, count_area, counts))
    valid = valid_all.reshape(groups, copies, pages, slot_count)
    valid = lax.dynamic_index_in_dim(valid, copy, 1, False).reshape(-1, slot_count)
    share = jnp.where(is_token, 1.0 / count_token, 1.0 / count_area)
    weight = (valid * share[None, :]).reshape(-1)
    grad_rows = (products * factor[:, None] - label_rows.astype(FLOAT)) * weight[:, None]
    grad_rows = grad_rows.astype(BFLOAT)
    grad_rows = grad_rows.reshape(
        lines["z"].count, lines["y"].count, lines["core"].count, -1, width
    )
    own, blocks = sends(grad_rows, lines["core"], 2)
    weighted = (rows_all.astype(FLOAT) * weight[:, None]).astype(BFLOAT)
    expo, weighted = after((expo, weighted), *blocks)
    mine = own_labels[:, None] == jnp.arange(shard_rows)[None, :]
    grad_logits = expo.astype(FLOAT) * factor[:, None] - mine.astype(FLOAT)
    own, blocks = sends(received(own, blocks, lines["core"]), lines["y"], 1)
    grad_logits = after(grad_logits.astype(BFLOAT), *blocks)
    head_low = contract_rows(grad_logits, weighted).astype(BFLOAT)
    totals = lax.dynamic_slice_in_dim(log_total * valid.reshape(-1), group * pages * slot_count, pages * slot_count)
    targets = jnp.sum(after(rows_all, *blocks).astype(FLOAT) * label_rows.astype(FLOAT), axis=1)
    losses = jnp.sum(totals.reshape(-1, slot_count), axis=0)
    losses = losses - jnp.sum(targets.reshape(-1, slot_count) * valid, axis=0)
    token_loss = jnp.sum(jnp.where(is_token, losses, 0.0))
    area_loss = jnp.sum(jnp.where(is_token, 0.0, losses))
    singles = jnp.where(lane == items + 1, token_loss, jnp.where(lane == items + 3, area_loss, singles))
    own, blocks = sends(received(own, blocks, lines["y"]), lines["z"], 0)
    blocks = list(after(tuple(blocks), head_low, singles))
    grad_rows = received(own, blocks, lines["z"]).reshape(-1, width)
    fifth = shard_rows // 5
    cuts = [fifth, 2 * fifth, shard_rows - (shard_rows - 2 * fifth) // 2]
    head_parts = [from_other_copies(part, lines) for part in jnp.split(head_low, cuts)]
    grad_rows = after(grad_rows, *head_parts[:2])
    grad_top = sum(contract_rows(pick, part) for part in two_parts(grad_rows))

    def compacted(spots, parts):
        spread = one_hot(spots, groups * stride)
        return sum(contract_rows(spread, part) for part in parts)

    def compacted_first(parts, grad_vectors, grad_bias):
        small = grad_vectors.reshape(grad_vectors.shape[0], groups, -1)
        small = jnp.transpose(small, (1, 0, 2)).reshape(groups, -1)
        grad_bias = jnp.transpose(grad_bias.reshape(feed_blocks, groups, own_rows), (1, 0, 2))
        small = jnp.concatenate([small, grad_bias.reshape(groups, -1)], axis=1)
        small = jnp.pad(small, ((0, 0), (0, small_rows * width - own_small)))
        small = jnp.stack(two_parts(small.reshape(groups, small_rows, width)), axis=1)
        small = small.reshape(groups, 2 * small_rows, width).astype(FLOAT)
        small = jnp.pad(small, ((0, 0), (capacity, 0), (0, 0))).reshape(groups * stride, width)
        return (compacted(places, parts) + small).astype(BFLOAT)

    def give(rows):
        rows = lax.all_to_all(rows.reshape(groups, stride, width), "fsdp", 0, 0, tiled=True)
        return rows.reshape(groups * stride, width)

    def spread_rows(wanted, rows):
        return contract_rows(one_hot(wanted, shard_rows), rows)

    def small_sum(rows):
        rows = rows.reshape(groups, stride, width)[:, capacity:].astype(FLOAT)
        rows = jnp.sum(rows, axis=0).reshape(2, small_rows * width)
        return (rows[0] + rows[1])[:own_small]

    if copies == 2:
        from_copies = lambda value: [value, shifted(value, lines["x"], 1)]
        copy_order = [copy, 1 - copy]
    else:
        from_copies = lambda value: list(lax.all_gather(value, "rep"))
        copy_order = list(range(copies))
    asked_of = [lax.dynamic_index_in_dim(asked, index, 0, False) for index in copy_order]

    def give_rows(index, rows):
        return spread_rows(asked_of[index], rows)

    tools = (compacted_first, give, from_copies, give_rows)
    layer_grads, spread, given, embedded_parts = layer_backward(
        weights, features_low, lengths, kept, grad_top, head_parts, lines, tools
    )
    mats_grad, feeds_grad = layer_grads
    up_grad = jnp.transpose(feeds_grad[0].reshape(feed_blocks, own_rows, groups, own_rows), (1, 2, 0, 3))
    up_grad = up_grad.reshape(own_rows, hidden)
    down_grad = feeds_grad[1].reshape(hidden // groups, width)
    small = [small_sum(rows) for rows in given]
    small = sum(small[1:], small[0])
    vectors_grad = small[: vectors.size].reshape(vectors.shape)
    bias_grad = small[vectors.size :]

    head_grad = head_low.astype(FLOAT) + jnp.concatenate(head_parts).astype(FLOAT)
    table_grad = head_grad + sum(spread[1:], spread[0])

    def another(state):
        turn, total = state
        spots, wanted = ask(turn)
        given = from_copies(give(compacted(spots, embedded_parts).astype(BFLOAT)))
        spread = [spread_rows(*pair) for pair in zip(from_copies(wanted), given)]
        return turn + 1, total + sum(spread[1:], spread[0])

    table_grad = lax.while_loop(lambda state: state[0] < turns, another, (jnp.int32(1), table_grad))[1]

    feed_cols = hidden // width
    sizes = [(shard_rows * groups, width)] + [(mats.shape[1] * groups, width)] * depth
    sizes += [(up.shape[0] * groups, hidden), (down.shape[0] * groups, width)]
    row_squares = [jnp.sum(grad * grad, axis=-1) for grad in (table_grad, mats_grad, up_grad, down_grad)]
    singles = jnp.where(lane == items, jnp.sum(small * small), singles)
    sums = jnp.concatenate(
        [
            jnp.sum(table_grad * table_grad, axis=0)[None],
            jnp.sum(mats_grad * mats_grad, axis=1),
            jnp.sum(up_grad * up_grad, axis=0).reshape(feed_cols, width),
            jnp.sum(down_grad * down_grad, axis=0)[None],
            singles[None],
        ]
    )
    cols_old = jnp.concatenate(
        [table_cols[None], mats_cols, up_cols.reshape(feed_cols, width), down_cols[None]]
    )
    sums = paired(sums, "fsdp", jnp.add)
    loss_parts = counts + paired(sums[-1, items + 1 : items + 5], "rep", jnp.add)
    totals = jnp.sum(sums[:-1], axis=1)
    norm_square = jnp.sum(totals) + sums[-1, items]
    grad_norm = jnp.sqrt(norm_square)
    clip = jnp.minimum(1.0, CLIP_NORM / grad_norm)
    square = clip * clip

    def renewed(old, value):
        return DECAY * old + (1.0 - DECAY) * (value + TINY_TERM)

    first_up, after_up = 1 + depth, 1 + depth + feed_cols
    of_item = [[k] for k in range(first_up)] + [list(range(first_up, after_up)), [after_up]]
    item_totals = jnp.concatenate(
        [totals[:first_up], jnp.sum(totals[first_up:after_up])[None], totals[after_up:]]
    )
    tall = jnp.array([size[0] for size in sizes], FLOAT)
    wide = jnp.array([size[1] for size in sizes], FLOAT)
    means = renewed(sums[-1, :items] / tall, square * item_totals / (tall * wide))
    repeats = [len(rows) for rows in of_item]
    tall_rows = jnp.array([s for size, n in zip(sizes, repeats) for s in [size[0]] * n], FLOAT)
    mean_rows = jnp.concatenate(
        [means[:first_up], jnp.broadcast_to(means[first_up], (feed_cols,)), means[first_up + 1 :]]
    )
    cols_new = renewed(cols_old, square * sums[:-1] / tall_rows[:, None])
    col_factors = lax.rsqrt(cols_new / mean_rows[:, None])
    step = LEARN_RATE * clip

    def updated(grad, param, rows_old, row_square, col_factor):
        rows_new = renewed(rows_old, square * row_square / grad.shape[-1])
        factor = step * lax.rsqrt(rows_new)
        return grad * clip, rows_new, param - grad * factor[..., None] * col_factor[..., None, :]

    up_factor = col_factors[first_up:after_up].reshape(hidden)
    table_out = updated(table_grad, table, table_rows, row_squares[0], col_factors[0])
    mats_out = updated(mats_grad, mats, mats_rows, row_squares[1], col_factors[1:first_up])
    up_out = updated(up_grad, up, up_rows, row_squares[2], up_factor)
    down_out = updated(down_grad, down, down_rows, row_squares[3], col_factors[after_up])
    clipped_vectors = vectors_grad * clip
    vectors_second_new = DECAY * vectors_second + (1.0 - DECAY) * (
        clipped_vectors * clipped_vectors + TINY_TERM
    )
    vectors_new = vectors - VECTOR_RATE * clipped_vectors * lax.rsqrt(vectors_second_new)
    clipped_bias = bias_grad * clip
    bias_second_new = DECAY * up_bias_second + (1.0 - DECAY) * (
        clipped_bias * clipped_bias + TINY_TERM
    )
    bias_new = up_bias - VECTOR_RATE * clipped_bias * lax.rsqrt(bias_second_new)
    return (
        table_out[0],
        table_out[1],
        cols_new[0],
        table_out[2],
        mats_out[0],
        mats_out[1],
        cols_new[1:first_up],
        mats_out[2],
        up_out[0],
        up_out[1],
        cols_new[first_up:after_up].reshape(hidden),
        up_out[2],
        down_out[0],
        down_out[1],
        cols_new[after_up],
        down_out[2],
        clipped_vectors,
        vectors_second_new,
        vectors_new,
        clipped_bias,
        bias_second_new,
        bias_new,
        grad_norm,
        loss_parts,
    )


def solution(mesh):
    return jax.shard_map(
        body,
        mesh=mesh,
        in_specs=(
            P(("fsdp", "rep")),
            P(None, ("fsdp", "rep")),
            P(("fsdp", "rep")),
            P(("fsdp", "rep"), None),
            P(("fsdp", "rep"), None),
            P("fsdp", None),
            P(None, "fsdp", None),
            P("fsdp", None),
            P("fsdp", None),
            P(None, "fsdp"),
            P("fsdp"),
            P("fsdp"),
            P(),
            P(None, "fsdp"),
            P(),
            P("fsdp"),
            P(),
            P("fsdp"),
            P(),
            P(None, "fsdp"),
            P("fsdp"),
        ),
        out_specs=(
            P("fsdp", None),
            P("fsdp"),
            P(),
            P("fsdp", None),
            P(None, "fsdp", None),
            P(None, "fsdp"),
            P(),
            P(None, "fsdp", None),
            P("fsdp", None),
            P("fsdp"),
            P(),
            P("fsdp", None),
            P("fsdp", None),
            P("fsdp"),
            P(),
            P("fsdp", None),
            P(None, "fsdp"),
            P(None, "fsdp"),
            P(None, "fsdp"),
            P("fsdp"),
            P("fsdp"),
            P("fsdp"),
            P(),
            P(),
        ),
        check_vma=False,
    )
```

```python
import math
from typing import NamedTuple

import jax
import jax.numpy as jnp
from jax import lax
from jax.experimental import pallas as pl
from jax.experimental.pallas import tpu as pltpu
from jax.sharding import PartitionSpec as P

HEAD_DIM = 64
PAGE_LEN = 512
M_TOK = 64
M_AREA = 64
STEP = 10


EPSILON = 1e-05
CLIP_NORM = 0.1
LEARN_RATE = 0.02
VECTOR_RATE = 0.3
TINY_TERM = 1e-30
NEGATIVE = -1e30
BFLOAT = jnp.bfloat16
FLOAT = jnp.float32
LANES = 128
DECAY = 1.0 - STEP ** (-0.8)


class Line(NamedTuple):
    axis: str
    total: int
    stride: int
    count: int


def lines_of(groups, copies):
    cores = min(2, groups)
    rest = (groups // cores).bit_length() - 1
    y_count = 1 << (rest // 2)
    z_count = groups // (cores * y_count)
    return {
        "z": Line("fsdp", groups, cores * y_count, z_count),
        "y": Line("fsdp", groups, cores, y_count),
        "core": Line("fsdp", groups, 1, cores),
        "x": Line("rep", copies, 1, copies),
    }


def place_on(line):
    return lax.axis_index(line.axis) // line.stride % line.count


def shifted(value, line, step):
    pairs = []
    for i in range(line.total):
        place = i // line.stride % line.count
        pairs.append((i, i + ((place + step) % line.count - place) * line.stride))
    return lax.ppermute(value, line.axis, pairs)


def gather_line(value, line, axis):
    count = line.count
    if count == 1:
        return value
    here = place_on(line)
    pieces = [value] + [shifted(value, line, step) for step in range(1, count)]
    blocks = []
    for place in range(count):
        blocks.append(lax.select_n(here, *[pieces[(i - place) % count] for i in range(count)]))
    return jnp.concatenate(blocks, axis=axis)


def sends(value, line, axis):
    size = value.shape[axis] // line.count
    here = place_on(line)

    def block(place):
        return lax.dynamic_slice_in_dim(value, place * size, size, axis)

    return block(here), [
        block((here + step) % line.count).astype(BFLOAT) for step in range(1, line.count)
    ]


def received(own, blocks, line):
    total = own.astype(FLOAT)
    for step, value in enumerate(blocks, 1):
        total = total + shifted(value, line, step).astype(FLOAT)
    return total


def reduce_line(value, line, axis):
    return received(*sends(value, line, axis), line)


def after(value, *others):
    return lax.optimization_barrier((value, *others))[0]


def paired(value, axis, combine, beside=None):
    size = lax.axis_size(axis)
    bit = 1
    while bit < size:
        pairs = [(i, i ^ bit) for i in range(size)]
        other = lax.ppermute(value, axis, pairs)
        if beside is not None and bit == 2:
            other = after(other, beside)
        value = combine(value, other)
        bit *= 2
    return value


def by_owner(value, lines):
    count, _, columns = value.shape
    return value.reshape(count, lines["z"].count, lines["y"].count, lines["core"].count, -1, columns)


AXES = {"z": 1, "y": 2, "core": 3, "x": 5}


def part_sends(value, lines, name):
    return sends(value, lines[name], AXES[name])


def part_received(pair, lines, name):
    return received(*pair, lines[name]).astype(BFLOAT)


def both_copies(value, lines):
    if lines["x"].count == 2:
        return value.astype(FLOAT) + shifted(value, lines["x"], 1).astype(FLOAT)
    return lax.psum(value, "rep").astype(FLOAT)


def from_other_copies(value, lines):
    if lines["x"].count == 2:
        return shifted(value, lines["x"], 1)
    return (lax.psum(value, "rep").astype(FLOAT) - value.astype(FLOAT)).astype(BFLOAT)


def layer_norm(value, gain, shift):
    center = value - jnp.mean(value, axis=-1, keepdims=True)
    spread = jnp.mean(center * center, axis=-1, keepdims=True)
    return center * lax.rsqrt(spread + EPSILON) * gain + shift


def box_features(boxes, width):
    count = width // 8
    freqs = jnp.exp(-math.log(10000.0) * jnp.arange(count, dtype=FLOAT) / count)
    angle = boxes.astype(FLOAT)[:, :, None] * freqs[None, None, :]
    waves = jnp.concatenate([jnp.sin(angle), jnp.cos(angle)], axis=2)
    return jnp.transpose(waves, (1, 0, 2)).reshape(boxes.shape[1], width)


def valid_slots(lengths, slot_count):
    n_tok = jnp.minimum(M_TOK, 1 + lengths * M_TOK // PAGE_LEN)
    n_area = jnp.minimum(M_AREA, 1 + lengths * (3 * M_AREA) // (4 * PAGE_LEN))
    index = jnp.arange(slot_count, dtype=jnp.int32)[None, :]
    return jnp.where(index < M_TOK, index < n_tok[:, None], index - M_TOK < n_area[:, None])


def product(left, right):
    return jnp.dot(left, right, preferred_element_type=FLOAT)


def contract_rows(left, right):
    return lax.dot_general(left, right, (((0,), (0,)), ((), ())), preferred_element_type=FLOAT)


def times_transposed(left, right):
    return lax.dot_general(left, right, (((1,), (1,)), ((), ())), preferred_element_type=FLOAT)


def two_parts(value):
    high = value.astype(BFLOAT)
    return high, (value - high.astype(FLOAT)).astype(BFLOAT)


def side(index):
    lane = lax.broadcasted_iota(jnp.int32, (1, LANES), 1)
    return lane // HEAD_DIM == index


def only(mask, value):
    return jnp.where(mask, value, jnp.zeros_like(value))


def attend_kernel(length_ref, stack_ref, out_ref):
    length = length_ref[pl.program_id(0)]
    box_query, box_key, query, key, value = (stack_ref[index] for index in range(1, 6))
    keys = jnp.concatenate([key, box_key, key], axis=1)
    keep = lax.broadcasted_iota(jnp.int32, (1, key.shape[0]), 1) < length
    scale = jnp.asarray(HEAD_DIM ** (-0.5), BFLOAT)
    mixed = jnp.zeros(out_ref.shape, FLOAT)
    for head in range(LANES // HEAD_DIM):
        mask = side(head)
        own = only(mask, query) * scale
        other = only(mask, box_query) * scale
        score = times_transposed(jnp.concatenate([own, own, other], axis=1), keys)
        score = jnp.where(keep, score, NEGATIVE)
        expo = jnp.exp(score - jnp.max(score, axis=1, keepdims=True))
        prob = (expo * (1.0 / jnp.sum(expo, axis=1, keepdims=True))).astype(BFLOAT)
        mixed = jnp.where(mask, product(prob, value), mixed)
    out_ref[...] = mixed.astype(BFLOAT)


def attend_back_kernel(length_ref, stack_ref, grad_ref, out_ref):
    length = length_ref[pl.program_id(0)]
    box_query, box_key, query, key, value = (stack_ref[index] for index in range(1, 6))
    grad = grad_ref[...]
    rows = key.shape[0]
    keys = jnp.concatenate([key, box_key, key], axis=1)
    both_queries = jnp.concatenate([query, box_query], axis=1)
    both_keys = jnp.concatenate([key, box_key], axis=1)
    keep = lax.broadcasted_iota(jnp.int32, (rows, 1), 0) < length
    scale = jnp.asarray(HEAD_DIM ** (-0.5), BFLOAT)
    outs = [jnp.zeros((rows, LANES), FLOAT) for _ in range(5)]
    for head in range(LANES // HEAD_DIM):
        mask = side(head)
        own = only(mask, query) * scale
        other = only(mask, box_query) * scale
        score = times_transposed(keys, jnp.concatenate([own, own, other], axis=1))
        score = jnp.where(keep, score, NEGATIVE)
        expo = jnp.exp(score - jnp.max(score, axis=0, keepdims=True))
        prob = expo * (1.0 / jnp.sum(expo, axis=0, keepdims=True))
        grad_value = product(prob.astype(BFLOAT), grad)
        grad_prob = times_transposed(only(mask, value), grad)
        grad_score = prob * (grad_prob - jnp.sum(prob * grad_prob, axis=0, keepdims=True))
        low = grad_score.astype(BFLOAT) * scale
        with_queries = product(low, both_queries)
        with_keys = contract_rows(low, both_keys)
        fresh = (
            with_keys[:, :LANES] + with_keys[:, LANES:],
            with_queries[:, :LANES] + with_queries[:, LANES:],
            grad_value,
            with_keys[:, :LANES],
            with_queries[:, :LANES],
        )
        outs = [jnp.where(mask, new, old) for new, old in zip(fresh, outs)]
    for index, out in enumerate(outs):
        out_ref[index] = out.astype(BFLOAT)


FREE = pl.CostEstimate(flops=0, transcendentals=0, bytes_accessed=0)


ROOMY = pltpu.CompilerParams(vmem_limit_bytes=36 * 1024 * 1024)


def attention_call(kernel, lengths, stack, arrays, stacked):
    count, tokens, width = stack.shape
    pages = lengths.shape[0]
    spec = pl.BlockSpec((tokens // pages, LANES), lambda page, pair: (page, pair))

    def stack_spec(count):
        return pl.BlockSpec((count, tokens // pages, LANES), lambda page, pair: (0, page, pair))

    shape = (stacked, tokens, width) if stacked else (tokens, width)
    return pl.pallas_call(
        kernel,
        grid=(pages, width // LANES),
        in_specs=[pl.BlockSpec(memory_space=pltpu.SMEM), stack_spec(count)] + [spec] * len(arrays),
        out_specs=stack_spec(stacked) if stacked else spec,
        out_shape=jax.ShapeDtypeStruct(shape, BFLOAT),
        compiler_params=ROOMY,
        cost_estimate=FREE,
    )(lengths, stack, *arrays)


def start_kernel(first_ref, grad_ref, mat_ref, out_ref, place_ref, sums_ref, total):
    step = pl.program_id(0)
    grad = grad_ref[...]
    term = times_transposed(grad, mat_ref[...])
    sums_ref[...] = jnp.sum(grad.astype(FLOAT), axis=0, keepdims=True)

    @pl.when(step == 0)
    def _():
        total[...] = term

    @pl.when(step == 1)
    def _():
        low = (total[...] + term).astype(BFLOAT)
        place_ref[...] = low
        sums_ref[...] = jnp.sum(low.astype(FLOAT), axis=0, keepdims=True)

    @pl.when(step == 2)
    def _():
        out_ref[...] = first_ref[...] + term

    @pl.when(step > 2)
    def _():
        out_ref[...] += term


def start_gradient(grad_first, pieces, packed, first_mat):
    tokens, width = grad_first.shape
    whole = pl.BlockSpec((tokens, width), lambda k: (0, 0))

    def piece(k):
        return jnp.where(k < 2, k + 3, k - 2)

    def mat(k):
        return first_mat + jnp.where(k < 2, k + 4, k - 1)

    return pl.pallas_call(
        start_kernel,
        grid=(5,),
        in_specs=[
            whole,
            pl.BlockSpec((None, tokens, width), lambda k: (piece(k), 0, 0)),
            pl.BlockSpec((None, width, width), lambda k: (mat(k), 0, 0)),
        ],
        out_specs=[whole, whole, pl.BlockSpec((None, 1, width), lambda k: (k, 0, 0))],
        out_shape=[
            jax.ShapeDtypeStruct((tokens, width), FLOAT),
            jax.ShapeDtypeStruct((tokens, width), BFLOAT),
            jax.ShapeDtypeStruct((5, 1, width), FLOAT),
        ],
        scratch_shapes=[pltpu.VMEM((tokens, width), FLOAT)],
        compiler_params=ROOMY,
        cost_estimate=FREE,
    )(grad_first, pieces, packed)


def token_kernel(act_ref, mixed_ref, grad_ref, attended_ref, out_ref):
    @pl.when(pl.program_id(0) < 3)
    def _():
        out_ref[...] = contract_rows(act_ref[...], grad_ref[...]).astype(BFLOAT)

    @pl.when(pl.program_id(0) == 3)
    def _():
        out_ref[...] = contract_rows(mixed_ref[...], attended_ref[...]).astype(BFLOAT)


def token_gradients(act, mixed, pieces, grad_attended):
    tokens, width = act.shape
    whole = pl.BlockSpec((tokens, width), lambda k: (0, 0))
    return pl.pallas_call(
        token_kernel,
        grid=(4,),
        in_specs=[
            whole,
            whole,
            pl.BlockSpec((None, tokens, width), lambda k: (jnp.minimum(k, 2), 0, 0)),
            whole,
        ],
        out_specs=pl.BlockSpec((None, width, width), lambda k: (k, 0, 0)),
        out_shape=jax.ShapeDtypeStruct((4, width, width), BFLOAT),
        compiler_params=ROOMY,
        cost_estimate=FREE,
    )(act, mixed, pieces, grad_attended)


def box_kernel(features_ref, place_ref, grad_ref, grad_place_ref, out_ref):
    @pl.when(pl.program_id(0) < 2)
    def _():
        out_ref[...] = contract_rows(place_ref[...], grad_ref[...]).astype(BFLOAT)

    @pl.when(pl.program_id(0) == 2)
    def _():
        out_ref[...] = contract_rows(features_ref[...], grad_place_ref[...]).astype(BFLOAT)


def box_gradients(features_low, stack, pieces, grad_place):
    tokens, width = grad_place.shape
    whole = pl.BlockSpec((tokens, width), lambda k: (0, 0))
    return pl.pallas_call(
        box_kernel,
        grid=(3,),
        in_specs=[
            whole,
            pl.BlockSpec((None, tokens, width), lambda k: (0, 0, 0)),
            pl.BlockSpec((None, tokens, width), lambda k: (jnp.minimum(k, 1) + 3, 0, 0)),
            whole,
        ],
        out_specs=pl.BlockSpec((None, width, width), lambda k: (k, 0, 0)),
        out_shape=jax.ShapeDtypeStruct((3, width, width), BFLOAT),
        compiler_params=ROOMY,
        cost_estimate=FREE,
    )(features_low, stack, pieces, grad_place)


def project_kernel(features_ref, act_ref, mat_ref, bias_ref, out_ref, place):
    step = pl.program_id(0)

    @pl.when(step == 0)
    def _():
        low = (product(features_ref[...], mat_ref[...]) + bias_ref[...]).astype(BFLOAT)
        place[...] = low
        out_ref[...] = low

    @pl.when((step > 0) & (step < 3))
    def _():
        out_ref[...] = product(place[...], mat_ref[...]).astype(BFLOAT)

    @pl.when(step >= 3)
    def _():
        out_ref[...] = (product(act_ref[...], mat_ref[...]) + bias_ref[...]).astype(BFLOAT)


def projections(features_low, act, packed, first_mat, gains):
    tokens, width = act.shape
    whole = pl.BlockSpec((tokens, width), lambda k: (0, 0))
    none = jnp.zeros_like(gains[0])
    biases = jnp.stack([gains[9], none, none, gains[6], none, gains[7]])[:, None]

    def mat(k):
        return first_mat + jnp.where(k == 0, 0, jnp.where(k < 3, k + 3, k - 2))

    return pl.pallas_call(
        project_kernel,
        grid=(6,),
        in_specs=[
            whole,
            whole,
            pl.BlockSpec((None, width, width), lambda k: (mat(k), 0, 0)),
            pl.BlockSpec((None, 1, width), lambda k: (k, 0, 0)),
        ],
        out_specs=pl.BlockSpec((None, tokens, width), lambda k: (k, 0, 0)),
        out_shape=jax.ShapeDtypeStruct((6, tokens, width), BFLOAT),
        scratch_shapes=[pltpu.VMEM((tokens, width), BFLOAT)],
        compiler_params=ROOMY,
        cost_estimate=FREE,
    )(features_low, act, packed, biases)


class Buckets(NamedTuple):
    owner: jax.Array
    row: jax.Array
    first: jax.Array
    rank: jax.Array
    fullest: jax.Array


def bucket_ids(ids, shard_rows):
    owner, row = ids // shard_rows, ids % shard_rows
    index = jnp.arange(ids.shape[0], dtype=jnp.int32)
    earlier = index[None, :] < index[:, None]
    same = ids[:, None] == ids[None, :]
    first = ~jnp.any(same & earlier, axis=1)
    before = (owner[:, None] == owner[None, :]) & earlier & first[None, :]
    rank = jnp.sum(before.astype(jnp.int32), axis=1)
    rank = jnp.sum(jnp.where(same & first[None, :], rank[None, :], 0), axis=1)
    return Buckets(owner, row, first, rank, jnp.max(rank) + 1)


def bucket_places(buckets, capacity, stride, turn):
    shifted = buckets.rank - turn * capacity
    inside = (shifted >= 0) & (shifted < capacity)
    return jnp.where(inside, buckets.owner * stride + shifted, -1)


def bucket_requests(buckets, places, groups, stride):
    hit = (places[:, None] == jnp.arange(groups * stride)[None, :]) & buckets.first[:, None]
    rows = jnp.sum(jnp.where(hit, buckets.row[:, None] + 1, 0), axis=0) - 1
    return rows.reshape(groups, stride)


def one_hot(index, count):
    return (index[:, None] == jnp.arange(count, dtype=jnp.int32)[None, :]).astype(BFLOAT)


def feed_kernel(middle_ref, up_ref, bias_ref, down_ref, active_ref, slope_ref, out_ref):
    value = product(middle_ref[...], up_ref[...]) + bias_ref[...]
    share = 0.5 * (1.0 + lax.erf(value * math.sqrt(0.5)))
    density = jnp.exp(-0.5 * value * value) * (1.0 / math.sqrt(2.0 * math.pi))
    active = (value * share).astype(BFLOAT)
    active_ref[...] = active
    slope_ref[...] = share + value * density
    out = product(active, down_ref[...])

    @pl.when(pl.program_id(0) == 0)
    def _():
        out_ref[...] = out

    @pl.when(pl.program_id(0) > 0)
    def _():
        out_ref[...] += out


def feed_forward(middle_low, packed, bias):
    tokens, width = middle_low.shape
    hidden = bias.shape[0]
    blocks = hidden // width
    whole = pl.BlockSpec((tokens, width), lambda j: (0, 0))
    columns = pl.BlockSpec((tokens, width), lambda j: (0, j))
    return pl.pallas_call(
        feed_kernel,
        grid=(blocks,),
        in_specs=[
            whole,
            pl.BlockSpec((None, width, width), lambda j: (j, 0, 0)),
            pl.BlockSpec((1, width), lambda j: (0, j)),
            pl.BlockSpec((None, width, width), lambda j: (blocks + j, 0, 0)),
        ],
        out_specs=[columns, columns, whole],
        out_shape=[
            jax.ShapeDtypeStruct((tokens, hidden), BFLOAT),
            jax.ShapeDtypeStruct((tokens, hidden), FLOAT),
            jax.ShapeDtypeStruct((tokens, width), FLOAT),
        ],
        compiler_params=ROOMY,
        cost_estimate=FREE,
    )(middle_low, packed, bias[None], packed)


def feed_back_kernel(
    grad_ref,
    middle_ref,
    active_ref,
    slope_ref,
    up_ref,
    down_ref,
    grads_ref,
    grad_bias_ref,
    out_ref,
):
    grad = grad_ref[...]
    grad_upper = (times_transposed(grad, down_ref[...]) * slope_ref[...]).astype(BFLOAT)
    grad_bias_ref[...] = jnp.sum(grad_upper.astype(FLOAT), axis=0, keepdims=True)
    grads_ref[0] = contract_rows(middle_ref[...], grad_upper).astype(BFLOAT)
    grads_ref[1] = contract_rows(active_ref[...], grad).astype(BFLOAT)
    out = times_transposed(grad_upper, up_ref[...])

    @pl.when(pl.program_id(0) == 0)
    def _():
        out_ref[...] = out

    @pl.when(pl.program_id(0) > 0)
    def _():
        out_ref[...] += out


def feed_backward(grad_feed, middle_low, active, slope, packed):
    tokens, width = middle_low.shape
    hidden = active.shape[1]
    blocks = hidden // width
    whole = pl.BlockSpec((tokens, width), lambda j: (0, 0))
    columns = pl.BlockSpec((tokens, width), lambda j: (0, j))
    return pl.pallas_call(
        feed_back_kernel,
        grid=(blocks,),
        in_specs=[
            whole,
            whole,
            columns,
            columns,
            pl.BlockSpec((None, width, width), lambda j: (j, 0, 0)),
            pl.BlockSpec((None, width, width), lambda j: (blocks + j, 0, 0)),
        ],
        out_specs=[
            pl.BlockSpec((2, None, width, width), lambda j: (0, j, 0, 0)),
            pl.BlockSpec((1, width), lambda j: (0, j)),
            whole,
        ],
        out_shape=[
            jax.ShapeDtypeStruct((2, blocks, width, width), BFLOAT),
            jax.ShapeDtypeStruct((1, hidden), FLOAT),
            jax.ShapeDtypeStruct((tokens, width), FLOAT),
        ],
        compiler_params=ROOMY,
        cost_estimate=FREE,
    )(grad_feed, middle_low, active, slope, packed, packed)


def logits_kernel(rows_ref, table_ref, expo_ref, stats_ref):
    logits = times_transposed(rows_ref[...], table_ref[...])
    peak = jnp.max(logits, axis=1, keepdims=True)
    expo = jnp.exp(logits - peak)
    expo_ref[...] = expo.astype(BFLOAT)
    mass = jnp.sum(expo, axis=1, keepdims=True)
    lane = lax.broadcasted_iota(jnp.int32, (logits.shape[0], LANES), 1)
    stats_ref[...] = jnp.where(lane == 0, peak, mass).T[:8]


def head_logits(rows_all, table_low):
    count, width = rows_all.shape
    shard_rows = table_low.shape[0]
    step = min(512, count)
    return pl.pallas_call(
        logits_kernel,
        grid=(count // step,),
        in_specs=[
            pl.BlockSpec((step, width), lambda i: (i, 0)),
            pl.BlockSpec((shard_rows, width), lambda i: (0, 0)),
        ],
        out_specs=[
            pl.BlockSpec((step, shard_rows), lambda i: (i, 0)),
            pl.BlockSpec((8, step), lambda i: (0, i)),
        ],
        out_shape=[
            jax.ShapeDtypeStruct((count, shard_rows), BFLOAT),
            jax.ShapeDtypeStruct((8, count), FLOAT),
        ],
        compiler_params=ROOMY,
        cost_estimate=FREE,
    )(rows_all, table_low)


def column_sum(value):
    return jnp.sum(value.astype(FLOAT), axis=0)


def layer_forward(weights, embedded, features_low, lengths):
    mats, packed, gains, up_bias = weights
    start_state = layer_norm(embedded, gains[0], gains[1])
    act = start_state.astype(BFLOAT)
    stack = projections(features_low, act, packed, packed.shape[0] - mats.shape[0], gains)
    mixed = attention_call(attend_kernel, lengths, stack, (), 0)
    first_sum = start_state + (product(mixed, mats[6]) + gains[8])
    middle = layer_norm(first_sum, gains[2], gains[3])
    middle_low = middle.astype(BFLOAT)
    active, slope, feed = feed_forward(middle_low, packed, up_bias)
    second_sum = middle + (feed + gains[10])
    kept = (
        embedded,
        act,
        stack,
        mixed,
        first_sum,
        middle_low,
        slope,
        active,
        second_sum,
    )
    return (layer_norm(second_sum, gains[4], gains[5]), kept)


def layer_backward(weights, features_low, lengths, kept, grad_out, head_parts, lines, tools):
    mats, packed, gains, up_bias = weights
    (
        embedded,
        act,
        stack,
        mixed,
        first_sum,
        middle_low,
        slope,
        active,
        second_sum,
    ) = kept
    compacted, give, from_copies, give_rows = tools

    def send(value, name):
        own, blocks = sends(value, lines[name], AXES[name])
        return own, blocks

    def travel(pair, name, *until):
        line = lines[name]
        moved = [shifted(block, line, step) for step, block in enumerate(pair[1], 1)]
        if until:
            moved = list(after(tuple(moved), *until))
        total = pair[0].astype(FLOAT)
        for value in moved:
            total = total + value.astype(FLOAT)
        return total.astype(BFLOAT)

    grad_second, gain_four, gain_five = jax.vjp(layer_norm, second_sum, gains[4], gains[5])[1](
        grad_out
    )
    grad_feed = grad_second.astype(BFLOAT)
    grad_feeds, grad_bias, fed_back = feed_backward(grad_feed, middle_low, active, slope, packed)
    feeds_sum = lax.psum_scatter(grad_feeds, "fsdp", scatter_dimension=2, tiled=True)
    grad_first, gain_two, gain_three = jax.vjp(layer_norm, first_sum, gains[2], gains[3])[1](
        grad_second + fed_back
    )
    grad_attended = grad_first.astype(BFLOAT)
    grad_mixed = times_transposed(grad_attended, mats[6]).astype(BFLOAT)
    pieces = attention_call(
        attend_back_kernel, lengths, stack, (grad_mixed,), 5
    )
    pieces = after(pieces, head_parts[2])
    first_mat = packed.shape[0] - mats.shape[0]
    grad_start, grad_place, sums = start_gradient(grad_first, pieces, packed, first_mat)
    grad_start = after(grad_start, head_parts[3])
    grad_embedded, gain_zero, gain_one = jax.vjp(layer_norm, embedded, gains[0], gains[1])[1](
        grad_start
    )
    grad_vectors = jnp.stack(
        [
            gain_zero,
            gain_one,
            gain_two,
            gain_three,
            gain_four,
            gain_five,
            sums[2, 0],
            sums[4, 0],
            column_sum(grad_attended),
            sums[1, 0],
            column_sum(grad_feed),
        ]
    )
    parts = two_parts(grad_embedded)
    compact = compacted(parts, grad_vectors, grad_bias)
    returned = give(compact)
    pieces = after(pieces, compact)
    token_part = token_gradients(act, mixed, pieces, grad_attended)
    token_core = send(by_owner(token_part, lines), "core")
    pieces = after(pieces, *token_core[1])
    box_part = box_gradients(features_low, stack, pieces, grad_place)
    token_y = send(travel(token_core, "core", box_part), "y")
    box_part = after(box_part, *token_y[1])
    box_core = send(by_owner(box_part, lines), "core")
    box_x = send(travel(box_core, "core"), "x")
    returned = after(returned, *box_x[1])
    rows = from_copies(returned)
    feeds_sum = after(feeds_sum, returned)
    others = after(tuple(rows[1:]), feeds_sum)
    token_z = send(travel(token_y, "y", feeds_sum), "z")
    box_y = send(travel(box_x, "x", token_z[1][0]), "y")
    spread = [give_rows(0, after(rows[0], *box_y[1]))]
    box_z = send(travel(box_y, "y", spread[0]), "z")
    others = after(others, *box_z[1])
    spread += [give_rows(index, value) for index, value in enumerate(others, 1)]
    token_sum = travel(token_z, "z", spread[-1])[:, 0, 0, 0]
    box_half = travel(box_z, "z", token_sum)[:, 0, 0, 0]
    feeds_other = after(from_other_copies(feeds_sum, lines), box_half)
    feeds_sum = feeds_sum.astype(FLOAT) + feeds_other.astype(FLOAT)
    token_mats = both_copies(token_sum, lines)
    box_mats = gather_line(box_half, lines["x"], 2).astype(FLOAT)
    grad_mats = jnp.concatenate([box_mats[2:], token_mats[:3], box_mats[:2], token_mats[3:]])
    return ((grad_mats, feeds_sum), spread, [rows[0], *others], parts)


def combine_mass(first, second):
    peak = jnp.maximum(first[0], second[0])
    mass = first[1] * jnp.exp(first[0] - peak) + second[1] * jnp.exp(second[0] - peak)
    return jnp.stack([peak, mass])


def body(
    token_ids,
    boxes,
    lengths,
    slots,
    labels,
    table,
    mats,
    up,
    down,
    vectors,
    up_bias,
    table_rows,
    table_cols,
    mats_rows,
    mats_cols,
    up_rows,
    up_cols,
    down_rows,
    down_cols,
    vectors_second,
    up_bias_second,
):
    pages = lengths.shape[0]
    tokens = token_ids.shape[0]
    page_len = tokens // pages
    width = table.shape[1]
    shard_rows = table.shape[0]
    slot_count = slots.shape[1]
    groups, copies = lax.axis_size("fsdp"), lax.axis_size("rep")
    group, copy = lax.axis_index("fsdp"), lax.axis_index("rep")
    lines = lines_of(groups, copies)
    table_low = table.astype(BFLOAT)

    own_small = vectors.size + up_bias.size
    small_rows = -(-own_small // width)
    stride = 16 + -(-tokens // (16 * groups)) * 16
    capacity = stride - 2 * small_rows
    buckets = bucket_ids(token_ids, shard_rows)
    places = bucket_places(buckets, capacity, stride, 0)
    requests = bucket_requests(buckets, places, groups, stride)
    own_news = jnp.concatenate([labels.reshape(-1), lengths, buckets.fullest[None]])
    news = jnp.concatenate(
        [
            jnp.repeat(requests, copies, axis=0),
            jnp.broadcast_to(own_news[None], (groups * copies, own_news.shape[0])),
        ],
        axis=1,
    )
    news = lax.all_to_all(news, ("fsdp", "rep"), 0, 0, tiled=True)
    asked = news[:, :stride].reshape(groups, copies, stride)
    asked = jnp.transpose(asked, (1, 0, 2)).reshape(copies, groups * stride)
    labels_all = news[:, stride : stride + pages * slot_count]
    labels_all = labels_all.reshape(groups, copies, pages * slot_count)
    labels_all = lax.dynamic_index_in_dim(labels_all, copy, 1, False).reshape(-1)
    lengths_all = news[:, stride + pages * slot_count : -1]
    turns = (jnp.max(news[:, -1]) + capacity - 1) // capacity

    def fetch(spots, wanted):
        rows = product(one_hot(wanted, shard_rows), table_low).astype(BFLOAT)
        rows = lax.all_to_all(rows.reshape(groups, stride, width), "fsdp", 0, 0, tiled=True)
        return product(one_hot(spots, groups * stride), rows.reshape(groups * stride, width))

    def ask(turn):
        spots = bucket_places(buckets, capacity, stride, turn)
        wanted = bucket_requests(buckets, spots, groups, stride)
        return spots, lax.all_to_all(wanted, "fsdp", 0, 0, tiled=True).reshape(-1)

    embedded = fetch(places, lax.dynamic_index_in_dim(asked, copy, 0, False))
    embedded = lax.while_loop(
        lambda state: state[0] < turns,
        lambda state: (state[0] + 1, state[1] + fetch(*ask(state[0]))),
        (jnp.int32(1), embedded),
    )[1]

    own_labels = labels_all - group * shard_rows
    label_rows = product(one_hot(own_labels, shard_rows), table_low).astype(BFLOAT)
    embedded = after(embedded, label_rows)

    depth = mats.shape[0]
    first_up, after_up = 1 + depth, 1 + depth + up_cols.shape[0] // width
    items = after_up + 1
    lane = jnp.arange(width)
    singles = jnp.pad(jnp.sum(mats_rows, axis=1), (1, width - first_up))
    singles = jnp.where(lane == 0, jnp.sum(table_rows), singles)
    singles = jnp.where((lane >= first_up) & (lane < after_up), jnp.sum(up_rows), singles)
    singles = jnp.where(lane == after_up, jnp.sum(down_rows), singles)
    embedded = after(embedded, singles)

    small = jnp.concatenate([vectors.astype(BFLOAT).reshape(-1), up_bias.astype(BFLOAT)])[None]

    def lay(first, second, bit):
        low = (group & bit) == 0
        return jnp.concatenate([jnp.where(low, first, second), jnp.where(low, second, first)])

    bit = 1
    while bit < groups:
        pairs = [(i, i ^ bit) for i in range(groups)]
        small = lay(small, lax.ppermute(small, "fsdp", pairs), bit)
        bit *= 2
    split = vectors.size
    gains = small[:, :split].reshape(groups, vectors.shape[0], -1)
    gains = jnp.transpose(gains, (1, 0, 2)).reshape(vectors.shape[0], width).astype(FLOAT)
    own_rows, hidden = up.shape
    feed_blocks = hidden // width
    bias = small[:, split:].reshape(groups, feed_blocks, own_rows)
    bias = jnp.transpose(bias, (1, 0, 2)).reshape(-1).astype(FLOAT)
    gains, bias = lax.optimization_barrier((gains, bias))
    up_blocks = up.astype(BFLOAT).reshape(own_rows, groups, feed_blocks, own_rows)
    up_blocks = jnp.transpose(up_blocks, (2, 0, 1, 3)).reshape(feed_blocks, own_rows, width)
    down_blocks = down.astype(BFLOAT).reshape(feed_blocks, own_rows, width)
    packed = jnp.concatenate([up_blocks, down_blocks, mats.astype(BFLOAT)])
    packed = lax.all_gather(packed, "fsdp", axis=1, tiled=True)
    layer_mats = packed[2 * feed_blocks :]
    weights = (layer_mats, packed, gains, bias)

    features_low = box_features(boxes, width).astype(BFLOAT)
    top_state, kept = layer_forward(weights, embedded, features_low, lengths)

    where_at = slots * lengths[:, None] // 256 + jnp.arange(pages)[:, None] * page_len
    pick = one_hot(where_at.reshape(-1), tokens)
    rows_low = product(pick, top_state.astype(BFLOAT)).astype(BFLOAT)
    rows_all = rows_low[None, None, None]
    for axis, name in enumerate(("z", "y", "core")):
        rows_all = gather_line(rows_all, lines[name], axis)
    rows_all = rows_all.reshape(-1, width)
    expo, stats = head_logits(rows_all, table_low)
    peak_here = stats[0]
    products = product(expo, table_low)
    stats = paired(stats[:2].reshape(2, -1, LANES), "fsdp", combine_mass, products).reshape(2, -1)
    products, peak, mass = lax.optimization_barrier((products, *stats))
    log_total = peak + jnp.log(mass)
    factor = jnp.exp(peak_here - log_total)

    is_token = jnp.arange(slot_count) < M_TOK
    valid_all = valid_slots(lengths_all.reshape(-1), slot_count).astype(FLOAT)
    count_token = jnp.sum(jnp.where(is_token, valid_all, 0.0))
    count_area = jnp.sum(jnp.where(is_token, 0.0, valid_all))
    figure = jnp.arange(4)
    counts = jnp.where(figure == 1, count_token, jnp.where(figure == 3, count_area, 0.0))
    count_token, count_area, counts = lax.optimization_barrier((count_token, count_area, counts))
    valid = valid_all.reshape(groups, copies, pages, slot_count)
    valid = lax.dynamic_index_in_dim(valid, copy, 1, False).reshape(-1, slot_count)
    share = jnp.where(is_token, 1.0 / count_token, 1.0 / count_area)
    weight = (valid * share[None, :]).reshape(-1)
    grad_rows = (products * factor[:, None] - label_rows.astype(FLOAT)) * weight[:, None]
    grad_rows = grad_rows.astype(BFLOAT)
    grad_rows = grad_rows.reshape(
        lines["z"].count, lines["y"].count, lines["core"].count, -1, width
    )
    own, blocks = sends(grad_rows, lines["core"], 2)
    weighted = (rows_all.astype(FLOAT) * weight[:, None]).astype(BFLOAT)
    expo, weighted = after((expo, weighted), *blocks)
    mine = own_labels[:, None] == jnp.arange(shard_rows)[None, :]
    grad_logits = expo.astype(FLOAT) * factor[:, None] - mine.astype(FLOAT)
    own, blocks = sends(received(own, blocks, lines["core"]), lines["y"], 1)
    grad_logits = after(grad_logits.astype(BFLOAT), *blocks)
    head_low = contract_rows(grad_logits, weighted).astype(BFLOAT)
    totals = lax.dynamic_slice_in_dim(log_total * valid.reshape(-1), group * pages * slot_count, pages * slot_count)
    targets = jnp.sum(after(rows_all, *blocks).astype(FLOAT) * label_rows.astype(FLOAT), axis=1)
    losses = jnp.sum(totals.reshape(-1, slot_count), axis=0)
    losses = losses - jnp.sum(targets.reshape(-1, slot_count) * valid, axis=0)
    token_loss = jnp.sum(jnp.where(is_token, losses, 0.0))
    area_loss = jnp.sum(jnp.where(is_token, 0.0, losses))
    singles = jnp.where(lane == items + 1, token_loss, jnp.where(lane == items + 3, area_loss, singles))
    own, blocks = sends(received(own, blocks, lines["y"]), lines["z"], 0)
    blocks = list(after(tuple(blocks), head_low, singles))
    grad_rows = received(own, blocks, lines["z"]).reshape(-1, width)
    fifth = shard_rows // 5
    cuts = [fifth, 2 * fifth, shard_rows - (shard_rows - 2 * fifth) // 2]
    head_parts = [from_other_copies(part, lines) for part in jnp.split(head_low, cuts)]
    grad_rows = after(grad_rows, *head_parts[:2])
    grad_top = sum(contract_rows(pick, part) for part in two_parts(grad_rows))

    def compacted(spots, parts):
        spread = one_hot(spots, groups * stride)
        return sum(contract_rows(spread, part) for part in parts)

    def compacted_first(parts, grad_vectors, grad_bias):
        small = grad_vectors.reshape(grad_vectors.shape[0], groups, -1)
        small = jnp.transpose(small, (1, 0, 2)).reshape(groups, -1)
        grad_bias = jnp.transpose(grad_bias.reshape(feed_blocks, groups, own_rows), (1, 0, 2))
        small = jnp.concatenate([small, grad_bias.reshape(groups, -1)], axis=1)
        small = jnp.pad(small, ((0, 0), (0, small_rows * width - own_small)))
        small = jnp.stack(two_parts(small.reshape(groups, small_rows, width)), axis=1)
        small = small.reshape(groups, 2 * small_rows, width).astype(FLOAT)
        small = jnp.pad(small, ((0, 0), (capacity, 0), (0, 0))).reshape(groups * stride, width)
        return (compacted(places, parts) + small).astype(BFLOAT)

    def give(rows):
        rows = lax.all_to_all(rows.reshape(groups, stride, width), "fsdp", 0, 0, tiled=True)
        return rows.reshape(groups * stride, width)

    def spread_rows(wanted, rows):
        return contract_rows(one_hot(wanted, shard_rows), rows)

    def small_sum(rows):
        rows = rows.reshape(groups, stride, width)[:, capacity:].astype(FLOAT)
        rows = jnp.sum(rows, axis=0).reshape(2, small_rows * width)
        return (rows[0] + rows[1])[:own_small]

    if copies == 2:
        from_copies = lambda value: [value, shifted(value, lines["x"], 1)]
        copy_order = [copy, 1 - copy]
    else:
        from_copies = lambda value: list(lax.all_gather(value, "rep"))
        copy_order = list(range(copies))
    asked_of = [lax.dynamic_index_in_dim(asked, index, 0, False) for index in copy_order]

    def give_rows(index, rows):
        return spread_rows(asked_of[index], rows)

    tools = (compacted_first, give, from_copies, give_rows)
    layer_grads, spread, given, embedded_parts = layer_backward(
        weights, features_low, lengths, kept, grad_top, head_parts, lines, tools
    )
    mats_grad, feeds_grad = layer_grads
    up_grad = jnp.transpose(feeds_grad[0].reshape(feed_blocks, own_rows, groups, own_rows), (1, 2, 0, 3))
    up_grad = up_grad.reshape(own_rows, hidden)
    down_grad = feeds_grad[1].reshape(hidden // groups, width)
    small = [small_sum(rows) for rows in given]
    small = sum(small[1:], small[0])
    vectors_grad = small[: vectors.size].reshape(vectors.shape)
    bias_grad = small[vectors.size :]

    head_grad = head_low.astype(FLOAT) + jnp.concatenate(head_parts).astype(FLOAT)
    table_grad = head_grad + sum(spread[1:], spread[0])

    def another(state):
        turn, total = state
        spots, wanted = ask(turn)
        given = from_copies(give(compacted(spots, embedded_parts).astype(BFLOAT)))
        spread = [spread_rows(*pair) for pair in zip(from_copies(wanted), given)]
        return turn + 1, total + sum(spread[1:], spread[0])

    table_grad = lax.while_loop(lambda state: state[0] < turns, another, (jnp.int32(1), table_grad))[1]

    feed_cols = hidden // width
    sizes = [(shard_rows * groups, width)] + [(mats.shape[1] * groups, width)] * depth
    sizes += [(up.shape[0] * groups, hidden), (down.shape[0] * groups, width)]
    row_squares = [jnp.sum(grad * grad, axis=-1) for grad in (table_grad, mats_grad, up_grad, down_grad)]
    singles = jnp.where(lane == items, jnp.sum(small * small), singles)
    sums = jnp.concatenate(
        [
            jnp.sum(table_grad * table_grad, axis=0)[None],
            jnp.sum(mats_grad * mats_grad, axis=1),
            jnp.sum(up_grad * up_grad, axis=0).reshape(feed_cols, width),
            jnp.sum(down_grad * down_grad, axis=0)[None],
            singles[None],
        ]
    )
    cols_old = jnp.concatenate(
        [table_cols[None], mats_cols, up_cols.reshape(feed_cols, width), down_cols[None]]
    )
    sums = paired(sums, "fsdp", jnp.add)
    loss_parts = counts + paired(sums[-1, items + 1 : items + 5], "rep", jnp.add)
    totals = jnp.sum(sums[:-1], axis=1)
    norm_square = jnp.sum(totals) + sums[-1, items]
    grad_norm = jnp.sqrt(norm_square)
    clip = jnp.minimum(1.0, CLIP_NORM / grad_norm)
    square = clip * clip

    def renewed(old, value):
        return DECAY * old + (1.0 - DECAY) * (value + TINY_TERM)

    repeats = [1] * first_up + [feed_cols, 1]
    tall_rows, wide_rows = (
        jnp.array([size[k] for size, n in zip(sizes, repeats) for _ in range(n)], FLOAT)
        for k in range(2)
    )
    row = jnp.arange(items)
    of_up = (row >= first_up) & (row < after_up)
    item_totals = jnp.where(of_up, jnp.sum(jnp.where(of_up, totals, 0.0)), totals)
    mean_rows = renewed(
        sums[-1, :items] / tall_rows, square * item_totals / (tall_rows * wide_rows)
    )
    cols_new = renewed(cols_old, square * sums[:-1] / tall_rows[:, None])
    col_factors = lax.rsqrt(cols_new / mean_rows[:, None])
    step = LEARN_RATE * clip

    def updated(grad, param, rows_old, row_square, col_factor):
        rows_new = renewed(rows_old, square * row_square / grad.shape[-1])
        factor = step * lax.rsqrt(rows_new)
        return grad * clip, rows_new, param - grad * factor[..., None] * col_factor[..., None, :]

    up_factor = col_factors[first_up:after_up].reshape(hidden)
    table_out = updated(table_grad, table, table_rows, row_squares[0], col_factors[0])
    mats_out = updated(mats_grad, mats, mats_rows, row_squares[1], col_factors[1:first_up])
    up_out = updated(up_grad, up, up_rows, row_squares[2], up_factor)
    down_out = updated(down_grad, down, down_rows, row_squares[3], col_factors[after_up])
    clipped_vectors = vectors_grad * clip
    vectors_second_new = DECAY * vectors_second + (1.0 - DECAY) * (
        clipped_vectors * clipped_vectors + TINY_TERM
    )
    vectors_new = vectors - VECTOR_RATE * clipped_vectors * lax.rsqrt(vectors_second_new)
    clipped_bias = bias_grad * clip
    bias_second_new = DECAY * up_bias_second + (1.0 - DECAY) * (
        clipped_bias * clipped_bias + TINY_TERM
    )
    bias_new = up_bias - VECTOR_RATE * clipped_bias * lax.rsqrt(bias_second_new)
    return (
        table_out[0],
        table_out[1],
        cols_new[0],
        table_out[2],
        mats_out[0],
        mats_out[1],
        cols_new[1:first_up],
        mats_out[2],
        up_out[0],
        up_out[1],
        cols_new[first_up:after_up].reshape(hidden),
        up_out[2],
        down_out[0],
        down_out[1],
        cols_new[after_up],
        down_out[2],
        clipped_vectors,
        vectors_second_new,
        vectors_new,
        clipped_bias,
        bias_second_new,
        bias_new,
        grad_norm,
        loss_parts,
    )


def solution(mesh):
    return jax.shard_map(
        body,
        mesh=mesh,
        in_specs=(
            P(("fsdp", "rep")),
            P(None, ("fsdp", "rep")),
            P(("fsdp", "rep")),
            P(("fsdp", "rep"), None),
            P(("fsdp", "rep"), None),
            P("fsdp", None),
            P(None, "fsdp", None),
            P("fsdp", None),
            P("fsdp", None),
            P(None, "fsdp"),
            P("fsdp"),
            P("fsdp"),
            P(),
            P(None, "fsdp"),
            P(),
            P("fsdp"),
            P(),
            P("fsdp"),
            P(),
            P(None, "fsdp"),
            P("fsdp"),
        ),
        out_specs=(
            P("fsdp", None),
            P("fsdp"),
            P(),
            P("fsdp", None),
            P(None, "fsdp", None),
            P(None, "fsdp"),
            P(),
            P(None, "fsdp", None),
            P("fsdp", None),
            P("fsdp"),
            P(),
            P("fsdp", None),
            P("fsdp", None),
            P("fsdp"),
            P(),
            P("fsdp", None),
            P(None, "fsdp"),
            P(None, "fsdp"),
            P(None, "fsdp"),
            P("fsdp"),
            P("fsdp"),
            P("fsdp"),
            P(),
            P(),
        ),
        check_vma=False,
    )
```

```python
import math
from typing import NamedTuple

import jax
import jax.numpy as jnp
from jax import lax
from jax.experimental import pallas as pl
from jax.experimental.pallas import tpu as pltpu
from jax.sharding import PartitionSpec as P

HEAD_DIM = 64
PAGE_LEN = 512
M_TOK = 64
M_AREA = 64
STEP = 10


EPSILON = 1e-05
CLIP_NORM = 0.1
LEARN_RATE = 0.02
VECTOR_RATE = 0.3
TINY_TERM = 1e-30
NEGATIVE = -1e30
BFLOAT = jnp.bfloat16
FLOAT = jnp.float32
LANES = 128
DECAY = 1.0 - STEP ** (-0.8)


class Line(NamedTuple):
    axis: str
    total: int
    stride: int
    count: int


def lines_of(groups, copies):
    cores = min(2, groups)
    rest = (groups // cores).bit_length() - 1
    y_count = 1 << (rest // 2)
    z_count = groups // (cores * y_count)
    return {
        "z": Line("fsdp", groups, cores * y_count, z_count),
        "y": Line("fsdp", groups, cores, y_count),
        "core": Line("fsdp", groups, 1, cores),
        "x": Line("rep", copies, 1, copies),
    }


def place_on(line):
    return lax.axis_index(line.axis) // line.stride % line.count


def shifted(value, line, step):
    pairs = []
    for i in range(line.total):
        place = i // line.stride % line.count
        pairs.append((i, i + ((place + step) % line.count - place) * line.stride))
    return lax.ppermute(value, line.axis, pairs)


def gather_line(value, line, axis):
    count = line.count
    if count == 1:
        return value
    here = place_on(line)
    pieces = [value] + [shifted(value, line, step) for step in range(1, count)]
    blocks = []
    for place in range(count):
        blocks.append(lax.select_n(here, *[pieces[(i - place) % count] for i in range(count)]))
    return jnp.concatenate(blocks, axis=axis)


def sends(value, line, axis):
    size = value.shape[axis] // line.count
    here = place_on(line)

    def block(place):
        return lax.dynamic_slice_in_dim(value, place * size, size, axis)

    return block(here), [
        block((here + step) % line.count).astype(BFLOAT) for step in range(1, line.count)
    ]


def received(own, blocks, line):
    total = own.astype(FLOAT)
    for step, value in enumerate(blocks, 1):
        total = total + shifted(value, line, step).astype(FLOAT)
    return total


def reduce_line(value, line, axis):
    return received(*sends(value, line, axis), line)


def after(value, *others):
    return lax.optimization_barrier((value, *others))[0]


def paired(value, axis, combine, beside=None):
    size = lax.axis_size(axis)
    bit = 1
    while bit < size:
        pairs = [(i, i ^ bit) for i in range(size)]
        other = lax.ppermute(value, axis, pairs)
        if beside is not None and bit == 2:
            other = after(other, beside)
        value = combine(value, other)
        bit *= 2
    return value


def by_owner(value, lines):
    count, _, columns = value.shape
    return value.reshape(count, lines["z"].count, lines["y"].count, lines["core"].count, -1, columns)


AXES = {"z": 1, "y": 2, "core": 3, "x": 5}


def part_sends(value, lines, name):
    return sends(value, lines[name], AXES[name])


def part_received(pair, lines, name):
    return received(*pair, lines[name]).astype(BFLOAT)


def both_copies(value, lines):
    if lines["x"].count == 2:
        return value.astype(FLOAT) + shifted(value, lines["x"], 1).astype(FLOAT)
    return lax.psum(value, "rep").astype(FLOAT)


def from_other_copies(value, lines):
    if lines["x"].count == 2:
        return shifted(value, lines["x"], 1)
    return (lax.psum(value, "rep").astype(FLOAT) - value.astype(FLOAT)).astype(BFLOAT)


def layer_norm(value, gain, shift):
    center = value - jnp.mean(value, axis=-1, keepdims=True)
    spread = jnp.mean(center * center, axis=-1, keepdims=True)
    return center * lax.rsqrt(spread + EPSILON) * gain + shift


def box_features(boxes, width):
    count = width // 8
    freqs = jnp.exp(-math.log(10000.0) * jnp.arange(count, dtype=FLOAT) / count)
    angle = boxes.astype(FLOAT)[:, :, None] * freqs[None, None, :]
    waves = jnp.concatenate([jnp.sin(angle), jnp.cos(angle)], axis=2)
    return jnp.transpose(waves, (1, 0, 2)).reshape(boxes.shape[1], width)


def valid_slots(lengths, slot_count):
    n_tok = jnp.minimum(M_TOK, 1 + lengths * M_TOK // PAGE_LEN)
    n_area = jnp.minimum(M_AREA, 1 + lengths * (3 * M_AREA) // (4 * PAGE_LEN))
    index = jnp.arange(slot_count, dtype=jnp.int32)[None, :]
    return jnp.where(index < M_TOK, index < n_tok[:, None], index - M_TOK < n_area[:, None])


def product(left, right):
    return jnp.dot(left, right, preferred_element_type=FLOAT)


def contract_rows(left, right):
    return lax.dot_general(left, right, (((0,), (0,)), ((), ())), preferred_element_type=FLOAT)


def times_transposed(left, right):
    return lax.dot_general(left, right, (((1,), (1,)), ((), ())), preferred_element_type=FLOAT)


def two_parts(value):
    high = value.astype(BFLOAT)
    return high, (value - high.astype(FLOAT)).astype(BFLOAT)


def side(index):
    lane = lax.broadcasted_iota(jnp.int32, (1, LANES), 1)
    return lane // HEAD_DIM == index


def only(mask, value):
    return jnp.where(mask, value, jnp.zeros_like(value))


def attend_kernel(length_ref, stack_ref, out_ref):
    length = length_ref[pl.program_id(0)]
    box_query, box_key, query, key, value = (stack_ref[index] for index in range(1, 6))
    keys = jnp.concatenate([key, box_key, key], axis=1)
    keep = lax.broadcasted_iota(jnp.int32, (1, key.shape[0]), 1) < length
    scale = jnp.asarray(HEAD_DIM ** (-0.5), BFLOAT)
    mixed = jnp.zeros(out_ref.shape, FLOAT)
    for head in range(LANES // HEAD_DIM):
        mask = side(head)
        own = only(mask, query) * scale
        other = only(mask, box_query) * scale
        score = times_transposed(jnp.concatenate([own, own, other], axis=1), keys)
        score = jnp.where(keep, score, NEGATIVE)
        expo = jnp.exp(score - jnp.max(score, axis=1, keepdims=True))
        prob = (expo * (1.0 / jnp.sum(expo, axis=1, keepdims=True))).astype(BFLOAT)
        mixed = jnp.where(mask, product(prob, value), mixed)
    out_ref[...] = mixed.astype(BFLOAT)


def attend_back_kernel(length_ref, stack_ref, grad_ref, out_ref):
    length = length_ref[pl.program_id(0)]
    box_query, box_key, query, key, value = (stack_ref[index] for index in range(1, 6))
    grad = grad_ref[...]
    rows = key.shape[0]
    keys = jnp.concatenate([key, box_key, key], axis=1)
    both_queries = jnp.concatenate([query, box_query], axis=1)
    both_keys = jnp.concatenate([key, box_key], axis=1)
    keep = lax.broadcasted_iota(jnp.int32, (rows, 1), 0) < length
    scale = jnp.asarray(HEAD_DIM ** (-0.5), BFLOAT)
    outs = [jnp.zeros((rows, LANES), FLOAT) for _ in range(5)]
    for head in range(LANES // HEAD_DIM):
        mask = side(head)
        own = only(mask, query) * scale
        other = only(mask, box_query) * scale
        score = times_transposed(keys, jnp.concatenate([own, own, other], axis=1))
        score = jnp.where(keep, score, NEGATIVE)
        expo = jnp.exp(score - jnp.max(score, axis=0, keepdims=True))
        prob = expo * (1.0 / jnp.sum(expo, axis=0, keepdims=True))
        grad_value = product(prob.astype(BFLOAT), grad)
        grad_prob = times_transposed(only(mask, value), grad)
        grad_score = prob * (grad_prob - jnp.sum(prob * grad_prob, axis=0, keepdims=True))
        low = grad_score.astype(BFLOAT) * scale
        with_queries = product(low, both_queries)
        with_keys = contract_rows(low, both_keys)
        fresh = (
            with_keys[:, :LANES] + with_keys[:, LANES:],
            with_queries[:, :LANES] + with_queries[:, LANES:],
            grad_value,
            with_keys[:, :LANES],
            with_queries[:, :LANES],
        )
        outs = [jnp.where(mask, new, old) for new, old in zip(fresh, outs)]
    for index, out in enumerate(outs):
        out_ref[index] = out.astype(BFLOAT)


FREE = pl.CostEstimate(flops=0, transcendentals=0, bytes_accessed=0)


ROOMY = pltpu.CompilerParams(vmem_limit_bytes=30 * 1024 * 1024)


def attention_call(kernel, lengths, stack, arrays, stacked):
    count, tokens, width = stack.shape
    pages = lengths.shape[0]
    spec = pl.BlockSpec((tokens // pages, LANES), lambda page, pair: (page, pair))

    def stack_spec(count):
        return pl.BlockSpec((count, tokens // pages, LANES), lambda page, pair: (0, page, pair))

    shape = (stacked, tokens, width) if stacked else (tokens, width)
    return pl.pallas_call(
        kernel,
        grid=(pages, width // LANES),
        in_specs=[pl.BlockSpec(memory_space=pltpu.SMEM), stack_spec(count)] + [spec] * len(arrays),
        out_specs=stack_spec(stacked) if stacked else spec,
        out_shape=jax.ShapeDtypeStruct(shape, BFLOAT),
        compiler_params=ROOMY,
        cost_estimate=FREE,
    )(lengths, stack, *arrays)


def start_kernel(first_ref, grad_ref, mat_ref, out_ref, place_ref, sums_ref, total):
    step = pl.program_id(0)
    grad = grad_ref[...]
    term = times_transposed(grad, mat_ref[...])
    sums_ref[...] = jnp.sum(grad.astype(FLOAT), axis=0, keepdims=True)

    @pl.when(step == 0)
    def _():
        total[...] = term

    @pl.when(step == 1)
    def _():
        low = (total[...] + term).astype(BFLOAT)
        place_ref[...] = low
        sums_ref[...] = jnp.sum(low.astype(FLOAT), axis=0, keepdims=True)

    @pl.when(step == 2)
    def _():
        out_ref[...] = first_ref[...] + term

    @pl.when(step > 2)
    def _():
        out_ref[...] += term


def start_gradient(grad_first, pieces, packed, first_mat):
    tokens, width = grad_first.shape
    whole = pl.BlockSpec((tokens, width), lambda k: (0, 0))

    def piece(k):
        return jnp.where(k < 2, k + 3, k - 2)

    def mat(k):
        return first_mat + jnp.where(k < 2, k + 4, k - 1)

    return pl.pallas_call(
        start_kernel,
        grid=(5,),
        in_specs=[
            whole,
            pl.BlockSpec((None, tokens, width), lambda k: (piece(k), 0, 0)),
            pl.BlockSpec((None, width, width), lambda k: (mat(k), 0, 0)),
        ],
        out_specs=[whole, whole, pl.BlockSpec((None, 1, width), lambda k: (k, 0, 0))],
        out_shape=[
            jax.ShapeDtypeStruct((tokens, width), FLOAT),
            jax.ShapeDtypeStruct((tokens, width), BFLOAT),
            jax.ShapeDtypeStruct((5, 1, width), FLOAT),
        ],
        scratch_shapes=[pltpu.VMEM((tokens, width), FLOAT)],
        compiler_params=ROOMY,
        cost_estimate=FREE,
    )(grad_first, pieces, packed)


def token_kernel(act_ref, mixed_ref, grad_ref, attended_ref, out_ref):
    @pl.when(pl.program_id(0) < 3)
    def _():
        out_ref[...] = contract_rows(act_ref[...], grad_ref[...]).astype(BFLOAT)

    @pl.when(pl.program_id(0) == 3)
    def _():
        out_ref[...] = contract_rows(mixed_ref[...], attended_ref[...]).astype(BFLOAT)


def token_gradients(act, mixed, pieces, grad_attended):
    tokens, width = act.shape
    whole = pl.BlockSpec((tokens, width), lambda k: (0, 0))
    return pl.pallas_call(
        token_kernel,
        grid=(4,),
        in_specs=[
            whole,
            whole,
            pl.BlockSpec((None, tokens, width), lambda k: (jnp.minimum(k, 2), 0, 0)),
            whole,
        ],
        out_specs=pl.BlockSpec((None, width, width), lambda k: (k, 0, 0)),
        out_shape=jax.ShapeDtypeStruct((4, width, width), BFLOAT),
        compiler_params=ROOMY,
        cost_estimate=FREE,
    )(act, mixed, pieces, grad_attended)


def box_kernel(features_ref, place_ref, grad_ref, grad_place_ref, out_ref):
    @pl.when(pl.program_id(0) < 2)
    def _():
        out_ref[...] = contract_rows(place_ref[...], grad_ref[...]).astype(BFLOAT)

    @pl.when(pl.program_id(0) == 2)
    def _():
        out_ref[...] = contract_rows(features_ref[...], grad_place_ref[...]).astype(BFLOAT)


def box_gradients(features_low, stack, pieces, grad_place):
    tokens, width = grad_place.shape
    whole = pl.BlockSpec((tokens, width), lambda k: (0, 0))
    return pl.pallas_call(
        box_kernel,
        grid=(3,),
        in_specs=[
            whole,
            pl.BlockSpec((None, tokens, width), lambda k: (0, 0, 0)),
            pl.BlockSpec((None, tokens, width), lambda k: (jnp.minimum(k, 1) + 3, 0, 0)),
            whole,
        ],
        out_specs=pl.BlockSpec((None, width, width), lambda k: (k, 0, 0)),
        out_shape=jax.ShapeDtypeStruct((3, width, width), BFLOAT),
        compiler_params=ROOMY,
        cost_estimate=FREE,
    )(features_low, stack, pieces, grad_place)


def project_kernel(features_ref, act_ref, mat_ref, bias_ref, out_ref, place):
    step = pl.program_id(0)

    @pl.when(step == 0)
    def _():
        low = (product(features_ref[...], mat_ref[...]) + bias_ref[...]).astype(BFLOAT)
        place[...] = low
        out_ref[...] = low

    @pl.when((step > 0) & (step < 3))
    def _():
        out_ref[...] = product(place[...], mat_ref[...]).astype(BFLOAT)

    @pl.when(step >= 3)
    def _():
        out_ref[...] = (product(act_ref[...], mat_ref[...]) + bias_ref[...]).astype(BFLOAT)


def projections(features_low, act, packed, first_mat, gains):
    tokens, width = act.shape
    whole = pl.BlockSpec((tokens, width), lambda k: (0, 0))
    none = jnp.zeros_like(gains[0])
    biases = jnp.stack([gains[9], none, none, gains[6], none, gains[7]])[:, None]

    def mat(k):
        return first_mat + jnp.where(k == 0, 0, jnp.where(k < 3, k + 3, k - 2))

    return pl.pallas_call(
        project_kernel,
        grid=(6,),
        in_specs=[
            whole,
            whole,
            pl.BlockSpec((None, width, width), lambda k: (mat(k), 0, 0)),
            pl.BlockSpec((None, 1, width), lambda k: (k, 0, 0)),
        ],
        out_specs=pl.BlockSpec((None, tokens, width), lambda k: (k, 0, 0)),
        out_shape=jax.ShapeDtypeStruct((6, tokens, width), BFLOAT),
        scratch_shapes=[pltpu.VMEM((tokens, width), BFLOAT)],
        compiler_params=ROOMY,
        cost_estimate=FREE,
    )(features_low, act, packed, biases)


class Buckets(NamedTuple):
    owner: jax.Array
    row: jax.Array
    first: jax.Array
    rank: jax.Array
    fullest: jax.Array


def bucket_ids(ids, shard_rows):
    owner, row = ids // shard_rows, ids % shard_rows
    index = jnp.arange(ids.shape[0], dtype=jnp.int32)
    earlier = index[None, :] < index[:, None]
    same = ids[:, None] == ids[None, :]
    first = ~jnp.any(same & earlier, axis=1)
    before = (owner[:, None] == owner[None, :]) & earlier & first[None, :]
    rank = jnp.sum(before.astype(jnp.int32), axis=1)
    rank = jnp.sum(jnp.where(same & first[None, :], rank[None, :], 0), axis=1)
    return Buckets(owner, row, first, rank, jnp.max(rank) + 1)


def bucket_places(buckets, capacity, stride, turn):
    shifted = buckets.rank - turn * capacity
    inside = (shifted >= 0) & (shifted < capacity)
    return jnp.where(inside, buckets.owner * stride + shifted, -1)


def bucket_requests(buckets, places, groups, stride):
    hit = (places[:, None] == jnp.arange(groups * stride)[None, :]) & buckets.first[:, None]
    rows = jnp.sum(jnp.where(hit, buckets.row[:, None] + 1, 0), axis=0) - 1
    return rows.reshape(groups, stride)


def one_hot(index, count):
    return (index[:, None] == jnp.arange(count, dtype=jnp.int32)[None, :]).astype(BFLOAT)


def feed_kernel(middle_ref, up_ref, bias_ref, down_ref, active_ref, slope_ref, out_ref):
    value = product(middle_ref[...], up_ref[...]) + bias_ref[...]
    share = 0.5 * (1.0 + lax.erf(value * math.sqrt(0.5)))
    density = jnp.exp(-0.5 * value * value) * (1.0 / math.sqrt(2.0 * math.pi))
    active = (value * share).astype(BFLOAT)
    active_ref[...] = active
    slope_ref[...] = share + value * density
    out = product(active, down_ref[...])

    @pl.when(pl.program_id(0) == 0)
    def _():
        out_ref[...] = out

    @pl.when(pl.program_id(0) > 0)
    def _():
        out_ref[...] += out


def feed_forward(middle_low, packed, bias):
    tokens, width = middle_low.shape
    hidden = bias.shape[0]
    blocks = hidden // width
    whole = pl.BlockSpec((tokens, width), lambda j: (0, 0))
    columns = pl.BlockSpec((tokens, width), lambda j: (0, j))
    return pl.pallas_call(
        feed_kernel,
        grid=(blocks,),
        in_specs=[
            whole,
            pl.BlockSpec((None, width, width), lambda j: (j, 0, 0)),
            pl.BlockSpec((1, width), lambda j: (0, j)),
            pl.BlockSpec((None, width, width), lambda j: (blocks + j, 0, 0)),
        ],
        out_specs=[columns, columns, whole],
        out_shape=[
            jax.ShapeDtypeStruct((tokens, hidden), BFLOAT),
            jax.ShapeDtypeStruct((tokens, hidden), FLOAT),
            jax.ShapeDtypeStruct((tokens, width), FLOAT),
        ],
        compiler_params=ROOMY,
        cost_estimate=FREE,
    )(middle_low, packed, bias[None], packed)


def feed_back_kernel(
    grad_ref,
    middle_ref,
    active_ref,
    slope_ref,
    up_ref,
    down_ref,
    grads_ref,
    grad_bias_ref,
    out_ref,
):
    grad = grad_ref[...]
    grad_upper = (times_transposed(grad, down_ref[...]) * slope_ref[...]).astype(BFLOAT)
    grad_bias_ref[...] = jnp.sum(grad_upper.astype(FLOAT), axis=0, keepdims=True)
    grads_ref[0] = contract_rows(middle_ref[...], grad_upper).astype(BFLOAT)
    grads_ref[1] = contract_rows(active_ref[...], grad).astype(BFLOAT)
    out = times_transposed(grad_upper, up_ref[...])

    @pl.when(pl.program_id(0) == 0)
    def _():
        out_ref[...] = out

    @pl.when(pl.program_id(0) > 0)
    def _():
        out_ref[...] += out


def feed_backward(grad_feed, middle_low, active, slope, packed):
    tokens, width = middle_low.shape
    hidden = active.shape[1]
    blocks = hidden // width
    whole = pl.BlockSpec((tokens, width), lambda j: (0, 0))
    columns = pl.BlockSpec((tokens, width), lambda j: (0, j))
    return pl.pallas_call(
        feed_back_kernel,
        grid=(blocks,),
        in_specs=[
            whole,
            whole,
            columns,
            columns,
            pl.BlockSpec((None, width, width), lambda j: (j, 0, 0)),
            pl.BlockSpec((None, width, width), lambda j: (blocks + j, 0, 0)),
        ],
        out_specs=[
            pl.BlockSpec((2, None, width, width), lambda j: (0, j, 0, 0)),
            pl.BlockSpec((1, width), lambda j: (0, j)),
            whole,
        ],
        out_shape=[
            jax.ShapeDtypeStruct((2, blocks, width, width), BFLOAT),
            jax.ShapeDtypeStruct((1, hidden), FLOAT),
            jax.ShapeDtypeStruct((tokens, width), FLOAT),
        ],
        compiler_params=ROOMY,
        cost_estimate=FREE,
    )(grad_feed, middle_low, active, slope, packed, packed)


def logits_kernel(rows_ref, table_ref, expo_ref, stats_ref):
    logits = times_transposed(rows_ref[...], table_ref[...])
    peak = jnp.max(logits, axis=1, keepdims=True)
    expo = jnp.exp(logits - peak)
    expo_ref[...] = expo.astype(BFLOAT)
    mass = jnp.sum(expo, axis=1, keepdims=True)
    lane = lax.broadcasted_iota(jnp.int32, (logits.shape[0], LANES), 1)
    stats_ref[...] = jnp.where(lane == 0, peak, mass).T[:8]


def head_logits(rows_all, table_low):
    count, width = rows_all.shape
    shard_rows = table_low.shape[0]
    step = min(512, count)
    return pl.pallas_call(
        logits_kernel,
        grid=(count // step,),
        in_specs=[
            pl.BlockSpec((step, width), lambda i: (i, 0)),
            pl.BlockSpec((shard_rows, width), lambda i: (0, 0)),
        ],
        out_specs=[
            pl.BlockSpec((step, shard_rows), lambda i: (i, 0)),
            pl.BlockSpec((8, step), lambda i: (0, i)),
        ],
        out_shape=[
            jax.ShapeDtypeStruct((count, shard_rows), BFLOAT),
            jax.ShapeDtypeStruct((8, count), FLOAT),
        ],
        compiler_params=ROOMY,
        cost_estimate=FREE,
    )(rows_all, table_low)


def column_sum(value):
    return jnp.sum(value.astype(FLOAT), axis=0)


def layer_forward(weights, embedded, features_low, lengths):
    mats, packed, gains, up_bias = weights
    start_state = layer_norm(embedded, gains[0], gains[1])
    act = start_state.astype(BFLOAT)
    stack = projections(features_low, act, packed, packed.shape[0] - mats.shape[0], gains)
    mixed = attention_call(attend_kernel, lengths, stack, (), 0)
    first_sum = start_state + (product(mixed, mats[6]) + gains[8])
    middle = layer_norm(first_sum, gains[2], gains[3])
    middle_low = middle.astype(BFLOAT)
    active, slope, feed = feed_forward(middle_low, packed, up_bias)
    second_sum = middle + (feed + gains[10])
    kept = (
        embedded,
        act,
        stack,
        mixed,
        first_sum,
        middle_low,
        slope,
        active,
        second_sum,
    )
    return (layer_norm(second_sum, gains[4], gains[5]), kept)


def layer_backward(weights, features_low, lengths, kept, grad_out, head_parts, lines, tools):
    mats, packed, gains, up_bias = weights
    (
        embedded,
        act,
        stack,
        mixed,
        first_sum,
        middle_low,
        slope,
        active,
        second_sum,
    ) = kept
    compacted, give, from_copies, give_rows = tools

    def send(value, name):
        own, blocks = sends(value, lines[name], AXES[name])
        return own, blocks

    def travel(pair, name, *until):
        line = lines[name]
        moved = [shifted(block, line, step) for step, block in enumerate(pair[1], 1)]
        if until:
            moved = list(after(tuple(moved), *until))
        total = pair[0].astype(FLOAT)
        for value in moved:
            total = total + value.astype(FLOAT)
        return total.astype(BFLOAT)

    grad_second, gain_four, gain_five = jax.vjp(layer_norm, second_sum, gains[4], gains[5])[1](
        grad_out
    )
    grad_feed = grad_second.astype(BFLOAT)
    grad_feeds, grad_bias, fed_back = feed_backward(grad_feed, middle_low, active, slope, packed)
    feeds_sum = lax.psum_scatter(grad_feeds, "fsdp", scatter_dimension=2, tiled=True)
    grad_first, gain_two, gain_three = jax.vjp(layer_norm, first_sum, gains[2], gains[3])[1](
        grad_second + fed_back
    )
    grad_attended = grad_first.astype(BFLOAT)
    grad_mixed = times_transposed(grad_attended, mats[6]).astype(BFLOAT)
    pieces = attention_call(
        attend_back_kernel, lengths, stack, (grad_mixed,), 5
    )
    pieces = after(pieces, head_parts[2])
    first_mat = packed.shape[0] - mats.shape[0]
    grad_start, grad_place, sums = start_gradient(grad_first, pieces, packed, first_mat)
    grad_start = after(grad_start, head_parts[3])
    grad_embedded, gain_zero, gain_one = jax.vjp(layer_norm, embedded, gains[0], gains[1])[1](
        grad_start
    )
    grad_vectors = jnp.stack(
        [
            gain_zero,
            gain_one,
            gain_two,
            gain_three,
            gain_four,
            gain_five,
            sums[2, 0],
            sums[4, 0],
            column_sum(grad_attended),
            sums[1, 0],
            column_sum(grad_feed),
        ]
    )
    parts = two_parts(grad_embedded)
    compact = compacted(parts, grad_vectors, grad_bias)
    returned = give(compact)
    pieces = after(pieces, compact)
    token_part = token_gradients(act, mixed, pieces, grad_attended)
    token_core = send(by_owner(token_part, lines), "core")
    pieces = after(pieces, *token_core[1])
    box_part = box_gradients(features_low, stack, pieces, grad_place)
    token_y = send(travel(token_core, "core", box_part), "y")
    box_part = after(box_part, *token_y[1])
    box_core = send(by_owner(box_part, lines), "core")
    box_x = send(travel(box_core, "core"), "x")
    returned = after(returned, *box_x[1])
    rows = from_copies(returned)
    feeds_sum = after(feeds_sum, returned)
    others = after(tuple(rows[1:]), feeds_sum)
    token_z = send(travel(token_y, "y", feeds_sum), "z")
    box_y = send(travel(box_x, "x", token_z[1][0]), "y")
    spread = [give_rows(0, after(rows[0], *box_y[1]))]
    box_z = send(travel(box_y, "y", spread[0]), "z")
    others = after(others, *box_z[1])
    spread += [give_rows(index, value) for index, value in enumerate(others, 1)]
    token_sum = travel(token_z, "z", spread[-1])[:, 0, 0, 0]
    box_half = travel(box_z, "z", token_sum)[:, 0, 0, 0]
    feeds_other = after(from_other_copies(feeds_sum, lines), box_half)
    feeds_sum = feeds_sum.astype(FLOAT) + feeds_other.astype(FLOAT)
    token_mats = both_copies(token_sum, lines)
    box_mats = gather_line(box_half, lines["x"], 2).astype(FLOAT)
    grad_mats = jnp.concatenate([box_mats[2:], token_mats[:3], box_mats[:2], token_mats[3:]])
    return ((grad_mats, feeds_sum), spread, [rows[0], *others], parts)


def combine_mass(first, second):
    peak = jnp.maximum(first[0], second[0])
    mass = first[1] * jnp.exp(first[0] - peak) + second[1] * jnp.exp(second[0] - peak)
    return jnp.stack([peak, mass])


def body(
    token_ids,
    boxes,
    lengths,
    slots,
    labels,
    table,
    mats,
    up,
    down,
    vectors,
    up_bias,
    table_rows,
    table_cols,
    mats_rows,
    mats_cols,
    up_rows,
    up_cols,
    down_rows,
    down_cols,
    vectors_second,
    up_bias_second,
):
    pages = lengths.shape[0]
    tokens = token_ids.shape[0]
    page_len = tokens // pages
    width = table.shape[1]
    shard_rows = table.shape[0]
    slot_count = slots.shape[1]
    groups, copies = lax.axis_size("fsdp"), lax.axis_size("rep")
    group, copy = lax.axis_index("fsdp"), lax.axis_index("rep")
    lines = lines_of(groups, copies)
    table_low = table.astype(BFLOAT)

    own_small = vectors.size + up_bias.size
    small_rows = -(-own_small // width)
    stride = 16 + -(-tokens // (16 * groups)) * 16
    capacity = stride - 2 * small_rows
    buckets = bucket_ids(token_ids, shard_rows)
    places = bucket_places(buckets, capacity, stride, 0)
    requests = bucket_requests(buckets, places, groups, stride)
    own_news = jnp.concatenate([labels.reshape(-1), lengths, buckets.fullest[None]])
    news = jnp.concatenate(
        [
            jnp.repeat(requests, copies, axis=0),
            jnp.broadcast_to(own_news[None], (groups * copies, own_news.shape[0])),
        ],
        axis=1,
    )
    news = lax.all_to_all(news, ("fsdp", "rep"), 0, 0, tiled=True)
    asked = news[:, :stride].reshape(groups, copies, stride)
    asked = jnp.transpose(asked, (1, 0, 2)).reshape(copies, groups * stride)
    labels_all = news[:, stride : stride + pages * slot_count]
    labels_all = labels_all.reshape(groups, copies, pages * slot_count)
    labels_all = lax.dynamic_index_in_dim(labels_all, copy, 1, False).reshape(-1)
    lengths_all = news[:, stride + pages * slot_count : -1]
    turns = (jnp.max(news[:, -1]) + capacity - 1) // capacity

    def fetch(spots, wanted):
        rows = product(one_hot(wanted, shard_rows), table_low).astype(BFLOAT)
        rows = lax.all_to_all(rows.reshape(groups, stride, width), "fsdp", 0, 0, tiled=True)
        return product(one_hot(spots, groups * stride), rows.reshape(groups * stride, width))

    def ask(turn):
        spots = bucket_places(buckets, capacity, stride, turn)
        wanted = bucket_requests(buckets, spots, groups, stride)
        return spots, lax.all_to_all(wanted, "fsdp", 0, 0, tiled=True).reshape(-1)

    embedded = fetch(places, lax.dynamic_index_in_dim(asked, copy, 0, False))
    embedded = lax.while_loop(
        lambda state: state[0] < turns,
        lambda state: (state[0] + 1, state[1] + fetch(*ask(state[0]))),
        (jnp.int32(1), embedded),
    )[1]

    own_labels = labels_all - group * shard_rows
    label_rows = product(one_hot(own_labels, shard_rows), table_low).astype(BFLOAT)
    embedded = after(embedded, label_rows)

    depth = mats.shape[0]
    first_up, after_up = 1 + depth, 1 + depth + up_cols.shape[0] // width
    items = after_up + 1
    lane = jnp.arange(width)
    singles = jnp.pad(jnp.sum(mats_rows, axis=1), (1, width - first_up))
    singles = jnp.where(lane == 0, jnp.sum(table_rows), singles)
    singles = jnp.where((lane >= first_up) & (lane < after_up), jnp.sum(up_rows), singles)
    singles = jnp.where(lane == after_up, jnp.sum(down_rows), singles)
    embedded = after(embedded, singles)

    small = jnp.concatenate([vectors.astype(BFLOAT).reshape(-1), up_bias.astype(BFLOAT)])[None]

    def lay(first, second, bit):
        low = (group & bit) == 0
        return jnp.concatenate([jnp.where(low, first, second), jnp.where(low, second, first)])

    bit = 1
    while bit < groups:
        pairs = [(i, i ^ bit) for i in range(groups)]
        small = lay(small, lax.ppermute(small, "fsdp", pairs), bit)
        bit *= 2
    split = vectors.size
    gains = small[:, :split].reshape(groups, vectors.shape[0], -1)
    gains = jnp.transpose(gains, (1, 0, 2)).reshape(vectors.shape[0], width).astype(FLOAT)
    own_rows, hidden = up.shape
    feed_blocks = hidden // width
    bias = small[:, split:].reshape(groups, feed_blocks, own_rows)
    bias = jnp.transpose(bias, (1, 0, 2)).reshape(-1).astype(FLOAT)
    gains, bias = lax.optimization_barrier((gains, bias))
    up_blocks = up.astype(BFLOAT).reshape(own_rows, groups, feed_blocks, own_rows)
    up_blocks = jnp.transpose(up_blocks, (2, 0, 1, 3)).reshape(feed_blocks, own_rows, width)
    down_blocks = down.astype(BFLOAT).reshape(feed_blocks, own_rows, width)
    packed = jnp.concatenate([up_blocks, down_blocks, mats.astype(BFLOAT)])
    packed = lax.all_gather(packed, "fsdp", axis=1, tiled=True)
    layer_mats = packed[2 * feed_blocks :]
    weights = (layer_mats, packed, gains, bias)

    features_low = box_features(boxes, width).astype(BFLOAT)
    top_state, kept = layer_forward(weights, embedded, features_low, lengths)

    where_at = slots * lengths[:, None] // 256 + jnp.arange(pages)[:, None] * page_len
    pick = one_hot(where_at.reshape(-1), tokens)
    rows_low = product(pick, top_state.astype(BFLOAT)).astype(BFLOAT)
    rows_all = rows_low[None, None, None]
    for axis, name in enumerate(("z", "y", "core")):
        rows_all = gather_line(rows_all, lines[name], axis)
    rows_all = rows_all.reshape(-1, width)
    expo, stats = head_logits(rows_all, table_low)
    peak_here = stats[0]
    products = product(expo, table_low)
    stats = paired(stats[:2].reshape(2, -1, LANES), "fsdp", combine_mass, products).reshape(2, -1)
    products, peak, mass = lax.optimization_barrier((products, *stats))
    log_total = peak + jnp.log(mass)
    factor = jnp.exp(peak_here - log_total)

    is_token = jnp.arange(slot_count) < M_TOK
    valid_all = valid_slots(lengths_all.reshape(-1), slot_count).astype(FLOAT)
    count_token = jnp.sum(jnp.where(is_token, valid_all, 0.0))
    count_area = jnp.sum(jnp.where(is_token, 0.0, valid_all))
    figure = jnp.arange(4)
    counts = jnp.where(figure == 1, count_token, jnp.where(figure == 3, count_area, 0.0))
    count_token, count_area, counts = lax.optimization_barrier((count_token, count_area, counts))
    valid = valid_all.reshape(groups, copies, pages, slot_count)
    valid = lax.dynamic_index_in_dim(valid, copy, 1, False).reshape(-1, slot_count)
    share = jnp.where(is_token, 1.0 / count_token, 1.0 / count_area)
    weight = (valid * share[None, :]).reshape(-1)
    grad_rows = (products * factor[:, None] - label_rows.astype(FLOAT)) * weight[:, None]
    grad_rows = grad_rows.astype(BFLOAT)
    grad_rows = grad_rows.reshape(
        lines["z"].count, lines["y"].count, lines["core"].count, -1, width
    )
    own, blocks = sends(grad_rows, lines["core"], 2)
    weighted = (rows_all.astype(FLOAT) * weight[:, None]).astype(BFLOAT)
    expo, weighted = after((expo, weighted), *blocks)
    mine = own_labels[:, None] == jnp.arange(shard_rows)[None, :]
    grad_logits = expo.astype(FLOAT) * factor[:, None] - mine.astype(FLOAT)
    own, blocks = sends(received(own, blocks, lines["core"]), lines["y"], 1)
    grad_logits = after(grad_logits.astype(BFLOAT), *blocks)
    head_low = contract_rows(grad_logits, weighted).astype(BFLOAT)
    totals = lax.dynamic_slice_in_dim(log_total * valid.reshape(-1), group * pages * slot_count, pages * slot_count)
    targets = jnp.sum(after(rows_all, *blocks).astype(FLOAT) * label_rows.astype(FLOAT), axis=1)
    losses = jnp.sum(totals.reshape(-1, slot_count), axis=0)
    losses = losses - jnp.sum(targets.reshape(-1, slot_count) * valid, axis=0)
    token_loss = jnp.sum(jnp.where(is_token, losses, 0.0))
    area_loss = jnp.sum(jnp.where(is_token, 0.0, losses))
    singles = jnp.where(lane == items + 1, token_loss, jnp.where(lane == items + 3, area_loss, singles))
    own, blocks = sends(received(own, blocks, lines["y"]), lines["z"], 0)
    blocks = list(after(tuple(blocks), head_low, singles))
    grad_rows = received(own, blocks, lines["z"]).reshape(-1, width)
    fifth = shard_rows // 5
    cuts = [fifth, 2 * fifth, shard_rows - (shard_rows - 2 * fifth) // 2]
    head_parts = [from_other_copies(part, lines) for part in jnp.split(head_low, cuts)]
    grad_rows = after(grad_rows, *head_parts[:2])
    grad_top = sum(contract_rows(pick, part) for part in two_parts(grad_rows))

    def compacted(spots, parts):
        spread = one_hot(spots, groups * stride)
        return sum(contract_rows(spread, part) for part in parts)

    def compacted_first(parts, grad_vectors, grad_bias):
        small = grad_vectors.reshape(grad_vectors.shape[0], groups, -1)
        small = jnp.transpose(small, (1, 0, 2)).reshape(groups, -1)
        grad_bias = jnp.transpose(grad_bias.reshape(feed_blocks, groups, own_rows), (1, 0, 2))
        small = jnp.concatenate([small, grad_bias.reshape(groups, -1)], axis=1)
        small = jnp.pad(small, ((0, 0), (0, small_rows * width - own_small)))
        small = jnp.stack(two_parts(small.reshape(groups, small_rows, width)), axis=1)
        small = small.reshape(groups, 2 * small_rows, width).astype(FLOAT)
        small = jnp.pad(small, ((0, 0), (capacity, 0), (0, 0))).reshape(groups * stride, width)
        return (compacted(places, parts) + small).astype(BFLOAT)

    def give(rows):
        rows = lax.all_to_all(rows.reshape(groups, stride, width), "fsdp", 0, 0, tiled=True)
        return rows.reshape(groups * stride, width)

    def spread_rows(wanted, rows):
        return contract_rows(one_hot(wanted, shard_rows), rows)

    def small_sum(rows):
        rows = rows.reshape(groups, stride, width)[:, capacity:].astype(FLOAT)
        rows = jnp.sum(rows, axis=0).reshape(2, small_rows * width)
        return (rows[0] + rows[1])[:own_small]

    if copies == 2:
        from_copies = lambda value: [value, shifted(value, lines["x"], 1)]
        copy_order = [copy, 1 - copy]
    else:
        from_copies = lambda value: list(lax.all_gather(value, "rep"))
        copy_order = list(range(copies))
    asked_of = [lax.dynamic_index_in_dim(asked, index, 0, False) for index in copy_order]

    def give_rows(index, rows):
        return spread_rows(asked_of[index], rows)

    tools = (compacted_first, give, from_copies, give_rows)
    layer_grads, spread, given, embedded_parts = layer_backward(
        weights, features_low, lengths, kept, grad_top, head_parts, lines, tools
    )
    mats_grad, feeds_grad = layer_grads
    up_grad = jnp.transpose(feeds_grad[0].reshape(feed_blocks, own_rows, groups, own_rows), (1, 2, 0, 3))
    up_grad = up_grad.reshape(own_rows, hidden)
    down_grad = feeds_grad[1].reshape(hidden // groups, width)
    small = [small_sum(rows) for rows in given]
    small = sum(small[1:], small[0])
    vectors_grad = small[: vectors.size].reshape(vectors.shape)
    bias_grad = small[vectors.size :]

    head_grad = head_low.astype(FLOAT) + jnp.concatenate(head_parts).astype(FLOAT)
    table_grad = head_grad + sum(spread[1:], spread[0])

    def another(state):
        turn, total = state
        spots, wanted = ask(turn)
        given = from_copies(give(compacted(spots, embedded_parts).astype(BFLOAT)))
        spread = [spread_rows(*pair) for pair in zip(from_copies(wanted), given)]
        return turn + 1, total + sum(spread[1:], spread[0])

    table_grad = lax.while_loop(lambda state: state[0] < turns, another, (jnp.int32(1), table_grad))[1]

    feed_cols = hidden // width
    sizes = [(shard_rows * groups, width)] + [(mats.shape[1] * groups, width)] * depth
    sizes += [(up.shape[0] * groups, hidden), (down.shape[0] * groups, width)]
    row_squares = [jnp.sum(grad * grad, axis=-1) for grad in (table_grad, mats_grad, up_grad, down_grad)]
    singles = jnp.where(lane == items, jnp.sum(small * small), singles)
    sums = jnp.concatenate(
        [
            jnp.sum(table_grad * table_grad, axis=0)[None],
            jnp.sum(mats_grad * mats_grad, axis=1),
            jnp.sum(up_grad * up_grad, axis=0).reshape(feed_cols, width),
            jnp.sum(down_grad * down_grad, axis=0)[None],
            singles[None],
        ]
    )
    cols_old = jnp.concatenate(
        [table_cols[None], mats_cols, up_cols.reshape(feed_cols, width), down_cols[None]]
    )
    sums = paired(sums, "fsdp", jnp.add)
    loss_parts = counts + paired(sums[-1, items + 1 : items + 5], "rep", jnp.add)
    totals = jnp.sum(sums[:-1], axis=1)
    norm_square = jnp.sum(totals) + sums[-1, items]
    grad_norm = jnp.sqrt(norm_square)
    clip = jnp.minimum(1.0, CLIP_NORM / grad_norm)
    square = clip * clip

    def renewed(old, value):
        return DECAY * old + (1.0 - DECAY) * (value + TINY_TERM)

    repeats = [1] * first_up + [feed_cols, 1]
    tall_rows, wide_rows = (
        jnp.array([size[k] for size, n in zip(sizes, repeats) for _ in range(n)], FLOAT)
        for k in range(2)
    )
    row = jnp.arange(items)
    of_up = (row >= first_up) & (row < after_up)
    item_totals = jnp.where(of_up, jnp.sum(jnp.where(of_up, totals, 0.0)), totals)
    mean_rows = renewed(
        sums[-1, :items] / tall_rows, square * item_totals / (tall_rows * wide_rows)
    )
    cols_new = renewed(cols_old, square * sums[:-1] / tall_rows[:, None])
    col_factors = lax.rsqrt(cols_new / mean_rows[:, None])
    step = LEARN_RATE * clip

    def updated(grad, param, rows_old, row_square, col_factor):
        rows_new = renewed(rows_old, square * row_square / grad.shape[-1])
        factor = step * lax.rsqrt(rows_new)
        return grad * clip, rows_new, param - grad * factor[..., None] * col_factor[..., None, :]

    up_factor = col_factors[first_up:after_up].reshape(hidden)
    table_out = updated(table_grad, table, table_rows, row_squares[0], col_factors[0])
    mats_out = updated(mats_grad, mats, mats_rows, row_squares[1], col_factors[1:first_up])
    up_out = updated(up_grad, up, up_rows, row_squares[2], up_factor)
    down_out = updated(down_grad, down, down_rows, row_squares[3], col_factors[after_up])
    clipped_vectors = vectors_grad * clip
    vectors_second_new = DECAY * vectors_second + (1.0 - DECAY) * (
        clipped_vectors * clipped_vectors + TINY_TERM
    )
    vectors_new = vectors - VECTOR_RATE * clipped_vectors * lax.rsqrt(vectors_second_new)
    clipped_bias = bias_grad * clip
    bias_second_new = DECAY * up_bias_second + (1.0 - DECAY) * (
        clipped_bias * clipped_bias + TINY_TERM
    )
    bias_new = up_bias - VECTOR_RATE * clipped_bias * lax.rsqrt(bias_second_new)
    return (
        table_out[0],
        table_out[1],
        cols_new[0],
        table_out[2],
        mats_out[0],
        mats_out[1],
        cols_new[1:first_up],
        mats_out[2],
        up_out[0],
        up_out[1],
        cols_new[first_up:after_up].reshape(hidden),
        up_out[2],
        down_out[0],
        down_out[1],
        cols_new[after_up],
        down_out[2],
        clipped_vectors,
        vectors_second_new,
        vectors_new,
        clipped_bias,
        bias_second_new,
        bias_new,
        grad_norm,
        loss_parts,
    )


def solution(mesh):
    return jax.shard_map(
        body,
        mesh=mesh,
        in_specs=(
            P(("fsdp", "rep")),
            P(None, ("fsdp", "rep")),
            P(("fsdp", "rep")),
            P(("fsdp", "rep"), None),
            P(("fsdp", "rep"), None),
            P("fsdp", None),
            P(None, "fsdp", None),
            P("fsdp", None),
            P("fsdp", None),
            P(None, "fsdp"),
            P("fsdp"),
            P("fsdp"),
            P(),
            P(None, "fsdp"),
            P(),
            P("fsdp"),
            P(),
            P("fsdp"),
            P(),
            P(None, "fsdp"),
            P("fsdp"),
        ),
        out_specs=(
            P("fsdp", None),
            P("fsdp"),
            P(),
            P("fsdp", None),
            P(None, "fsdp", None),
            P(None, "fsdp"),
            P(),
            P(None, "fsdp", None),
            P("fsdp", None),
            P("fsdp"),
            P(),
            P("fsdp", None),
            P("fsdp", None),
            P("fsdp"),
            P(),
            P("fsdp", None),
            P(None, "fsdp"),
            P(None, "fsdp"),
            P(None, "fsdp"),
            P("fsdp"),
            P("fsdp"),
            P("fsdp"),
            P(),
            P(),
        ),
        check_vma=False,
    )
```
